32 devices in a mesh: dp: 16 (over z, x, core), tensor: 2 (over y).
Axes of the slice: x: 2, y: 2, z: 4, core: 2. Of those that a mesh axis runs over, the one named last changes fastest.
Arguments:
- tokens: bfloat16 [32, 1024, 768], P(None, 'dp'), may hold values from -6 to 6
- cotangent: bfloat16 [32, 1024, 768], P(None, 'dp'), may hold values from -6 to 6
- landmark_ids: int32 [32, 1024], replicated, may hold values from 0 to 64, as said below
- w_query: bfloat16 [768, 768], P('dp', 'tensor')
- w_key: bfloat16 [768, 768], P('dp', 'tensor')
- w_value: bfloat16 [768, 768], P('dp', 'tensor'), may hold values from -0.21875 to 0.21875
- b_query: bfloat16 [768], P('tensor'), may hold values from -3 to 3
- b_value: bfloat16 [768], P('tensor'), may hold values from -3 to 3
- conv_taps: bfloat16 [12, 33], P('tensor'), may hold values from -1 to 1
- w_out: bfloat16 [768, 768], P('dp', 'tensor'), may hold values from -0.3125 to 0.3125
- b_out: bfloat16 [768], replicated, may hold values from -2 to 2
- first_gain: bfloat16 [768], replicated, may hold values from 0.5 to 1.5
- first_shift: bfloat16 [768], replicated, may hold values from -2 to 2
- w_inner: bfloat16 [768, 3072], P('dp', 'tensor'), may hold values from -0.21875 to 0.21875
- b_inner: bfloat16 [3072], P('tensor'), may hold values from -2 to 2
- w_outer: bfloat16 [768, 3072], P('dp', 'tensor'), may hold values from -0.109375 to 0.109375
- b_outer: bfloat16 [768], replicated, may hold values from -2 to 2
- second_gain: bfloat16 [768], replicated, may hold values from 0.5 to 1.5
- second_shift: bfloat16 [768], replicated, may hold values from -2 to 2
Outputs:
- layer_out: bfloat16 [32, 1024, 768], P(None, 'dp')
- grad_tokens: bfloat16 [32, 1024, 768], P(None, 'dp')
- grad_w_query: float32 [768, 768], P('dp', 'tensor')
- grad_w_key: float32 [768, 768], P('dp', 'tensor')
- grad_w_value: float32 [768, 768], P('dp', 'tensor')
- grad_b_query: float32 [768], P('tensor')
- grad_b_value: float32 [768], P('tensor')
- grad_conv_taps: float32 [12, 33], P('tensor')
- grad_w_out: float32 [768, 768], P('dp', 'tensor')
- grad_b_out: float32 [768], P('dp')
- grad_first_gain: float32 [768], P('dp')
- grad_first_shift: float32 [768], P('dp')
- grad_w_inner: float32 [768, 3072], P('dp', 'tensor')
- grad_b_inner: float32 [3072], P('tensor')
- grad_w_outer: float32 [768, 3072], P('dp', 'tensor')
- grad_b_outer: float32 [768], P('dp')
- grad_second_gain: float32 [768], P('dp')
- grad_second_shift: float32 [768], P('dp')
The draws below stay inside these ranges and needn't reach their ends.
Inputs may be any that keep to these rules, and one draw needn't show every extreme that they name: `landmark_ids`: along a sequence the ids never fall, every id below 64 occurs in every sequence, and ids equal to 64 fill the end of a sequence; one sequence has none of them.
All inputs are finite; a program needn't handle non-finite values.
Results may differ from the reference program's by a relative error of at most 0.025.
Values may be sent and summed in bfloat16 or wider, within the bound.
A program may use at most 320 MiB of HBM per device.

```python
import jax
import jax.numpy as jnp
from jax import lax

D = 768
HEADS = 12
HD = 64
FF = 3072
LAND = 64
KW = 33
ITERS = 6
LEN = 1024
NSEQ = 32
N_TENSOR = 2


def shared_part(key):
    return jax.random.truncated_normal(jax.random.fold_in(key, 101), -4.0, 4.0, (D, D), jnp.float32)


def draw_w_query(key, part):
    own = jax.random.truncated_normal(jax.random.fold_in(key, 211), -4.0, 4.0, (D, D), jnp.float32)
    return ((0.8 * shared_part(key) + 0.6 * own) * (2.0 / D) ** 0.5).astype(jnp.bfloat16)


def draw_w_key(key, part):
    own = jax.random.truncated_normal(jax.random.fold_in(key, 223), -4.0, 4.0, (D, D), jnp.float32)
    return ((0.8 * shared_part(key) + 0.6 * own) * (2.0 / D) ** 0.5).astype(jnp.bfloat16)


def sequence_lengths(key):
    lengths = jax.random.randint(jax.random.fold_in(key, 301), (NSEQ,), LEN // 4, LEN)
    chosen = jax.random.randint(jax.random.fold_in(key, 302), (), 0, NSEQ)
    return jnp.where(jnp.arange(NSEQ) == chosen, LEN, lengths).astype(jnp.int32)


def draw_landmark_ids(key, part):
    lengths = sequence_lengths(key)
    reach = jnp.maximum(lengths // (2 * LAND), 1)
    jitter = jax.random.randint(jax.random.fold_in(key, 303), (NSEQ, LAND - 1), 0, reach[:, None])
    cuts = jnp.arange(1, LAND, dtype=jnp.int32)[None, :] * lengths[:, None] // LAND + jitter
    places = jnp.arange(LEN, dtype=jnp.int32)
    segment_ids = jnp.sum((places[None, :, None] >= cuts[:, None, :]).astype(jnp.int32), axis=2)
    return jnp.where(places[None, :] < lengths[:, None], segment_ids, LAND).astype(jnp.int32)


def block_scale(own_key, dims, split, low, largest):
    def one(dim, blocks):
        heights = jax.random.uniform(jax.random.fold_in(jax.random.fold_in(own_key, 6), dim), (blocks,), jnp.float32, low / len(split), largest / len(split))
        return jnp.repeat(jnp.exp(heights), dims[dim] // blocks).reshape((-1,) + (1,) * (len(dims) - dim - 1))

    factor_of = one(*split[0])
    for cut in split[1:]:
        factor_of = factor_of * one(*cut)
    return factor_of


def normal_values(stream_key, shape, deviation, most, split=(), kind=jnp.bfloat16):
    level = block_scale(stream_key, shape, split, -0.22, 0.18) if split else 1.0
    values = jax.random.normal(stream_key, shape, jnp.float32) * deviation * level
    return jnp.minimum(jnp.maximum(values, -most), most).astype(kind)


def setup_inputs(seed: int = 0) -> dict:
    splits = jax.random.split(jax.random.key(seed), 20)
    return {
        "tokens": normal_values(splits[0], (NSEQ, LEN, D), 1.0, 6.0, ((1, 16),)),
        "cotangent": normal_values(splits[1], (NSEQ, LEN, D), 1.0, 6.0, ((1, 16),)),
        "landmark_ids": draw_landmark_ids(jax.random.fold_in(splits[19], 71), 0),
        "w_query": draw_w_query(jax.random.fold_in(splits[19], 71), 0),
        "w_key": draw_w_key(jax.random.fold_in(splits[19], 71), 0),
        "w_value": normal_values(splits[5], (D, D), D ** -0.5, 0.21875, ((0, 16), (1, 2))),
        "b_query": normal_values(splits[6], (D,), 0.5, 3.0, ((0, 2),)),
        "b_value": normal_values(splits[7], (D,), 0.5, 3.0, ((0, 2),)),
        "conv_taps": normal_values(splits[8], (HEADS, KW), 0.2, 1.0, ((0, 2),)),
        "w_out": normal_values(splits[9], (D, D), (D // 2) ** -0.5, 0.3125, ((0, 16), (1, 2))),
        "b_out": normal_values(splits[10], (D,), 0.3, 2.0),
        "first_gain": jnp.clip(1.0 + 0.1 * jax.random.normal(splits[11], (D,), jnp.float32), 0.5, 1.5).astype(jnp.bfloat16),
        "first_shift": normal_values(splits[12], (D,), 0.3, 2.0),
        "w_inner": normal_values(splits[13], (D, FF), D ** -0.5, 0.21875, ((0, 16), (1, 2))),
        "b_inner": normal_values(splits[14], (FF,), 0.3, 2.0, ((0, 2),)),
        "w_outer": normal_values(splits[15], (D, FF), FF ** -0.5, 0.109375, ((0, 16), (1, 2))),
        "b_outer": normal_values(splits[16], (D,), 0.3, 2.0),
        "second_gain": jnp.clip(1.0 + 0.1 * jax.random.normal(splits[17], (D,), jnp.float32), 0.5, 1.5).astype(jnp.bfloat16),
        "second_shift": normal_values(splits[18], (D,), 0.3, 2.0),
    }


@jax.custom_vjp
def reduced_value(v):
    return lax.optimization_barrier(v.astype(jnp.bfloat16)).astype(jnp.float32)

@jax.custom_vjp
def reduced_backward(v):
    return v

def low_keep(v):
    return (reduced_value(v), None)

def low_pass(kept, grad):
    return (grad,)

def back_keep(v):
    return (v, None)

def back_low(kept, grad):
    return (reduced_value(grad),)
reduced_value.defvjp(low_keep, low_pass)
reduced_backward.defvjp(back_keep, back_low)

def contract_dims(spec, left, right):
    return jnp.einsum(spec, left, right, precision=lax.Precision.HIGHEST)

def layer_norm(rows, gain, shift):
    center = rows - lax.optimization_barrier(jnp.mean(rows, axis=-1, keepdims=True))
    spread = lax.optimization_barrier(jnp.mean(center * center, axis=-1, keepdims=True))
    return center * lax.rsqrt(spread + 1e-05) * gain + shift

def exact_gelu(values):
    return jax.nn.gelu(values, approximate=False)

def depthwise(values, taps):
    width = taps.shape[1]
    reach = width // 2
    length = values.shape[0]
    padded = jnp.pad(values, ((reach, reach), (0, 0), (0, 0)))
    total = jnp.zeros_like(values)
    for offset in range(width):
        total = total + taps[:, offset][None, :, None] * padded[offset:offset + length]
    return total

def pseudo_inverse(kernel_matrix):
    extent = kernel_matrix.shape[-1]
    identity = jnp.eye(extent, dtype=jnp.float32)
    total = lax.optimization_barrier(jnp.sum(kernel_matrix * kernel_matrix, axis=(1, 2), keepdims=True))
    approx = jnp.swapaxes(kernel_matrix, 1, 2) / total
    for step in range(ITERS):
        applied = contract_dims('hij,hjk->hik', kernel_matrix, approx)
        inner = 7.0 * identity - applied
        inner = 15.0 * identity - contract_dims('hij,hjk->hik', applied, inner)
        inner = 13.0 * identity - contract_dims('hij,hjk->hik', applied, inner)
        approx = 0.25 * contract_dims('hij,hjk->hik', approx, inner)
    return approx

def attend(queries, keys_all, values_all, member_mask, valid_count, valid, taps):
    length = queries.shape[0]
    heads = taps.shape[0]
    query_head_rows = queries.reshape(length, heads, -1)
    key_head_rows = keys_all.reshape(length, heads, -1)
    value_head_rows = values_all.reshape(length, heads, -1)
    landmark_queries_mean = reduced_value(reduced_backward(contract_dims('gf,fwa->gwa', member_mask, query_head_rows)) / valid_count[:, None, None])
    landmark_keys_mean = reduced_value(reduced_backward(contract_dims('gf,fwa->gwa', member_mask, key_head_rows)) / valid_count[:, None, None])
    first_factor = reduced_backward(contract_dims('uow,qow->oqu', query_head_rows, landmark_keys_mean))
    near_block = reduced_value(jax.nn.softmax(first_factor, axis=1))
    kernel_matrix = jax.nn.softmax(contract_dims('yoq,uoq->oyu', landmark_queries_mean, landmark_keys_mean), axis=2)
    inverse_matrix = pseudo_inverse(kernel_matrix)
    third_factor = reduced_backward(contract_dims('zwp,owp->wzo', landmark_queries_mean, key_head_rows))
    third_factor = jnp.where(valid[None, None, :], third_factor, -1e+30)
    far_block = reduced_value(jax.nn.softmax(third_factor, axis=2))
    summary_matrix = reduced_backward(contract_dims('zyj,jzt->zyt', far_block, value_head_rows))
    mixed_heads = reduced_value(contract_dims('gfv,gvx->gfx', inverse_matrix, summary_matrix))
    attended_rows = contract_dims('azr,azs->ras', near_block, mixed_heads)
    masked = jnp.where(valid[:, None, None], value_head_rows, 0.0)
    context = reduced_backward(reduced_value(attended_rows + depthwise(masked, taps)))
    return context.reshape(length, -1)

def forward(rows, seg_ids, params):
    w_query, w_key, w_value, b_query, b_value, conv_taps, w_out, b_out, first_gain, first_shift, w_inner, b_inner, w_outer, b_outer, second_gain, second_shift = params
    groups = N_TENSOR
    head_group = HEADS // groups
    column_count = D // groups
    unit_count = FF // groups
    scale = HD ** (-0.25)
    valid = seg_ids < LAND
    member_mask = (seg_ids[None, :] == jnp.arange(LAND, dtype=jnp.int32)[:, None]).astype(jnp.float32)
    valid_count = lax.optimization_barrier(jnp.sum(member_mask, axis=1))
    attn_total = jnp.zeros(rows.shape, jnp.float32)
    for group in range(groups):
        lower = group * column_count
        upper = lower + column_count
        rows_in = reduced_backward(rows)
        queries = reduced_value((reduced_backward(contract_dims('nd,dc->nc', rows_in, w_query[:, lower:upper])) + b_query[lower:upper]) * scale)
        keys_all = reduced_value(reduced_backward(contract_dims('nd,dc->nc', rows_in, w_key[:, lower:upper])) * scale)
        values_all = reduced_value(reduced_backward(contract_dims('nd,dc->nc', rows_in, w_value[:, lower:upper])) + b_value[lower:upper])
        taps = conv_taps[group * head_group:(group + 1) * head_group]
        context = attend(queries, keys_all, values_all, member_mask, valid_count, valid, taps)
        attn_total = attn_total + reduced_value(contract_dims('nc,dc->nd', context, w_out[:, lower:upper]))
    attn_out = reduced_backward(attn_total) + b_out
    hidden = layer_norm(rows + attn_out, first_gain, first_shift)
    hidden_low = reduced_value(hidden)
    ffn_total = jnp.zeros(rows.shape, jnp.float32)
    for group in range(groups):
        lower = group * unit_count
        upper = lower + unit_count
        rows_hidden = reduced_backward(hidden_low)
        inner = reduced_backward(contract_dims('nd,df->nf', rows_hidden, w_inner[:, lower:upper])) + b_inner[lower:upper]
        active = reduced_value(exact_gelu(inner))
        ffn_total = ffn_total + reduced_value(contract_dims('nf,df->nd', active, w_outer[:, lower:upper]))
    ffn_out = reduced_backward(ffn_total) + b_outer
    return layer_norm(hidden + ffn_out, second_gain, second_shift)

def reference(tokens, cotangent, landmark_ids, w_query, w_key, w_value, b_query, b_value, conv_taps, w_out, b_out, first_gain, first_shift, w_inner, b_inner, w_outer, b_outer, second_gain, second_shift):
    params = tuple((item.astype(jnp.float32) for item in (w_query, w_key, w_value, b_query, b_value, conv_taps, w_out, b_out, first_gain, first_shift, w_inner, b_inner, w_outer, b_outer, second_gain, second_shift)))

    def one_sequence(totals, inputs):
        rows, cot_rows, seg_ids = inputs

        def layer(rows_f, weights):
            return forward(rows_f, seg_ids, weights)
        result, pull = jax.vjp(layer, rows.astype(jnp.float32), params)
        grad_rows, grad_params = pull(cot_rows.astype(jnp.float32))
        totals = tuple((left + right for left, right in zip(totals, grad_params)))
        return (totals, (result.astype(jnp.bfloat16), grad_rows.astype(jnp.bfloat16)))
    zeros = tuple((jnp.zeros(item.shape, jnp.float32) for item in params))
    totals, (layer_out, grad_tokens) = lax.scan(one_sequence, zeros, (tokens, cotangent, landmark_ids))
    return (layer_out, grad_tokens, totals[0], totals[1], totals[2], totals[3], totals[4], totals[5], totals[6], totals[7], totals[8], totals[9], totals[10], totals[11], totals[12], totals[13], totals[14], totals[15])
```

```python
import jax
import jax.numpy as jnp
from jax import lax
from jax.sharding import PartitionSpec as P

LAND = 64
ITERS = 6


def contract_dims(spec, left, right):
    return jnp.einsum(spec, left, right, precision=lax.Precision.HIGHEST)


def partial_product(spec, left, right):
    return jnp.einsum(spec, left, right, preferred_element_type=jnp.float32)


def layer_norm(rows, gain, shift):
    center = rows - jnp.mean(rows, axis=-1, keepdims=True)
    spread = jnp.mean(center * center, axis=-1, keepdims=True)
    return center * lax.rsqrt(spread + 1e-05) * gain + shift


def exact_gelu(values):
    return jax.nn.gelu(values, approximate=False)


def depthwise(values, taps):
    width = taps.shape[1]
    reach = width // 2
    length = values.shape[0]
    padded = jnp.pad(values, ((reach, reach), (0, 0), (0, 0)))
    total = jnp.zeros_like(values)
    for offset in range(width):
        total = total + taps[:, offset][None, :, None] * padded[offset : offset + length]
    return total


def pseudo_inverse(kernel_matrix):
    extent = kernel_matrix.shape[-1]
    identity = jnp.eye(extent, dtype=jnp.float32)
    total = jnp.sum(kernel_matrix * kernel_matrix, axis=(1, 2), keepdims=True)
    approx = jnp.swapaxes(kernel_matrix, 1, 2) / total
    for step in range(ITERS):
        applied = contract_dims("hij,hjk->hik", kernel_matrix, approx)
        inner = 7.0 * identity - applied
        inner = 15.0 * identity - contract_dims("hij,hjk->hik", applied, inner)
        inner = 13.0 * identity - contract_dims("hij,hjk->hik", applied, inner)
        approx = 0.25 * contract_dims("hij,hjk->hik", approx, inner)
    return approx


def softmax_back(probs, grad, reduce_axis):
    return probs * (grad - jnp.sum(probs * grad, axis=reduce_axis, keepdims=True))


def sequence_step(rows, cot_rows, seg_ids, weights):
    (
        w_query,
        w_key,
        w_value,
        b_query,
        b_value,
        conv_taps,
        w_out,
        b_out,
        first_gain,
        first_shift,
        w_inner,
        b_inner,
        w_outer,
        b_outer,
        second_gain,
        second_shift,
    ) = weights
    single_float = jnp.float32
    reduced_dtype = jnp.bfloat16
    length = rows.shape[0]
    heads = conv_taps.shape[0]
    column_count = w_query.shape[1]
    head_dim = column_count // heads
    scale = head_dim ** (-0.25)
    rows_f = rows.astype(single_float)
    valid = seg_ids < LAND
    compare = seg_ids[None, :] == jnp.arange(LAND, dtype=jnp.int32)[:, None]
    member_mask = compare.astype(reduced_dtype)
    valid_count = jnp.sum(compare.astype(single_float), axis=1)[:, None, None]
    queries = (
        (jnp.dot(rows, w_query, preferred_element_type=single_float) + b_query.astype(single_float))
        * scale
    ).astype(reduced_dtype)
    keys_all = (jnp.dot(rows, w_key, preferred_element_type=single_float) * scale).astype(
        reduced_dtype
    )
    values_all = (
        jnp.dot(rows, w_value, preferred_element_type=single_float) + b_value.astype(single_float)
    ).astype(reduced_dtype)
    query_head_rows = queries.reshape(length, heads, head_dim)
    key_head_rows = keys_all.reshape(length, heads, head_dim)
    value_head_rows = values_all.reshape(length, heads, head_dim)
    landmark_queries_mean = (
        partial_product("gf,fwa->gwa", member_mask, query_head_rows) / valid_count
    ).astype(reduced_dtype)
    landmark_keys_mean = (
        partial_product("gf,fwa->gwa", member_mask, key_head_rows) / valid_count
    ).astype(reduced_dtype)
    near_block_float = jax.nn.softmax(
        partial_product("uow,qow->oqu", query_head_rows, landmark_keys_mean), axis=1
    )
    near_block = near_block_float.astype(reduced_dtype)
    kernel_matrix = jax.nn.softmax(
        partial_product("yoq,uoq->oyu", landmark_queries_mean, landmark_keys_mean), axis=2
    )
    inverse_matrix, inverse_back = jax.vjp(pseudo_inverse, kernel_matrix)
    third_factor = partial_product("zwp,owp->wzo", landmark_queries_mean, key_head_rows)
    third_factor = jnp.where(valid[None, None, :], third_factor, -1e30)
    far_f = jax.nn.softmax(third_factor, axis=2)
    far_block = far_f.astype(reduced_dtype)
    summary_matrix = partial_product("zyj,jzt->zyt", far_block, value_head_rows)
    mixed_heads = contract_dims("gfv,gvx->gfx", inverse_matrix, summary_matrix).astype(
        reduced_dtype
    )
    attended_rows = partial_product("azr,azs->ras", near_block, mixed_heads)
    masked = jnp.where(valid[:, None, None], value_head_rows.astype(single_float), 0.0)
    conv_out, conv_back = jax.vjp(depthwise, masked, conv_taps.astype(single_float))
    context = (attended_rows + conv_out).astype(reduced_dtype).reshape(length, column_count)
    attn_part = partial_product("nc,dc->nd", context, w_out)
    attn_out = attn_part + b_out.astype(single_float)
    hidden, first_norm_back = jax.vjp(
        layer_norm,
        rows_f + attn_out,
        first_gain.astype(single_float),
        first_shift.astype(single_float),
    )
    hidden_low = hidden.astype(reduced_dtype)
    inner = jnp.dot(hidden_low, w_inner, preferred_element_type=single_float) + b_inner.astype(
        single_float
    )
    active_f, gelu_back = jax.vjp(exact_gelu, inner)
    active = active_f.astype(reduced_dtype)
    ffn_part = partial_product("nf,df->nd", active, w_outer)
    ffn_out = ffn_part + b_outer.astype(single_float)
    result, second_norm_back = jax.vjp(
        layer_norm,
        hidden + ffn_out,
        second_gain.astype(single_float),
        second_shift.astype(single_float),
    )
    out_rows = result.astype(reduced_dtype)
    grad_second, grad_second_gain, grad_second_shift = second_norm_back(
        cot_rows.astype(single_float)
    )
    grad_b_outer = jnp.sum(grad_second, axis=0)
    grad_ffn = grad_second.astype(reduced_dtype)
    grad_w_outer = partial_product("nd,nf->df", grad_ffn, active)
    grad_active = partial_product("nd,df->nf", grad_ffn, w_outer)
    (grad_inner,) = gelu_back(grad_active)
    grad_b_inner = jnp.sum(grad_inner, axis=0)
    grad_inner_low = grad_inner.astype(reduced_dtype)
    grad_w_inner = partial_product("nd,nf->df", hidden_low, grad_inner_low)
    hidden_part = partial_product("nf,df->nd", grad_inner_low, w_inner)
    grad_hidden = grad_second + hidden_part
    grad_first, grad_first_gain, grad_first_shift = first_norm_back(grad_hidden)
    grad_b_out = jnp.sum(grad_first, axis=0)
    grad_attn = grad_first.astype(reduced_dtype)
    grad_w_out = partial_product("nd,nc->dc", grad_attn, context)
    context_gradient = (
        partial_product("nd,dc->nc", grad_attn, w_out)
        .astype(reduced_dtype)
        .reshape(length, heads, head_dim)
    )
    grad_masked, grad_taps = conv_back(context_gradient.astype(single_float))
    values_gradient = jnp.where(valid[:, None, None], grad_masked, 0.0)
    near_block_gradient = partial_product("erl,ryl->rye", context_gradient, mixed_heads)
    mixed_gradient = partial_product("zyj,jzt->zyt", near_block, context_gradient)
    first_scores_gradient = softmax_back(near_block_float, near_block_gradient, 1).astype(
        reduced_dtype
    )
    queries_gradient = partial_product("uba,buo->auo", first_scores_gradient, landmark_keys_mean)
    landmark_key_gradient = partial_product("sjw,wsu->jsu", first_scores_gradient, query_head_rows)
    summary_gradient = contract_dims("sqe,sqg->seg", inverse_matrix, mixed_gradient).astype(
        reduced_dtype
    )
    inverse_gradient = contract_dims("lcp,lzp->lcz", mixed_gradient, summary_matrix)
    far_block_gradient = partial_product("byl,sbl->bys", summary_gradient, value_head_rows)
    values_gradient = values_gradient + partial_product("azr,azs->ras", far_block, summary_gradient)
    third_factor_gradient = softmax_back(far_f, far_block_gradient, 2).astype(reduced_dtype)
    landmark_query_gradient = partial_product("sjw,wsu->jsu", third_factor_gradient, key_head_rows)
    keys_gradient = partial_product("uba,buo->auo", third_factor_gradient, landmark_queries_mean)
    (grad_kernel,) = inverse_back(inverse_gradient)
    middle_gradient = softmax_back(kernel_matrix, grad_kernel, 2)
    landmark_query_gradient = landmark_query_gradient + contract_dims(
        "tiz,ztn->itn", middle_gradient, landmark_keys_mean.astype(single_float)
    )
    landmark_key_gradient = landmark_key_gradient + contract_dims(
        "xql,qxb->lxb", middle_gradient, landmark_queries_mean.astype(single_float)
    )
    queries_gradient = queries_gradient + partial_product(
        "wf,wqb->fqb", member_mask, (landmark_query_gradient / valid_count).astype(reduced_dtype)
    )
    keys_gradient = keys_gradient + partial_product(
        "wf,wqb->fqb", member_mask, (landmark_key_gradient / valid_count).astype(reduced_dtype)
    )
    queries_gradient = queries_gradient.reshape(length, column_count) * scale
    values_gradient = values_gradient.reshape(length, column_count)
    grad_b_query = jnp.sum(queries_gradient, axis=0)
    grad_b_value = jnp.sum(values_gradient, axis=0)
    pre_query = queries_gradient.astype(reduced_dtype)
    pre_key = (keys_gradient.reshape(length, column_count) * scale).astype(reduced_dtype)
    pre_value = values_gradient.astype(reduced_dtype)
    grad_w_query = partial_product("nd,nc->dc", rows, pre_query)
    grad_w_key = partial_product("nd,nc->dc", rows, pre_key)
    grad_w_value = partial_product("nd,nc->dc", rows, pre_value)
    token_part = (
        partial_product("nc,dc->nd", pre_query, w_query)
        + partial_product("nc,dc->nd", pre_key, w_key)
        + partial_product("nc,dc->nd", pre_value, w_value)
    )
    grad_rows = (
        grad_first + token_part
    ).astype(reduced_dtype)
    grads = (
        grad_w_query,
        grad_w_key,
        grad_w_value,
        grad_b_query,
        grad_b_value,
        grad_taps,
        grad_w_out,
        grad_b_out,
        grad_first_gain,
        grad_first_shift,
        grad_w_inner,
        grad_b_inner,
        grad_w_outer,
        grad_b_outer,
        grad_second_gain,
        grad_second_shift,
    )
    return (out_rows, grad_rows, grads)


def local(tokens, cotangent, landmark_ids, w_query, w_key, w_value, b_query, b_value, conv_taps, w_out, b_out,
          first_gain, first_shift, w_inner, b_inner, w_outer, b_outer, second_gain, second_shift):
    groups = lax.axis_size("dp")
    tens = lax.axis_index("tensor")
    here = lax.axis_index("dp")
    half = tokens.shape[1]

    def to_owner(array):
        mine = lax.dynamic_slice_in_dim(array, tens * groups, groups, 0)
        moved = lax.all_to_all(mine, "dp", split_axis=0, concat_axis=0, tiled=True)
        return moved.reshape(groups * half, array.shape[2])

    def to_home(rows):
        moved = lax.all_to_all(rows.reshape(groups, half, rows.shape[1]), "dp", split_axis=0, concat_axis=0, tiled=True)
        return lax.all_gather(moved, "tensor", axis=0, tiled=True)

    rows = to_owner(tokens)
    cot = to_owner(cotangent)
    ids = lax.dynamic_index_in_dim(landmark_ids, tens * groups + here, 0, keepdims=False)
    packed = jnp.concatenate([w_query, w_key, w_value, w_out, w_inner, w_outer], axis=1)
    widths = [w.shape[1] for w in (w_query, w_key, w_value, w_out, w_inner, w_outer)]
    whole = lax.all_gather(packed, ("tensor", "dp"), axis=0, tiled=True)
    tn = lax.axis_size("tensor")
    depth = groups * packed.shape[0]
    whole = whole.reshape(tn, depth, packed.shape[1])
    mats = []
    at = 0
    for w in widths:
        mats.append(jnp.concatenate([whole[t, :, at : at + w] for t in range(tn)], axis=1))
        at += w
    small = lax.all_gather(
        jnp.concatenate([b_query, b_value, b_inner, conv_taps.reshape(-1)]), "tensor", axis=0
    )
    bq = small[:, : b_query.shape[0]].reshape(-1)
    at = b_query.shape[0]
    bv = small[:, at : at + b_value.shape[0]].reshape(-1)
    at += b_value.shape[0]
    bi = small[:, at : at + b_inner.shape[0]].reshape(-1)
    at += b_inner.shape[0]
    taps = small[:, at:].reshape(-1, conv_taps.shape[1])
    weights = (mats[0], mats[1], mats[2], bq, bv, taps, mats[3], b_out, first_gain, first_shift,
               mats[4], bi, mats[5], b_outer, second_gain, second_shift)
    out_rows, grad_rows, g = sequence_step(rows, cot, ids, weights)
    wide = [g[0], g[1], g[2], g[6], g[10], g[12]]
    parts = []
    for t in range(tn):
        parts.append(jnp.concatenate([m[:, t * w : (t + 1) * w] for m, w in zip(wide, widths)], axis=1))
    scat = lax.psum_scatter(
        jnp.concatenate(parts, axis=0).astype(jnp.bfloat16), ("tensor", "dp"), scatter_dimension=0, tiled=True
    ).astype(jnp.float32)
    wgrads = []
    at = 0
    for w in widths:
        wgrads.append(scat[:, at : at + w])
        at += w
    vec = jnp.concatenate([g[7], g[8], g[9], g[13], g[14], g[15], g[3], g[4], g[11], g[5].reshape(-1)])
    vec = lax.psum(vec, ("tensor", "dp"))
    d = g[7].shape[0]
    share = d // groups
    norms = [lax.dynamic_slice_in_dim(vec, k * d + here * share, share, 0) for k in range(6)]
    at = 6 * d
    gbq = lax.dynamic_slice_in_dim(vec, at + tens * b_query.shape[0], b_query.shape[0], 0)
    at += d
    gbv = lax.dynamic_slice_in_dim(vec, at + tens * b_value.shape[0], b_value.shape[0], 0)
    at += d
    gbi = lax.dynamic_slice_in_dim(vec, at + tens * b_inner.shape[0], b_inner.shape[0], 0)
    at += bi.shape[0]
    n = conv_taps.size
    gt = lax.dynamic_slice_in_dim(vec, at + tens * n, n, 0).reshape(conv_taps.shape)
    return (to_home(out_rows), to_home(grad_rows), wgrads[0], wgrads[1], wgrads[2], gbq, gbv, gt, wgrads[3],
            norms[0], norms[1], norms[2], wgrads[4], gbi, wgrads[5], norms[3], norms[4], norms[5])


def solution(mesh):
    return jax.shard_map(
        local,
        mesh=mesh,
        in_specs=(
            P(None, "dp", None),
            P(None, "dp", None),
            P(),
            P("dp", "tensor"),
            P("dp", "tensor"),
            P("dp", "tensor"),
            P("tensor"),
            P("tensor"),
            P("tensor", None),
            P("dp", "tensor"),
            P(),
            P(),
            P(),
            P("dp", "tensor"),
            P("tensor"),
            P("dp", "tensor"),
            P(),
            P(),
            P(),
        ),
        out_specs=(
            P(None, "dp", None),
            P(None, "dp", None),
            P("dp", "tensor"),
            P("dp", "tensor"),
            P("dp", "tensor"),
            P("tensor"),
            P("tensor"),
            P("tensor", None),
            P("dp", "tensor"),
            P("dp"),
            P("dp"),
            P("dp"),
            P("dp", "tensor"),
            P("tensor"),
            P("dp", "tensor"),
            P("dp"),
            P("dp"),
            P("dp"),
        ),
        check_vma=False,
    )
```

```python
import functools
import jax
import jax.numpy as jnp
from jax import lax
from jax.experimental import pallas as pl
from jax.experimental.pallas import tpu as pltpu

from jax.sharding import PartitionSpec as P

F32 = jnp.float32
BF = jnp.bfloat16
LAND = 64
ITERS = 6
HEADS_HERE = 6
ROWS_BQ, ROWS_BV, ROWS_BI, ROWS_TAPS, ROWS_FLIP = 0, 3, 6, 18, 24
EDGE = 112


def nn(a, b):
    return lax.dot_general(a, b, (((1,), (0,)), ((), ())), preferred_element_type=F32)


def nt(a, b):
    return lax.dot_general(a, b, (((1,), (1,)), ((), ())), preferred_element_type=F32)


def turn(a):
    return jnp.transpose(a, (1, 0))


def same_head(rows, columns):
    left = lax.broadcasted_iota(jnp.int32, (rows, columns), 0) // LAND
    right = lax.broadcasted_iota(jnp.int32, (rows, columns), 1) // LAND
    return left == right


def spread(small):
    n = small.shape[1] // LAND
    tall = jnp.concatenate([small] * n, axis=0)
    return jnp.where(same_head(n * LAND, n * LAND), tall, jnp.zeros_like(tall))


def gather_diag(full):
    n = full.shape[1] // LAND
    lane = lax.broadcasted_iota(jnp.int32, (LAND, full.shape[1]), 1) // LAND
    out = full[:LAND]
    for h in range(1, n):
        out = jnp.where(lane == h, full[h * LAND : (h + 1) * LAND], out)
    return out


def halves(a):
    high = a.astype(BF)
    return high, (a - high.astype(F32)).astype(BF)


def pair_nn(a, b):
    ah, al = halves(a)
    bh, bl = halves(b)
    bh, bl = spread(bh), spread(bl)
    wide = jnp.concatenate([bh, bl], axis=1)
    r = nn(jnp.concatenate([ah, al], axis=1), jnp.concatenate([wide, wide], axis=0))
    return r[:, : 2 * LAND] + r[:, 2 * LAND :]


def pair_nt(a, b):
    ah, al = halves(a)
    bh, bl = halves(b)
    bh, bl = spread(bh), spread(bl)
    tall = jnp.concatenate([bh, bl], axis=0)
    r = nt(jnp.concatenate([ah, al], axis=1), jnp.concatenate([tall, tall], axis=1))
    return r[:, : 2 * LAND] + r[:, 2 * LAND :]


def pair_turn(a):
    t = turn(a)
    return jnp.concatenate([t[:LAND], t[LAND:]], axis=1)


def pair_sum(a):
    left = lax.broadcasted_iota(jnp.int32, a.shape, 1) < LAND
    low = jnp.sum(jnp.where(left, a, 0.0), axis=1, keepdims=True)
    high = jnp.sum(jnp.where(left, 0.0, a), axis=1, keepdims=True)
    return jnp.where(left, low, high)


def pair_softmax(a):
    left = lax.broadcasted_iota(jnp.int32, a.shape, 1) < LAND
    low = jnp.max(jnp.where(left, a, -1e30), axis=1, keepdims=True)
    high = jnp.max(jnp.where(left, -1e30, a), axis=1, keepdims=True)
    e = jnp.exp(a - jnp.where(left, low, high))
    return e / pair_sum(e)


def pair_eye():
    r = lax.broadcasted_iota(jnp.int32, (LAND, 2 * LAND), 0)
    c = lax.broadcasted_iota(jnp.int32, (LAND, 2 * LAND), 1) % LAND
    return jnp.where(r == c, 1.0, 0.0).astype(F32)


def toeplitz(row, size, width):
    return pltpu.roll(jnp.broadcast_to(row, (size, width)), 0, 1, stride=1, stride_axis=0)


def blocks_of(ref, lower, block):
    length = ref.shape[1] - 256
    return jnp.concatenate(
        [ref[lower : lower + LAND, at : at + block + 256] for at in range(0, length, block)], axis=0
    )


def unblock(stacked, block):
    n = stacked.shape[0] // LAND
    return jnp.concatenate([stacked[i * LAND : (i + 1) * LAND] for i in range(n)], axis=1)


def own_sequence():
    return lax.axis_index("tensor") * lax.axis_size("dp") + lax.axis_index("dp")


def side_row(small_ref, t, first, count):
    return jnp.concatenate([small_ref[t, r : r + 1, :] for r in range(first, first + count)], axis=1)


def band_of(small_ref, head, first):
    t, h = head // HEADS_HERE, head % HEADS_HERE
    row = small_ref[t, first + h : first + h + 1, :]
    row = jnp.concatenate([row, jnp.zeros((1, 384), F32)], axis=1)
    return toeplitz(pltpu.roll(row, EDGE, 1), 256, 512).astype(BF)


def attend_forward(x_ref, w_ref, small_ref, ids_ref,
                   q_ref, k_ref, v_ref, near_ref, far_ref, ctx_ref, lq_ref, lk_ref, mix_ref, sum_ref, ker_ref,
                   z_ref, a_ref, v2_ref, w2_ref, pad_ref):
    length, width = x_ref.shape
    tn = w_ref.shape[0]
    cols = width // tn
    scale = LAND ** -0.25
    rows_at = 256
    pairs = width // 128
    groups = width // 256
    bq = [side_row(small_ref, t, ROWS_BQ, 3) for t in range(tn)]
    bv = [side_row(small_ref, t, ROWS_BV, 3) for t in range(tn)]

    def project(i, carry):
        at = pl.ds(pl.multiple_of(i * rows_at, rows_at), rows_at)
        for t in range(tn):
            out = nn(x_ref[at, :], w_ref[t])
            own = slice(t * cols, (t + 1) * cols)
            q_ref[at, own] = ((out[:, :cols] + bq[t]) * scale).astype(BF)
            k_ref[at, own] = (out[:, cols : 2 * cols] * scale).astype(BF)
            v_ref[at, own] = (out[:, 2 * cols :] + bv[t]).astype(BF)
        return carry

    lax.fori_loop(0, length // rows_at, project, 0)

    ids = ids_ref[pl.ds(own_sequence(), 1), :]
    member = jnp.where(lax.broadcasted_iota(jnp.int32, (LAND, length), 0) == ids, 1.0, 0.0).astype(F32)
    count = jnp.sum(member, axis=1, keepdims=True)
    member = member.astype(BF)
    valid = ids < LAND
    lq_ref[...] = (nn(member, q_ref[...]) / count).astype(BF)
    lk_ref[...] = (nn(member, k_ref[...]) / count).astype(BF)

    eye = pair_eye()
    for p in range(pairs):
        own = slice(p * 128, (p + 1) * 128)
        scores = nt(lq_ref[:, own], spread(lk_ref[:, own]))
        kernel = pair_softmax(scores)
        ker_ref[:, own] = kernel
        left = lax.broadcasted_iota(jnp.int32, kernel.shape, 1) < LAND
        total = jnp.sum(pair_sum(kernel * kernel), axis=0, keepdims=True)
        z_ref[0, :, own] = pair_turn(kernel) / total

    for g in range(groups):
        own = slice(g * 256, (g + 1) * 256)
        scores = nt(spread(lk_ref[:, own]), q_ref[:, own]).reshape(4, LAND, length)
        scores = jnp.exp(scores - jnp.max(scores, axis=1, keepdims=True))
        scores = scores / jnp.sum(scores, axis=1, keepdims=True)
        near_ref[own, :] = scores.reshape(256, length).astype(BF)
        scores = nt(spread(lq_ref[:, own]), k_ref[:, own])
        scores = jnp.where(valid, scores, -1e30)
        scores = jnp.exp(scores - jnp.max(scores, axis=1, keepdims=True))
        scores = scores / jnp.sum(scores, axis=1, keepdims=True)
        far_ref[own, :] = scores.astype(BF)
        sum_ref[:, own] = gather_diag(nn(far_ref[own, :], v_ref[:, own]))

    def iterate(n, carry):
        for p in range(pairs):
            own = slice(p * 128, (p + 1) * 128)
            z = z_ref[n, :, own]
            a = pair_nn(ker_ref[:, own], z)
            v2 = 15.0 * eye - pair_nn(a, 7.0 * eye - a)
            w2 = 13.0 * eye - pair_nn(a, v2)
            a_ref[n, :, own] = a
            v2_ref[n, :, own] = v2
            w2_ref[n, :, own] = w2
            z_ref[n + 1, :, own] = 0.25 * pair_nn(z, w2)
        return carry

    lax.fori_loop(0, ITERS, iterate, 0)

    for p in range(pairs):
        own = slice(p * 128, (p + 1) * 128)
        mix_ref[:, own] = pair_nn(z_ref[ITERS, :, own], sum_ref[:, own]).astype(BF)

    pad_ref[...] = jnp.zeros_like(pad_ref)
    for g in range(groups):
        own = slice(g * 256, (g + 1) * 256)
        att = nn(turn(spread(mix_ref[:, own])), near_ref[own, :])
        vt = turn(v_ref[:, own])
        pad_ref[:, 128 : 128 + length] = jnp.where(valid, vt, jnp.zeros_like(vt))
        parts = []
        for h in range(4):
            band = band_of(small_ref, 4 * g + h, ROWS_TAPS)
            parts.append(unblock(nt(blocks_of(pad_ref, h * LAND, 256), band), 256))
        att = (att + jnp.concatenate(parts, axis=0)).astype(BF)
        ctx_ref[:, own] = turn(att)


def call_attend_forward(x, w, small, ids):
    length, width = x.shape
    s = jax.ShapeDtypeStruct
    big = s((length, width), BF)
    tall = s((width, length), BF)
    low = s((LAND, width), BF)
    wide = s((LAND, width), F32)
    steps = s((ITERS, LAND, width), F32)
    vm = pl.BlockSpec(memory_space=pltpu.VMEM)
    tn = w.shape[0]
    cols = width // tn
    wspec = pl.BlockSpec((tn, width, 3 * cols), lambda i: (0, 0, 0))
    full = lambda a: pl.BlockSpec(a.shape, lambda i: (0,) * len(a.shape))
    outs = (big, big, big, tall, tall, big, low, low, low, wide, wide, s((ITERS + 1, LAND, width), F32), steps, steps, steps)
    return pl.pallas_call(
        attend_forward,
        grid=(1,),
        out_shape=outs,
        in_specs=[full(x), wspec, full(small), full(ids)],
        out_specs=tuple(full(o) for o in outs),
        scratch_shapes=[pltpu.VMEM((256, length + 256), BF)],
        compiler_params=pltpu.CompilerParams(vmem_limit_bytes=60 * 2**20),
        name="attend_forward",
    )(x, w, small, ids)


ROOT_HALF = 0.7071067811865476
P_ERF = 0.3275911
C_ERF = (0.254829592, -0.284496736, 1.421413741, -1.453152027, 1.061405429)


def gelu_both(u):
    x = jnp.abs(u) * ROOT_HALF
    e = jnp.exp(-0.5 * u * u)
    t = 1.0 / (1.0 + P_ERF * x)
    poly = C_ERF[4]
    for c in (C_ERF[3], C_ERF[2], C_ERF[1], C_ERF[0]):
        poly = poly * t + c
    tail = 0.5 * poly * t * e
    phi = jnp.where(u < 0.0, tail, 1.0 - tail)
    return u * phi, phi + u * e * 0.3989422804014327


def norm_parts(r):
    n = r.shape[1]
    center = r - jnp.sum(r, axis=1, keepdims=True) * (1.0 / n)
    spread_ = jnp.sum(center * center, axis=1, keepdims=True) * (1.0 / n)
    rstd = lax.rsqrt(spread_ + 1e-05)
    return center * rstd, rstd


def norm_back(e, normed, rstd):
    n = e.shape[1]
    mean_e = jnp.sum(e, axis=1, keepdims=True) * (1.0 / n)
    mean_en = jnp.sum(e * normed, axis=1, keepdims=True) * (1.0 / n)
    return rstd * (e - mean_e - normed * mean_en)


def fold(a):
    return jnp.sum(a.reshape(a.shape[0] // 8, 8, a.shape[1]), axis=0)


def feed(x_ref, cot_ref, ctx_ref, wo_ref, wi_ref, wf_ref, vec_in_ref, small_ref,
         out_ref, gr1_ref, dc_ref, dwo_ref, dwi_ref, dwf_ref, vec_ref, bsum_ref,
         act_ref, gi_ref, hid_ref, gr2_ref, hidf_ref, turn_ref, gp_ref):
    length, width = x_ref.shape
    tn = wo_ref.shape[0]
    cols = width // tn
    units = wi_ref.shape[2]
    size = 256
    chunk = 512
    bo, g1, s1, bf, g2, s2 = [vec_in_ref[k : k + 1, :].astype(F32) for k in range(6)]
    bi = [side_row(small_ref, t, ROWS_BI, 12) for t in range(tn)]
    vec_ref[...] = jnp.zeros_like(vec_ref)
    bsum_ref[...] = jnp.zeros_like(bsum_ref)

    def step(i, carry):
        at = pl.ds(pl.multiple_of(i * size, size), size)
        attn = bo + x_ref[at, :].astype(F32)
        for t in range(tn):
            attn = attn + nt(ctx_ref[at, t * cols : (t + 1) * cols], wo_ref[t])
        n1, rstd1 = norm_parts(attn)
        hidden = n1 * g1 + s1
        hid = hidden.astype(BF)
        hid_ref[at, :] = hid
        r2 = hidden + bf
        for t in range(tn):
            for c in range(0, units, chunk):
                own = slice(t * units + c, t * units + c + chunk)
                u = nn(hid, wi_ref[t, :, c : c + chunk]) + bi[t][:, c : c + chunk]
                act, gp = gelu_both(u)
                act_ref[at, own] = act.astype(BF)
                gp_ref[:, own] = gp
        for t in range(tn):
            r2 = r2 + nt(act_ref[at, t * units : (t + 1) * units], wf_ref[t])
        n2, rstd2 = norm_parts(r2)
        out_ref[at, :] = (n2 * g2 + s2).astype(BF)
        cot = cot_ref[at, :].astype(F32)
        gr2 = norm_back(cot * g2, n2, rstd2)
        vec_ref[5] += fold(cot)
        vec_ref[4] += fold(cot * n2)
        vec_ref[3] += fold(gr2)
        low = gr2.astype(BF)
        gr2_ref[at, :] = low
        for t in range(tn):
            for c in range(0, units, chunk):
                own = slice(t * units + c, t * units + c + chunk)
                gi = nn(low, wf_ref[t, :, c : c + chunk]) * gp_ref[:, own]
                bsum_ref[:, own] += fold(gi)
                gi_ref[at, own] = gi.astype(BF)
        gh = gr2
        for t in range(tn):
            gh = gh + nt(gi_ref[at, t * units : (t + 1) * units], wi_ref[t])
        gr1 = norm_back(gh * g1, n1, rstd1)
        vec_ref[2] += fold(gh)
        vec_ref[1] += fold(gh * n1)
        vec_ref[0] += fold(gr1)
        low1 = gr1.astype(BF)
        gr1_ref[at, :] = low1
        for t in range(tn):
            dc_ref[at, t * cols : (t + 1) * cols] = nn(low1, wo_ref[t]).astype(BF)
        return carry

    lax.fori_loop(0, length // size, step, 0)

    turn_ref[...] = turn(gr2_ref[...])
    for t in range(tn):
        for c in range(0, units, chunk):
            own = slice(t * units + c, t * units + c + chunk)
            dwf_ref[t, :, c : c + chunk] = nn(turn_ref[...], act_ref[:, own]).astype(BF)
    turn_ref[...] = turn(hid_ref[...])
    for t in range(tn):
        for c in range(0, units, chunk):
            own = slice(t * units + c, t * units + c + chunk)
            dwi_ref[t, :, c : c + chunk] = nn(turn_ref[...], gi_ref[:, own]).astype(BF)
    turn_ref[...] = turn(gr1_ref[...])
    for t in range(tn):
        dwo_ref[t] = nn(turn_ref[...], ctx_ref[:, t * cols : (t + 1) * cols]).astype(BF)


def call_feed(x, cot, ctx, w, vec_in, small):
    length, width = x.shape
    tn = w.shape[0]
    cols = width // tn
    units = (w.shape[2] - 4 * cols) // 2
    s = jax.ShapeDtypeStruct
    big = s((length, width), BF)
    full = lambda a: pl.BlockSpec(a.shape, lambda i: (0,) * len(a.shape))
    outs = (big, big, big, s((tn, width, cols), BF), s((tn, width, units), BF), s((tn, width, units), BF),
            s((6, 8, width), F32), s((8, tn * units), F32))
    return pl.pallas_call(
        feed,
        grid=(1,),
        out_shape=outs,
        in_specs=[full(x), full(cot), full(ctx),
                  pl.BlockSpec((tn, width, cols), lambda i: (0, 0, 3)),
                  pl.BlockSpec((tn, width, units), lambda i: (0, 0, 1)),
                  pl.BlockSpec((tn, width, units), lambda i: (0, 0, 2)),
                  full(vec_in), full(small)],
        out_specs=tuple(full(o) for o in outs),
        scratch_shapes=[pltpu.VMEM((length, tn * units), BF), pltpu.VMEM((length, tn * units), BF),
                        pltpu.VMEM((length, width), BF), pltpu.VMEM((length, width), BF),
                        pltpu.VMEM((8, 128), F32), pltpu.VMEM((width, length), BF),
                        pltpu.VMEM((256, tn * units), F32)],
        compiler_params=pltpu.CompilerParams(vmem_limit_bytes=62 * 2**20),
        name="feed_forward",
    )(x, cot, ctx, w, w, w, vec_in, small)


def attend_backward(x_ref, w_ref, ids_ref, small_ref, q_ref, k_ref, v_ref, near_ref, far_ref, lq_ref, lk_ref, mix_ref,
                    sum_ref, ker_ref, z_ref, a_ref, v2_ref, w2_ref, dc_ref, gr1_ref,
                    gtok_ref, dw_ref, vecq_ref, vecv_ref, gtap_ref,
                    pre_ref, glq_ref, glk_ref, gsum_ref, gz_ref, gk_ref, padv_ref, padc_ref, xt_ref):
    length, width = x_ref.shape
    tn = w_ref.shape[0]
    cols = width // tn
    scale = LAND ** -0.25
    pairs = width // 128
    groups = width // 256
    ids = ids_ref[pl.ds(own_sequence(), 1), :]
    member = jnp.where(lax.broadcasted_iota(jnp.int32, (LAND, length), 0) == ids, 1.0, 0.0).astype(F32)
    count = jnp.sum(member, axis=1, keepdims=True)
    member = member.astype(BF)
    valid = ids < LAND
    eye = pair_eye()

    for g in range(groups):
        own = slice(g * 256, (g + 1) * 256)
        gsum_ref[:, own] = gather_diag(nn(near_ref[own, :], dc_ref[:, own]))
    for p in range(pairs):
        own = slice(p * 128, (p + 1) * 128)
        gmix = gsum_ref[:, own]
        gz_ref[:, own] = pair_nt(gmix, sum_ref[:, own])
        gsum_ref[:, own] = pair_nn(pair_turn(z_ref[ITERS, :, own]), gmix)

    gk_ref[...] = jnp.zeros_like(gk_ref)

    def iterate(m, carry):
        n = ITERS - 1 - m
        for p in range(pairs):
            own = slice(p * 128, (p + 1) * 128)
            grad = 0.25 * gz_ref[:, own]
            kernel = ker_ref[:, own]
            z = z_ref[n, :, own]
            a = a_ref[n, :, own]
            v2 = v2_ref[n, :, own]
            w2 = w2_ref[n, :, own]
            dw2 = pair_nn(pair_turn(z), grad)
            at = pair_turn(a)
            dv2 = -pair_nn(at, dw2)
            da = -pair_nt(dw2, v2) - pair_nt(dv2, 7.0 * eye - a) + pair_nn(at, dv2)
            gk_ref[:, own] += pair_nt(da, z)
            gz_ref[:, own] = pair_nt(grad, w2) + pair_nn(pair_turn(kernel), da)
        return carry

    lax.fori_loop(0, ITERS, iterate, 0)

    for p in range(pairs):
        own = slice(p * 128, (p + 1) * 128)
        kernel = ker_ref[:, own]
        gz = gz_ref[:, own]
        total = jnp.sum(pair_sum(kernel * kernel), axis=0, keepdims=True)
        kt = pair_turn(kernel)
        back = jnp.sum(pair_sum(gz * kt), axis=0, keepdims=True)
        gk = gk_ref[:, own] + pair_turn(gz) / total - kernel * (2.0 * back / (total * total))
        mid = kernel * (gk - pair_sum(kernel * gk))
        glq_ref[:, own] = pair_nn(mid, lk_ref[:, own].astype(F32))
        glk_ref[:, own] = pair_nn(pair_turn(mid), lq_ref[:, own].astype(F32))

    flip = jnp.where(
        lax.broadcasted_iota(jnp.int32, (256, 256), 0) + lax.broadcasted_iota(jnp.int32, (256, 256), 1) == 255, 1.0, 0.0
    ).astype(BF)
    padv_ref[...] = jnp.zeros_like(padv_ref)
    padc_ref[...] = jnp.zeros_like(padc_ref)
    inner = slice(128, 128 + length)
    for g in range(groups):
        own = slice(g * 256, (g + 1) * 256)
        lk4 = spread(lk_ref[:, own])
        lq4 = spread(lq_ref[:, own])
        near = near_ref[own, :].astype(F32)
        gnear = nt(spread(mix_ref[:, own]), dc_ref[:, own])
        drop = jnp.sum((near * gnear).reshape(4, LAND, length), axis=1, keepdims=True)
        first = (near * (gnear.reshape(4, LAND, length) - drop).reshape(256, length)).astype(BF)
        glk_ref[:, own] += gather_diag(nn(first, q_ref[:, own]))
        gsum4 = spread(gsum_ref[:, own].astype(BF))
        far = far_ref[own, :].astype(F32)
        gfar = nt(gsum4, v_ref[:, own])
        drop = jnp.sum(far * gfar, axis=1, keepdims=True)
        third = (far * (gfar - drop)).astype(BF)
        glq_ref[:, own] += gather_diag(nn(third, k_ref[:, own]))
        glq = turn((glq_ref[:, own] / count).astype(BF))
        glk = turn((glk_ref[:, own] / count).astype(BF))
        dq = (nn(turn(lk4), first) + nn(glq, member)) * scale
        dk = (nn(turn(lq4), third) + nn(glk, member)) * scale
        dv = nn(turn(gsum4), far_ref[own, :])

        vt = turn(v_ref[:, own])
        padv_ref[:, inner] = jnp.where(valid, vt, jnp.zeros_like(vt))
        padc_ref[:, inner] = turn(dc_ref[:, own])
        parts = []
        for h in range(4):
            band = band_of(small_ref, 4 * g + h, ROWS_FLIP)
            parts.append(unblock(nt(blocks_of(padc_ref, h * LAND, 256), band), 256))
            plain = jnp.concatenate(
                [padc_ref[h * LAND : (h + 1) * LAND, 128 + at : 128 + at + 256] for at in range(0, length, 256)], axis=0
            )
            gram = nn(nt(flip, plain).astype(BF), blocks_of(padv_ref, h * LAND, 256))
            gram = pltpu.roll(gram, 0, 1, stride=1, stride_axis=0)
            gtap_ref[4 * g + h : 4 * g + h + 1, :] = jnp.sum(gram, axis=0, keepdims=True)
        dv = dv + jnp.where(valid, jnp.concatenate(parts, axis=0), 0.0)
        vecq_ref[own, :] = jnp.sum(dq, axis=1, keepdims=True)
        vecv_ref[own, :] = jnp.sum(dv, axis=1, keepdims=True)
        for lower in range(0, 256, 128):
            c = g * 256 + lower
            t, r = c // cols, c % cols
            pre_ref[t, r : r + 128, :] = dq[lower : lower + 128].astype(BF)
            pre_ref[t, cols + r : cols + r + 128, :] = dk[lower : lower + 128].astype(BF)
            pre_ref[t, 2 * cols + r : 2 * cols + r + 128, :] = dv[lower : lower + 128].astype(BF)

    xt_ref[...] = turn(x_ref[...])
    for t in range(tn):
        dw_ref[t] = nt(xt_ref[...], pre_ref[t]).astype(BF)
    for at in range(0, length, 256):
        part = nn(w_ref[0], pre_ref[0, :, at : at + 256])
        for t in range(1, tn):
            part = part + nn(w_ref[t], pre_ref[t, :, at : at + 256])
        gtok_ref[at : at + 256, :] = (gr1_ref[at : at + 256, :].astype(F32) + turn(part)).astype(BF)


def call_attend_backward(x, w, ids, small, saved, dc, gr1):
    (q, k, v, near, far, lq, lk, mix, summ, ker, z, a, v2, w2) = saved
    length, width = x.shape
    tn = w.shape[0]
    cols = width // tn
    s = jax.ShapeDtypeStruct
    full = lambda a: pl.BlockSpec(a.shape, lambda i: (0,) * len(a.shape))
    outs = (s((length, width), BF), s((tn, width, 3 * cols), BF), s((width, 1), F32), s((width, 1), F32),
            s((width // LAND, 512), F32))
    args = (x, w, ids, small, q, k, v, near, far, lq, lk, mix, summ, ker, z, a, v2, w2, dc, gr1)
    specs = [full(b) for b in args]
    specs[1] = pl.BlockSpec((tn, width, 3 * cols), lambda i: (0, 0, 0))
    small = pltpu.VMEM((LAND, width), F32)
    return pl.pallas_call(
        attend_backward,
        grid=(1,),
        out_shape=outs,
        in_specs=specs,
        out_specs=tuple(full(o) for o in outs),
        scratch_shapes=[pltpu.VMEM((tn, 3 * cols, length), BF), small, small, small, small, small,
                        pltpu.VMEM((256, length + 256), BF), pltpu.VMEM((256, length + 256), BF),
                        pltpu.VMEM((width, length), BF)],
        compiler_params=pltpu.CompilerParams(vmem_limit_bytes=60 * 2**20),
        name="attend_backward",
    )(*args)


FLIP_AT = 367
MESH = pl.DeviceIdType.MESH


class Place:
    def __init__(self, dp, tn):
        self.dp, self.tn = dp, tn
        self.nz = dp // 4
        i = lax.axis_index("dp")
        self.i = i
        self.t = lax.axis_index("tensor")
        self.c = lax.rem(i, 2)
        self.x = lax.rem(i // 2, 2)
        self.z = i // 4

    def at(self, z=None, x=None, c=None, t=None):
        z = self.z if z is None else z
        x = self.x if x is None else x
        c = self.c if c is None else c
        t = self.t if t is None else t
        return (z * 4 + x * 2 + c, t)


def greet(me):
    bar = pltpu.get_barrier_semaphore()
    for k in range(1, me.dp):
        pl.semaphore_signal(bar, 1, device_id=(lax.rem(me.i + k, me.dp), me.t), device_id_type=MESH)
    pl.semaphore_signal(bar, 1, device_id=(me.i, 1 - me.t), device_id_type=MESH)
    pl.semaphore_wait(bar, me.dp)


def remote(src, dst, ss, rs, to):
    return pltpu.make_async_remote_copy(
        src_ref=src, dst_ref=dst, send_sem=ss, recv_sem=rs, device_id=to, device_id_type=MESH
    )


class ToOwner:
    def __init__(self, me, src, out, ss, rs, local):
        self.copies = []
        for k in range(1, me.dp):
            j = lax.rem(me.i + k, me.dp)
            self.copies.append(remote(src.at[me.t * me.dp + j], out.at[me.i], ss.at[k], rs.at[k], (j, me.t)))
        self.own = pltpu.make_async_copy(src.at[me.t * me.dp + me.i], out.at[me.i], local)

    def start(self):
        for c in self.copies:
            c.start()
        self.own.start()

    def wait(self):
        for c in self.copies:
            c.wait()
        self.own.wait()


def gather_steps(me, src, out, ss, rs, local, cuts):
    t, z, x, c = me.t, me.z, me.x, me.c
    n = me.nz
    px, py, sib = me.at(x=1 - x), me.at(t=1 - t), me.at(c=1 - c)
    lanes = []
    for q, (lo, hi) in enumerate(cuts):
        w = pl.ds(lo, hi - lo)
        base = q * (n + 4)

        def move(ref, k, to):
            return remote(ref, ref, ss.at[base + k], rs.at[base + k], to)

        own = pltpu.make_async_copy(src.at[:, w], out.at[t, z, x, c, :, w], local.at[q])
        zs = []
        for k in range(1, n):
            to = me.at(z=lax.rem(z + k, n))
            zs.append(remote(src.at[:, w], out.at[t, z, x, c, :, w], ss.at[base + k], rs.at[base + k], to))
        if q % 2 == 0:
            first, second = move(out.at[t, :, x, c, :, w], n, px), move(out.at[t, :, :, c, :, w], n + 1, py)
            d2, d3 = move(out.at[t, :, :, c, :, w], n + 2, sib), move(out.at[1 - t, :, :, c, :, w], n + 3, sib)
        else:
            first, second = move(out.at[t, :, x, c, :, w], n, py), move(out.at[:, :, x, c, :, w], n + 1, px)
            d2, d3 = move(out.at[:, :, x, c, :, w], n + 2, sib), move(out.at[:, :, 1 - x, c, :, w], n + 3, sib)
        lanes.append([([], zs + [own]), (zs + [own], [first]), ([first], [second, d2]), ([second], [d3]), ([d2, d3], [])])
    depth = len(lanes[0])
    order = []
    for step in range(depth + len(lanes) // 2):
        for q in range(len(lanes)):
            if 0 <= step - q // 2 < depth:
                order.append(lanes[q][step - q // 2])
    return order


def run_stage(stage):
    for c in stage[0]:
        c.wait()
    for c in stage[1]:
        c.start()


def gather_sems(dp, chunks):
    n = (dp // 4 + 4) * chunks
    return [pltpu.SemaphoreType.DMA((n,)), pltpu.SemaphoreType.DMA((n,)), pltpu.SemaphoreType.DMA((chunks,))]


def even_cuts(width, n):
    return [(k * width // n, (k + 1) * width // n) for k in range(n)]


def owner_sems(dp):
    return [pltpu.SemaphoreType.DMA((dp,)), pltpu.SemaphoreType.DMA((dp,)), pltpu.SemaphoreType.DMA]


ANY = pl.BlockSpec(memory_space=pl.ANY)


def bring(dp, tn, order, chunks, *refs):
    n = len(order)
    ins, outs, sems = refs[:n], refs[n : 2 * n], refs[2 * n :]
    me = Place(dp, tn)
    greet(me)
    plans = []
    for k, kind in enumerate(order):
        s = sems[3 * k : 3 * k + 3]
        if kind == "pair":
            side = remote(ins[k], outs[k].at[me.t], s[0].at[0], s[1].at[0], (me.i, 1 - me.t))
            here = pltpu.make_async_copy(ins[k], outs[k].at[me.t], s[2])
            plans.append([([], [side, here]), ([side, here], [])])
        elif kind == "rows":
            plan = ToOwner(me, ins[k], outs[k], *s)
            plans.append([([], plan.copies + [plan.own]), (plan.copies + [plan.own], [])])
        else:
            w = ins[k].shape[1]
            plans.append(gather_steps(me, ins[k], outs[k], *s, even_cuts(w, chunks)))
    for p in plans:
        run_stage(p[0])
    for p, kind in zip(plans, order):
        if kind == "w":
            for st in p[1:]:
                run_stage(st)
    for p, kind in zip(plans, order):
        if kind != "w":
            for st in p[1:]:
                run_stage(st)


def call_bring(dp, tn, order, arrays, cid, chunks=4):
    outs, scratch = [], []
    for kind, a in zip(order, arrays):
        if kind == "pair":
            outs.append(jax.ShapeDtypeStruct((tn,) + a.shape, a.dtype))
            scratch += owner_sems(1)
        elif kind == "rows":
            outs.append(jax.ShapeDtypeStruct((dp,) + a.shape[1:], a.dtype))
            scratch += owner_sems(dp)
        else:
            outs.append(jax.ShapeDtypeStruct((tn, dp // 4, 2, 2) + a.shape, a.dtype))
            scratch += gather_sems(dp, chunks)
    return pl.pallas_call(
        functools.partial(bring, dp, tn, order, chunks),
        out_shape=tuple(outs),
        in_specs=[ANY] * len(arrays),
        out_specs=tuple([ANY] * len(outs)),
        scratch_shapes=scratch,
        compiler_params=pltpu.CompilerParams(collective_id=cid, has_side_effects=True),
        name="bring",
    )(*arrays)


def add_low(a, b):
    return (a.astype(F32) + b.astype(F32)).astype(BF)


def rows_home(me, src, out, ss, rs, local):
    mine = me.t * me.dp + me.i
    first, second = [], []
    for k in range(1, me.dp):
        j = lax.rem(me.i + k, me.dp)
        first.append(remote(src.at[j], out.at[mine], ss.at[k], rs.at[k], (j, me.t)))
    own = pltpu.make_async_copy(src.at[me.i], out.at[mine], local)
    partner = (me.i, 1 - me.t)
    n = me.dp
    second.append(remote(src.at[me.i], out.at[mine], ss.at[n], rs.at[n], partner))
    for k in range(1, me.dp):
        j = me.t * me.dp + lax.rem(me.i + me.dp - k, me.dp)
        second.append(remote(out.at[j], out.at[j], ss.at[n + k], rs.at[n + k], partner))
    return first, own, second


def reduce_lane(me, k, src, lo, w, bufs, ss, rs, puts):
    t, z, x, c = me.t, me.z, me.x, me.c
    n = me.nz
    base = k * (n + 2)
    rc, rx, ry, rz = bufs
    cols = pl.ds(0, w)
    own = pl.ds(lo, w)

    def move(a, b, q, to):
        return remote(a, b, ss.at[base + q], rs.at[base + q], to)

    core = move(src.at[:, :, :, 1 - c, :, own], rc.at[:, :, :, :, cols], 0, me.at(c=1 - c))
    east = move(rc.at[:, :, 1 - x, :, cols], rx.at[:, :, :, cols], 1, me.at(x=1 - x))
    north = move(rx.at[1 - t, :, :, cols], ry.at[:, :, cols], 2, me.at(t=1 - t))
    lines = []
    for q in range(1, n):
        to = lax.rem(z + q, n)
        lines.append(move(ry.at[to, :, cols], rz.at[q, :, cols], 2 + q, me.at(z=to)))

    def s0():
        core.start()

    def s1():
        core.wait()
        rc[:, :, :, :, :w] = add_low(rc[:, :, :, :, :w], src[:, :, :, c, :, own])
        east.start()

    def s2():
        east.wait()
        rx[:, :, :, :w] = add_low(rx[:, :, :, :w], rc[:, :, x, :, :w])
        north.start()

    def s3():
        north.wait()
        ry[:, :, :w] = add_low(ry[:, :, :w], rx[t, :, :, :w])
        for m in lines:
            m.start()

    def s4():
        total = ry[z, :, :w].astype(F32)
        for m in lines:
            m.wait()
        for q in range(1, n):
            total = total + rz[q, :, :w].astype(F32)
        for dst, at, first, width in puts:
            dst[:, at : at + width] = total[:, first : first + width]

    return [s0, s1, s2, s3, s4]


def carry_home(dp, tn, count, n_dst, chunks, *refs):
    n_in = 4 + count
    o_rows, g_rows = refs[:2]
    grads = refs[2 : 2 + count]
    norms, rest = refs[2 + count : n_in]
    o_home, g_home = refs[n_in : n_in + 2]
    douts = refs[n_in + 2 : n_in + 2 + n_dst]
    n_out, r_out = refs[n_in + 2 + n_dst : n_in + 4 + n_dst]
    sc = list(refs[n_in + 4 + n_dst :])
    me = Place(dp, tn)
    row_sems = [sc[0:3], sc[3:6]]
    v_ss, v_rs, nbuf, rbuf, nall, rall, nsum, rsum = sc[6:14]
    g_ss, g_rs = sc[14:16]
    bufs = [sc[16 + 4 * k : 20 + 4 * k] for k in range(len(chunks))]
    greet(me)
    plans = [rows_home(me, a, b, *s) for a, b, s in ((o_rows, o_home, row_sems[0]), (g_rows, g_home, row_sems[1]))]
    partner = (me.i, 1 - me.t)
    v1 = [remote(norms, nbuf, v_ss.at[0], v_rs.at[0], partner),
          remote(rest.at[1 - me.t], rbuf, v_ss.at[1], v_rs.at[1], partner)]
    lanes = [reduce_lane(me, k, grads[g], lo, w, bufs[k], g_ss, g_rs, [(douts[d],) + tuple(r) for d, *r in puts])
             for k, (g, lo, w, puts) in enumerate(chunks)]
    for lane in lanes:
        lane[0]()
    for c in v1:
        c.start()
    for first, own, second in plans:
        for c in first:
            c.start()
        own.start()
        second[0].start()
    for c in v1:
        c.wait()
    nsum[...] = norms[...] + nbuf[...]
    rsum[...] = rest[me.t] + rbuf[...]
    v2 = []
    for k in range(1, dp):
        j = lax.rem(me.i + k, dp)
        v2.append(remote(nsum.at[j], nall.at[k], v_ss.at[2 * k], v_rs.at[2 * k], (j, me.t)))
        v2.append(remote(rsum, rall.at[k], v_ss.at[2 * k + 1], v_rs.at[2 * k + 1], (j, me.t)))
    for c in v2:
        c.start()
    for s in (1, 2):
        for lane in lanes:
            lane[s]()
    for first, own, second in plans:
        for a, b in zip(first, second[1:]):
            a.wait()
            b.start()
    for s in (3, 4):
        for lane in lanes:
            lane[s]()
    for c in v2:
        c.wait()
    ntot = nsum[me.i]
    rtot = rsum[...]
    for k in range(1, dp):
        ntot = ntot + nall[k]
        rtot = rtot + rall[k]
    n_out[...] = ntot
    r_out[...] = rtot
    for first, own, second in plans:
        own.wait()
        for c in second:
            c.wait()


def call_carry_home(dp, tn, o_rows, g_rows, grads, chunks, widths, norms, rest, cid):
    s = jax.ShapeDtypeStruct
    count = len(grads)
    nz = dp // 4
    r, w = o_rows.shape[1:]
    depth = grads[0].shape[4]
    home = s((tn * dp, r, w), BF)
    douts = [s((depth, w2), F32) for w2 in widths]
    outs = [home, home] + douts + [s(norms.shape[1:], F32), s(rest.shape[1:], F32)]
    dma = pltpu.SemaphoreType.DMA
    scratch = [dma((2 * dp,)), dma((2 * dp,)), dma, dma((2 * dp,)), dma((2 * dp,)), dma,
               dma((2 * dp,)), dma((2 * dp,)),
               pltpu.VMEM(norms.shape, F32), pltpu.VMEM(rest.shape[1:], F32),
               pltpu.VMEM((dp,) + norms.shape[1:], F32), pltpu.VMEM((dp,) + rest.shape[1:], F32),
               pltpu.VMEM(norms.shape, F32), pltpu.VMEM(rest.shape[1:], F32),
               dma(((nz + 2) * len(chunks),)), dma(((nz + 2) * len(chunks),))]
    for _, _, gw, _ in chunks:
        scratch += [pltpu.VMEM((tn, nz, 2, depth, gw), BF), pltpu.VMEM((tn, nz, depth, gw), BF),
                    pltpu.VMEM((nz, depth, gw), BF), pltpu.VMEM((nz, depth, gw), BF)]
    vm = pl.BlockSpec(memory_space=pltpu.VMEM)
    return pl.pallas_call(
        functools.partial(carry_home, dp, tn, count, len(widths), chunks),
        out_shape=tuple(outs),
        in_specs=[ANY, ANY] + [vm] * (count + 2),
        out_specs=tuple([ANY, ANY] + [vm] * (len(widths) + 2)),
        scratch_shapes=scratch,
        compiler_params=pltpu.CompilerParams(
            collective_id=cid, has_side_effects=True, vmem_limit_bytes=60 * 2**20
        ),
        name="carry_home",
    )(o_rows, g_rows, *grads, norms, rest)


def local(tokens, cotangent, landmark_ids, w_query, w_key, w_value, b_query, b_value, conv_taps, w_out, b_out,
          first_gain, first_shift, w_inner, b_inner, w_outer, b_outer, second_gain, second_shift):
    dp = lax.axis_size("dp")
    tn = lax.axis_size("tensor")
    here = lax.axis_index("dp")
    tens = lax.axis_index("tensor")
    part, width = tokens.shape[1:]
    length = dp * part
    cols = w_query.shape[1]
    units = w_inner.shape[1]
    heads, taps = conv_taps.shape
    packed = jnp.concatenate([w_query, w_key, w_value, w_out, w_inner, w_outer], axis=1)
    tap_rows = jnp.pad(conv_taps.astype(F32), ((0, 0), (0, 128 - taps)))
    flip_rows = jnp.pad(conv_taps[:, ::-1].astype(F32), ((0, 0), (0, 128 - taps)))
    flat = jnp.concatenate([b_query, b_value, b_inner]).astype(F32).reshape(-1, 128)
    small = jnp.concatenate([flat, tap_rows, flip_rows, jnp.zeros((2, 128), F32)], axis=0)
    vec_in = jnp.stack([b_out, first_gain, first_shift, b_outer, second_gain, second_shift])

    rows, cot, whole, small = call_bring(
        dp, tn, ("rows", "rows", "w", "pair"), (tokens, cotangent, packed, small), 0, 6
    )
    rows = rows.reshape(length, width)
    cot = cot.reshape(length, width)
    whole = whole.reshape(tn, width, packed.shape[1])
    q, k, v, near, far, ctx, *rest_saved = call_attend_forward(rows, whole, small, landmark_ids)
    out_rows, gr1, dc, dwo, dwi, dwf, vec, bsum = call_feed(rows, cot, ctx, whole, vec_in, small)
    grad_rows, dwqkv, gbq, gbv, gtap = call_attend_backward(
        rows, whole, landmark_ids, small, (q, k, v, near, far, *rest_saved), dc, gr1
    )
    share = width // dp
    norms = jnp.sum(vec, axis=1).reshape(6, dp, share).transpose(1, 0, 2).reshape(dp, 6 * share)
    norms = jnp.pad(norms, ((0, 0), (0, 1024 - 6 * share))).reshape(dp, 8, 128)
    rest = jnp.concatenate(
        [gbq.reshape(tn, cols), gbv.reshape(tn, cols), jnp.sum(bsum, axis=0).reshape(tn, units),
         gtap[:, FLIP_AT : FLIP_AT + taps].reshape(tn, heads * taps)], axis=1)
    rest = jnp.pad(rest, ((0, 0), (0, 24 * 128 - rest.shape[1]))).reshape(tn, 24, 128)

    def cut(g):
        return g.reshape(tn, dp // 4, 2, 2, width // dp, g.shape[2])

    half = units // 2
    chunks = (
        (2, 0, half, ((5, 0, 0, half),)), (2, half, half, ((5, half, 0, half),)),
        (1, 0, half, ((4, 0, 0, half),)), (1, half, half, ((4, half, 0, half),)),
        (0, 0, cols, ((3, 0, 0, cols),)),
        (3, 0, 3 * cols, ((0, 0, 0, cols), (1, 0, cols, cols), (2, 0, 2 * cols, cols))),
    )
    out_home, grad_home, gq, gk, gv, go, gi, gf, nsum, rsum = call_carry_home(
        dp, tn, out_rows.reshape(dp, part, width), grad_rows.reshape(dp, part, width),
        [cut(dwo), cut(dwi), cut(dwf), cut(dwqkv)], chunks, (cols, cols, cols, cols, units, units), norms, rest, 1
    )
    n = nsum.reshape(-1)[: 6 * share].reshape(6, share)
    r = rsum.reshape(-1)
    at = 2 * cols + units
    return (out_home, grad_home, gq, gk, gv, r[:cols], r[cols : 2 * cols],
            r[at : at + heads * taps].reshape(heads, taps), go, n[0], n[1], n[2], gi, r[2 * cols : at], gf,
            n[3], n[4], n[5])


def solution(mesh):
    return jax.shard_map(
        local,
        mesh=mesh,
        in_specs=(
            P(None, "dp", None),
            P(None, "dp", None),
            P(),
            P("dp", "tensor"),
            P("dp", "tensor"),
            P("dp", "tensor"),
            P("tensor"),
            P("tensor"),
            P("tensor", None),
            P("dp", "tensor"),
            P(),
            P(),
            P(),
            P("dp", "tensor"),
            P("tensor"),
            P("dp", "tensor"),
            P(),
            P(),
            P(),
        ),
        out_specs=(
            P(None, "dp", None),
            P(None, "dp", None),
            P("dp", "tensor"),
            P("dp", "tensor"),
            P("dp", "tensor"),
            P("tensor"),
            P("tensor"),
            P("tensor", None),
            P("dp", "tensor"),
            P("dp"),
            P("dp"),
            P("dp"),
            P("dp", "tensor"),
            P("tensor"),
            P("dp", "tensor"),
            P("dp"),
            P("dp"),
            P("dp"),
        ),
        check_vma=False,
    )
```

```python
import functools

import jax
import jax.numpy as jnp
from jax import lax
from jax.experimental import pallas as pl
from jax.experimental.pallas import tpu as pltpu
from jax.sharding import PartitionSpec as P

F32 = jnp.float32
BF = jnp.bfloat16
MESH = pl.DeviceIdType.MESH
ANY = pl.BlockSpec(memory_space=pl.ANY)
VM = pl.BlockSpec(memory_space=pltpu.VMEM)
DMA = pltpu.SemaphoreType.DMA
SMALL_ROWS = 32


class Place:
    def __init__(self, dp, tn):
        self.dp, self.tn = dp, tn
        self.nz = dp // 4
        i = lax.axis_index("dp")
        self.i = i
        self.t = lax.axis_index("tensor")
        self.c = lax.rem(i, 2)
        self.x = lax.rem(i // 2, 2)
        self.z = i // 4

    def at(self, z=None, x=None, c=None, t=None):
        z = self.z if z is None else z
        x = self.x if x is None else x
        c = self.c if c is None else c
        t = self.t if t is None else t
        return (z * 4 + x * 2 + c, t)


def greet(me, rows=True):
    bar = pltpu.get_barrier_semaphore()
    if rows:
        peers = [(lax.rem(me.i + k, me.dp), me.t) for k in range(1, me.dp)]
    else:
        peers = [me.at(z=lax.rem(me.z + k, me.nz)) for k in range(1, me.nz)] + [me.at(x=1 - me.x), me.at(c=1 - me.c)]
    peers.append((me.i, 1 - me.t))
    for p in peers:
        pl.semaphore_signal(bar, 1, device_id=p, device_id_type=MESH)
    pl.semaphore_wait(bar, len(peers))


def remote(src, dst, ss, rs, to):
    return pltpu.make_async_remote_copy(
        src_ref=src, dst_ref=dst, send_sem=ss, recv_sem=rs, device_id=to, device_id_type=MESH
    )


def start_all(copies):
    for c in copies:
        c.start()


def wait_all(copies):
    for c in copies:
        c.wait()


def to_owner(me, src, out, ss, rs, local):
    copies = []
    for k in range(1, me.dp):
        j = lax.rem(me.i + k, me.dp)
        copies.append(remote(src.at[me.t * me.dp + j], out.at[me.i], ss.at[k], rs.at[k], (j, me.t)))
    copies.append(pltpu.make_async_copy(src.at[me.t * me.dp + me.i], out.at[me.i], local))
    return copies


def to_home(me, src, out, ss, rs, local):
    copies = []
    for k in range(1, me.dp):
        j = lax.rem(me.i + k, me.dp)
        copies.append(remote(src.at[j], out.at[me.i], ss.at[k], rs.at[k], (j, me.t)))
    copies.append(pltpu.make_async_copy(src.at[me.i], out.at[me.i], local))
    return copies


def gather_lane(me, src, own, out, cols, north_first, ss, rs, local):
    t, z, x, c, n = me.t, me.z, me.x, me.c, me.nz
    px, py, sib = me.at(x=1 - x), me.at(t=1 - t), me.at(c=1 - c)

    def move(ref, k, to):
        return remote(ref, ref, ss.at[k], rs.at[k], to)

    zs = [pltpu.make_async_copy(src.at[:, own], out.at[t, z, x, c, :, cols], local)]
    for k in range(1, n):
        to = me.at(z=lax.rem(z + k, n))
        zs.append(remote(src.at[:, own], out.at[t, z, x, c, :, cols], ss.at[k], rs.at[k], to))
    if north_first:
        first, second = move(out.at[t, :, x, c, :, cols], n, py), move(out.at[:, :, x, c, :, cols], n + 1, px)
        d2, d3 = move(out.at[:, :, x, c, :, cols], n + 2, sib), move(out.at[:, :, 1 - x, c, :, cols], n + 3, sib)
    else:
        first, second = move(out.at[t, :, x, c, :, cols], n, px), move(out.at[t, :, :, c, :, cols], n + 1, py)
        d2, d3 = move(out.at[t, :, :, c, :, cols], n + 2, sib), move(out.at[1 - t, :, :, c, :, cols], n + 3, sib)

    def s0():
        start_all(zs)

    def s1():
        wait_all(zs)
        first.start()

    def s2():
        first.wait()
        second.start()
        d2.start()

    def s3():
        second.wait()
        d3.start()

    def s4():
        d2.wait()
        d3.wait()

    return [s0, s1, s2, s3, s4]


def gather_count(dp):
    return dp // 4 + 4


def add_low(a, b):
    return (a.astype(F32) + b.astype(F32)).astype(BF)


def reduce_lane(me, src, lo, w, bufs, ss, rs, local, puts):
    t, z, x, c, n = me.t, me.z, me.x, me.c, me.nz
    mine, rc, rx, ry, rz = bufs
    cols = pl.ds(lo, w)

    def move(a, b, q, to):
        return remote(a, b, ss.at[q], rs.at[q], to)

    keep = pltpu.make_async_copy(src.at[:, :, :, c, :, cols], mine, local)
    core = move(src.at[:, :, :, 1 - c, :, cols], rc, 0, me.at(c=1 - c))
    east = move(rc.at[:, :, 1 - x], rx, 1, me.at(x=1 - x))
    north = move(rx.at[1 - t], ry, 2, me.at(t=1 - t))
    lines = []
    for q in range(1, n):
        to = lax.rem(z + q, n)
        lines.append(move(ry.at[to], rz.at[q], 2 + q, me.at(z=to)))

    def s0():
        keep.start()
        core.start()

    def s1():
        keep.wait()
        core.wait()
        rc[...] = add_low(rc[...], mine[...])
        east.start()

    def s2():
        east.wait()
        rx[...] = add_low(rx[...], rc[:, :, x])
        north.start()

    def s3():
        north.wait()
        ry[...] = add_low(ry[...], rx[t])
        start_all(lines)

    def s4():
        total = ry[z].astype(F32)
        wait_all(lines)
        for q in range(1, n):
            total = total + rz[q].astype(F32)
        for dst, at, first, width in puts:
            dst[:, at : at + width] = total[:, first : first + width]

    return [s0, s1, s2, s3, s4]


def reduce_bufs(dp, tn, depth, w):
    nz = dp // 4
    return [pltpu.VMEM((tn, nz, 2, depth, w), BF), pltpu.VMEM((tn, nz, 2, depth, w), BF),
            pltpu.VMEM((tn, nz, depth, w), BF), pltpu.VMEM((nz, depth, w), BF), pltpu.VMEM((nz, depth, w), BF)]


def reduce_count(dp):
    return dp // 4 + 2


class Sub:
    def __init__(self, ref, base):
        self.ref, self.base = ref, base

    @property
    def at(self):
        return self

    def __getitem__(self, k):
        return self.ref.at[self.base + k]


class Ticks:
    def __init__(self, stages):
        self.stages = list(stages)

    def __call__(self, count=1):
        for _ in range(min(count, len(self.stages))):
            self.stages.pop(0)()

    def rest(self):
        self(len(self.stages))


def sems(n):
    return [DMA((n,)), DMA((n,))]


def params(cid, mib):
    return pltpu.CompilerParams(collective_id=cid, has_side_effects=True, vmem_limit_bytes=mib * 2**20)


def bring(dp, tn, tok, wq, wk, wv, wo, bq, bv, bi, taps, rows, wqkv, wout, small,
          r_ss, r_rs, g_ss, g_rs, local, piece):
    me = Place(dp, tn)
    cols = wq.shape[1]
    n = gather_count(dp)
    lanes = []
    for k, (src, dst, lo) in enumerate(((wq, wqkv, 0), (wk, wqkv, cols), (wv, wqkv, 2 * cols), (wo, wout, 0))):
        lanes.append(gather_lane(me, src, pl.ds(0, cols), dst, pl.ds(lo, cols), k % 2 == 1,
                                 Sub(g_ss, k * n), Sub(g_rs, k * n), local.at[k]))
    piece[...] = jnp.zeros_like(piece)
    for ref, first in ((bq, ROWS_BQ), (bv, ROWS_BV), (bi, ROWS_BI)):
        for r in range(ref.shape[1] // 128):
            piece[first + r : first + r + 1, :] = ref[:, r * 128 : (r + 1) * 128].astype(F32)
    heads, width = taps.shape
    tap = taps[...].astype(F32)
    piece[ROWS_TAPS : ROWS_TAPS + heads, :width] = tap
    greet(me)
    for s in (0, 1):
        for lane in lanes[2 * s : 2 * s + 2]:
            lane[0]()
    moved = to_owner(me, tok, rows, r_ss, r_rs, local.at[4])
    start_all(moved)
    side = [remote(piece, small.at[me.t], r_ss.at[0], r_rs.at[0], (me.i, 1 - me.t)),
            pltpu.make_async_copy(piece, small.at[me.t], local.at[5])]
    start_all(side)
    for pair, stage in ((0, 1), (0, 2), (1, 1), (0, 3), (1, 2), (1, 3), (0, 4), (1, 4)):
        for lane in lanes[2 * pair : 2 * pair + 2]:
            lane[stage]()
    wait_all(side)
    wait_all(moved)


def call_bring(dp, tn, tok, wq, wk, wv, wo, bq, bv, bi, taps):
    s = jax.ShapeDtypeStruct
    depth, cols = wq.shape
    lead = (tn, dp // 4, 2, 2, depth)
    outs = (s((dp,) + tok.shape[1:], BF), s(lead + (3 * cols,), BF), s(lead + (cols,), BF), s((tn, SMALL_ROWS, 128), F32))
    return pl.pallas_call(
        functools.partial(bring, dp, tn),
        out_shape=outs,
        in_specs=[ANY] * 5 + [VM] * 4,
        out_specs=(ANY, ANY, ANY, ANY),
        scratch_shapes=sems(dp) + sems(4 * gather_count(dp)) + [DMA((6,)), pltpu.VMEM((SMALL_ROWS, 128), F32)],
        compiler_params=params(0, 16),
        name="bring",
    )(tok, wq, wk, wv, wo, bq, bv, bi, taps)


def carry_home(dp, tn, g_rows, dwqkv, norms, rest, g_home, gq, gk, gv, n_out, r_out,
               r_ss, r_rs, v_ss, v_rs, g_ss, g_rs, local, nbuf, rbuf, nall, rall, nsum, rsum, *bufs):
    me = Place(dp, tn)
    cols = gq.shape[1]
    n = reduce_count(dp)
    lanes = []
    for k, dst in enumerate((gq, gk, gv)):
        lanes.append(reduce_lane(me, dwqkv, k * cols, cols, bufs[5 * k : 5 * k + 5], Sub(g_ss, k * n), Sub(g_rs, k * n),
                                 local.at[1 + k], [(dst, 0, 0, cols)]))
    greet(me)
    mine = me.t * dp
    first = []
    for k in range(1, dp):
        j = lax.rem(me.i + k, dp)
        first.append(remote(g_rows.at[j], g_home.at[mine + me.i], r_ss.at[k], r_rs.at[k], (j, me.t)))
    own = pltpu.make_async_copy(g_rows.at[me.i], g_home.at[mine + me.i], local.at[0])
    partner = (me.i, 1 - me.t)
    second = [remote(g_rows.at[me.i], g_home.at[mine + me.i], r_ss.at[dp], r_rs.at[dp], partner)]
    for k in range(1, dp):
        j = mine + lax.rem(me.i + dp - k, dp)
        second.append(remote(g_home.at[j], g_home.at[j], r_ss.at[dp + k], r_rs.at[dp + k], partner))
    v1 = [remote(norms, nbuf, v_ss.at[0], v_rs.at[0], partner),
          remote(rest.at[1 - me.t], rbuf, v_ss.at[1], v_rs.at[1], partner)]
    for lane in lanes:
        lane[0]()
    start_all(v1)
    start_all(first)
    own.start()
    second[0].start()
    for lane in lanes:
        lane[1]()
    wait_all(v1)
    nsum[...] = norms[...] + nbuf[...]
    rsum[...] = rest[me.t] + rbuf[...]
    v2 = []
    for k in range(1, dp):
        j = lax.rem(me.i + k, dp)
        v2.append(remote(nsum.at[j], nall.at[k], v_ss.at[2 * k], v_rs.at[2 * k], (j, me.t)))
        v2.append(remote(rsum, rall.at[k], v_ss.at[2 * k + 1], v_rs.at[2 * k + 1], (j, me.t)))
    start_all(v2)
    todo = list(zip(first, second[1:]))
    stages = [lane[s] for s in (2, 3) for lane in lanes]
    at = [2, 4, 6, 8, 10, 12]
    for k, (a, b) in enumerate(todo):
        while at and k == at[0]:
            at.pop(0)
            stages.pop(0)()
        a.wait()
        b.start()
    for st in stages:
        st()
    wait_all(v2)
    ntot = nsum[me.i]
    rtot = rsum[...]
    for k in range(1, dp):
        ntot = ntot + nall[k]
        rtot = rtot + rall[k]
    n_out[...] = ntot
    r_out[...] = rtot
    for lane in lanes:
        lane[4]()
    own.wait()
    wait_all(second)


def call_carry_home(dp, tn, g_rows, dwqkv, norms, rest):
    s = jax.ShapeDtypeStruct
    r, w = g_rows.shape[1:]
    depth, cols = dwqkv.shape[4], dwqkv.shape[5] // 3
    share = s((depth, cols), F32)
    outs = (s((tn * dp, r, w), BF), share, share, share, s(norms.shape[1:], F32), s(rest.shape[1:], F32))
    scratch = sems(2 * dp) + sems(2 * dp) + sems(3 * reduce_count(dp)) + [DMA((4,))]
    scratch += [pltpu.VMEM(norms.shape, F32), pltpu.VMEM(rest.shape[1:], F32),
                pltpu.VMEM((dp,) + norms.shape[1:], F32), pltpu.VMEM((dp,) + rest.shape[1:], F32),
                pltpu.VMEM(norms.shape, F32), pltpu.VMEM(rest.shape[1:], F32)]
    for _ in range(3):
        scratch += reduce_bufs(dp, tn, depth, cols)
    return pl.pallas_call(
        functools.partial(carry_home, dp, tn),
        out_shape=outs,
        in_specs=[ANY, ANY, VM, VM],
        out_specs=(ANY,) + (VM,) * 5,
        scratch_shapes=scratch,
        compiler_params=params(4, 48),
        name="carry_home",
    )(g_rows, dwqkv, norms, rest)


F32 = jnp.float32
BF = jnp.bfloat16
LAND = 64
ITERS = 6
HEADS_HERE = 6
ROWS_BQ, ROWS_BV, ROWS_BI, ROWS_TAPS = 0, 3, 6, 18
EDGE = 112
TAPS = 33
FLIP_AT = 367


def nn(a, b):
    return lax.dot_general(a, b, (((1,), (0,)), ((), ())), preferred_element_type=F32)


def nt(a, b):
    return lax.dot_general(a, b, (((1,), (1,)), ((), ())), preferred_element_type=F32)


def turn(a):
    return jnp.transpose(a, (1, 0))


def same_head(rows, columns):
    left = lax.broadcasted_iota(jnp.int32, (rows, columns), 0) // LAND
    right = lax.broadcasted_iota(jnp.int32, (rows, columns), 1) // LAND
    return left == right


def spread(small):
    n = small.shape[1] // LAND
    tall = jnp.concatenate([small] * n, axis=0)
    return jnp.where(same_head(n * LAND, n * LAND), tall, jnp.zeros_like(tall))


def gather_diag(full):
    n = full.shape[1] // LAND
    lane = lax.broadcasted_iota(jnp.int32, (LAND, full.shape[1]), 1) // LAND
    out = full[:LAND]
    for h in range(1, n):
        out = jnp.where(lane == h, full[h * LAND : (h + 1) * LAND], out)
    return out


def halves(a):
    high = a.astype(BF)
    return high, (a - high.astype(F32)).astype(BF)


def pair_nn(a, b):
    ah, al = halves(a)
    bh, bl = halves(b)
    bh, bl = spread(bh), spread(bl)
    wide = jnp.concatenate([bh, bl], axis=1)
    r = nn(jnp.concatenate([ah, al], axis=1), jnp.concatenate([wide, wide], axis=0))
    return r[:, : 2 * LAND] + r[:, 2 * LAND :]


def pair_nt(a, b):
    ah, al = halves(a)
    bh, bl = halves(b)
    bh, bl = spread(bh), spread(bl)
    tall = jnp.concatenate([bh, bl], axis=0)
    r = nt(jnp.concatenate([ah, al], axis=1), jnp.concatenate([tall, tall], axis=1))
    return r[:, : 2 * LAND] + r[:, 2 * LAND :]


def pair_turn(a):
    t = turn(a)
    return jnp.concatenate([t[:LAND], t[LAND:]], axis=1)


def pair_sum(a):
    left = lax.broadcasted_iota(jnp.int32, a.shape, 1) < LAND
    low = jnp.sum(jnp.where(left, a, 0.0), axis=1, keepdims=True)
    high = jnp.sum(jnp.where(left, 0.0, a), axis=1, keepdims=True)
    return jnp.where(left, low, high)


def pair_softmax(a):
    left = lax.broadcasted_iota(jnp.int32, a.shape, 1) < LAND
    low = jnp.max(jnp.where(left, a, -1e30), axis=1, keepdims=True)
    high = jnp.max(jnp.where(left, -1e30, a), axis=1, keepdims=True)
    e = jnp.exp(a - jnp.where(left, low, high))
    return e / pair_sum(e)


def pair_eye():
    r = lax.broadcasted_iota(jnp.int32, (LAND, 2 * LAND), 0)
    c = lax.broadcasted_iota(jnp.int32, (LAND, 2 * LAND), 1) % LAND
    return jnp.where(r == c, 1.0, 0.0).astype(F32)


def toeplitz(row, size, width):
    return pltpu.roll(jnp.broadcast_to(row, (size, width)), 0, 1, stride=1, stride_axis=0)


def blocks_of(ref, lower, block):
    length = ref.shape[1] - 256
    return jnp.concatenate(
        [ref[lower : lower + LAND, at : at + block + 256] for at in range(0, length, block)], axis=0
    )


def unblock(stacked, block):
    n = stacked.shape[0] // LAND
    return jnp.concatenate([stacked[i * LAND : (i + 1) * LAND] for i in range(n)], axis=1)


def own_sequence():
    return lax.axis_index("tensor") * lax.axis_size("dp") + lax.axis_index("dp")


def side_row(small_ref, t, first, count):
    return jnp.concatenate([small_ref[t, r : r + 1, :] for r in range(first, first + count)], axis=1)


def band_of(rows, head):
    h = head % HEADS_HERE
    row = jnp.concatenate([rows[head // HEADS_HERE][h : h + 1, :], jnp.zeros((1, 384), F32)], axis=1)
    return toeplitz(pltpu.roll(row, EDGE, 1), 256, 512).astype(BF)


def tap_rows(small_ref, t):
    return small_ref[t, ROWS_TAPS : ROWS_TAPS + 8, :]


def reversed_taps(rows):
    turned = jnp.where(
        lax.broadcasted_iota(jnp.int32, (128, 128), 0) + lax.broadcasted_iota(jnp.int32, (128, 128), 1) == TAPS - 1, 1.0, 0.0
    ).astype(BF)
    return nn(rows.astype(BF), turned)


def attend_forward(dp, x_ref, w_ref, small_ref, ids_ref, wi_ref, wf_ref,
                   q_ref, k_ref, v_ref, near_ref, far_ref, ctx_ref, lq_ref, lk_ref, mix_ref, sum_ref, ker_ref,
                   z_ref, a_ref, v2_ref, w2_ref, wi_all, wf_all, pad_ref, g_ss, g_rs, local):
    length, width = x_ref.shape
    tn = w_ref.shape[0]
    cols = width // tn
    scale = LAND ** -0.25
    rows_at = 256
    pairs = width // 128
    groups = width // 256
    me = Place(dp, tn)
    n = gather_count(dp)
    half = wi_ref.shape[1] // 2
    lanes = []
    for p, (src, dst) in enumerate(((wi_ref, wi_all), (wf_ref, wf_all))):
        for h in range(2):
            own, k = pl.ds(h * half, half), 2 * p + h
            lanes.append(gather_lane(me, src, own, dst, own, h == 1, Sub(g_ss, k * n), Sub(g_rs, k * n), local.at[k]))

    def stage(pair, s):
        def run():
            for lane in lanes[2 * pair : 2 * pair + 2]:
                lane[s]()
        return run

    greet(me, False)
    stage(0, 0)()
    stage(1, 0)()
    tick = Ticks([stage(0, 1), stage(0, 2), stage(1, 1), stage(0, 3), stage(1, 2), stage(1, 3), stage(0, 4), stage(1, 4)])
    bq = [side_row(small_ref, t, ROWS_BQ, 3) for t in range(tn)]
    bv = [side_row(small_ref, t, ROWS_BV, 3) for t in range(tn)]

    def project(i, carry):
        at = pl.ds(pl.multiple_of(i * rows_at, rows_at), rows_at)
        for t in range(tn):
            out = nn(x_ref[at, :], w_ref[t])
            own = slice(t * cols, (t + 1) * cols)
            q_ref[at, own] = ((out[:, :cols] + bq[t]) * scale).astype(BF)
            k_ref[at, own] = (out[:, cols : 2 * cols] * scale).astype(BF)
            v_ref[at, own] = (out[:, 2 * cols :] + bv[t]).astype(BF)
        return carry

    lax.fori_loop(0, length // rows_at, project, 0)

    ids = ids_ref[pl.ds(own_sequence(), 1), :]
    member = jnp.where(lax.broadcasted_iota(jnp.int32, (LAND, length), 0) == ids, 1.0, 0.0).astype(F32)
    count = jnp.sum(member, axis=1, keepdims=True)
    member = member.astype(BF)
    valid = ids < LAND
    lq_ref[...] = (nn(member, q_ref[...]) / count).astype(BF)
    lk_ref[...] = (nn(member, k_ref[...]) / count).astype(BF)

    eye = pair_eye()
    for p in range(pairs):
        own = slice(p * 128, (p + 1) * 128)
        scores = nt(lq_ref[:, own], spread(lk_ref[:, own]))
        kernel = pair_softmax(scores)
        ker_ref[:, own] = kernel
        left = lax.broadcasted_iota(jnp.int32, kernel.shape, 1) < LAND
        total = jnp.sum(pair_sum(kernel * kernel), axis=0, keepdims=True)
        z_ref[0, :, own] = pair_turn(kernel) / total

    for g in range(groups):
        own = slice(g * 256, (g + 1) * 256)
        scores = nt(spread(lk_ref[:, own]), q_ref[:, own]).reshape(4, LAND, length)
        scores = jnp.exp(scores - jnp.max(scores, axis=1, keepdims=True))
        scores = scores / jnp.sum(scores, axis=1, keepdims=True)
        near_ref[own, :] = scores.reshape(256, length).astype(BF)
        scores = nt(spread(lq_ref[:, own]), k_ref[:, own])
        scores = jnp.where(valid, scores, -1e30)
        scores = jnp.exp(scores - jnp.max(scores, axis=1, keepdims=True))
        scores = scores / jnp.sum(scores, axis=1, keepdims=True)
        far_ref[own, :] = scores.astype(BF)
        sum_ref[:, own] = gather_diag(nn(far_ref[own, :], v_ref[:, own]))
        if g == 1:
            tick()

    def iterate(n, carry):
        for p in range(pairs):
            own = slice(p * 128, (p + 1) * 128)
            z = z_ref[n, :, own]
            a = pair_nn(ker_ref[:, own], z)
            v2 = 15.0 * eye - pair_nn(a, 7.0 * eye - a)
            w2 = 13.0 * eye - pair_nn(a, v2)
            a_ref[n, :, own] = a
            v2_ref[n, :, own] = v2
            w2_ref[n, :, own] = w2
            z_ref[n + 1, :, own] = 0.25 * pair_nn(z, w2)
        return carry

    lax.fori_loop(0, ITERS // 2, iterate, 0)
    tick()
    lax.fori_loop(ITERS // 2, ITERS, iterate, 0)
    tick(2)

    for p in range(pairs):
        own = slice(p * 128, (p + 1) * 128)
        mix_ref[:, own] = pair_nn(z_ref[ITERS, :, own], sum_ref[:, own]).astype(BF)

    pad_ref[...] = jnp.zeros_like(pad_ref)
    taps = [tap_rows(small_ref, t) for t in range(tn)]
    for g in range(groups):
        own = slice(g * 256, (g + 1) * 256)
        att = nn(turn(spread(mix_ref[:, own])), near_ref[own, :])
        vt = turn(v_ref[:, own])
        pad_ref[:, 128 : 128 + length] = jnp.where(valid, vt, jnp.zeros_like(vt))
        parts = []
        for h in range(4):
            band = band_of(taps, 4 * g + h)
            parts.append(unblock(nt(blocks_of(pad_ref, h * LAND, 256), band), 256))
        att = (att + jnp.concatenate(parts, axis=0)).astype(BF)
        ctx_ref[:, own] = turn(att)
        if g == 0:
            tick()
    tick.rest()


def call_attend_forward(dp, x, w, small, ids, wi, wf):
    length, width = x.shape
    s = jax.ShapeDtypeStruct
    big = s((length, width), BF)
    tall = s((width, length), BF)
    low = s((LAND, width), BF)
    wide = s((LAND, width), F32)
    steps = s((ITERS, LAND, width), F32)
    tn = w.shape[0]
    depth, units = wi.shape
    whole = s((tn, dp // 4, 2, 2, depth, units), BF)
    outs = (big, big, big, tall, tall, big, low, low, low, wide, wide, s((ITERS + 1, LAND, width), F32), steps, steps, steps,
            whole, whole)
    return pl.pallas_call(
        functools.partial(attend_forward, dp),
        out_shape=outs,
        in_specs=[VM] * 4 + [ANY] * 2,
        out_specs=tuple([VM] * 15 + [ANY] * 2),
        scratch_shapes=[pltpu.VMEM((256, length + 256), BF)] + sems(4 * gather_count(dp)) + [DMA((4,))],
        compiler_params=params(1, 56),
        name="attend_forward",
    )(x, w, small, ids, wi, wf)


ROOT_HALF = 0.7071067811865476
P_ERF = 0.3275911
C_ERF = (0.254829592, -0.284496736, 1.421413741, -1.453152027, 1.061405429)


def gelu_both(u):
    x = jnp.abs(u) * ROOT_HALF
    e = jnp.exp(-0.5 * u * u)
    t = 1.0 / (1.0 + P_ERF * x)
    poly = C_ERF[4]
    for c in (C_ERF[3], C_ERF[2], C_ERF[1], C_ERF[0]):
        poly = poly * t + c
    tail = 0.5 * poly * t * e
    phi = jnp.where(u < 0.0, tail, 1.0 - tail)
    return u * phi, phi + u * e * 0.3989422804014327


def norm_parts(r):
    n = r.shape[1]
    center = r - jnp.sum(r, axis=1, keepdims=True) * (1.0 / n)
    spread_ = jnp.sum(center * center, axis=1, keepdims=True) * (1.0 / n)
    rstd = lax.rsqrt(spread_ + 1e-05)
    return center * rstd, rstd


def norm_back(e, normed, rstd):
    n = e.shape[1]
    mean_e = jnp.sum(e, axis=1, keepdims=True) * (1.0 / n)
    mean_en = jnp.sum(e * normed, axis=1, keepdims=True) * (1.0 / n)
    return rstd * (e - mean_e - normed * mean_en)


def fold(a):
    return jnp.sum(a.reshape(a.shape[0] // 8, 8, a.shape[1]), axis=0)


def feed(dp, x_ref, ctx_ref, wo_ref, wi_ref, wf_ref, bo_in, g1_in, s1_in, bf_in, g2_in, s2_in, small_ref, cot_ref,
         gr1_ref, dc_ref, dwo_ref, dwi_ref, dwf_ref, vec_ref, bsum_ref, half_ref,
         act_ref, gi_ref, hid_ref, gr2_ref, turn_ref, n1_ref, n2_ref, rs1_ref, rs2_ref, out_ref, cots_ref,
         c_ss, c_rs, h_ss, h_rs, local):
    length, width = x_ref.shape
    tn = wo_ref.shape[0]
    cols = width // tn
    units = wi_ref.shape[2]
    size = 256
    chunk = 512
    part = length // dp
    per = size // part
    me = Place(dp, tn)
    greet(me)
    arriving = to_owner(me, cot_ref, cots_ref, c_ss, c_rs, local.at[0])
    leaving = to_home(me, out_ref, half_ref, h_ss, h_rs, local.at[1])
    start_all(arriving)
    bo, g1, s1, bf, g2, s2 = [r[...].astype(F32) for r in (bo_in, g1_in, s1_in, bf_in, g2_in, s2_in)]
    bi = [side_row(small_ref, t, ROWS_BI, units // 128) for t in range(tn)]
    vec_ref[...] = jnp.zeros_like(vec_ref)
    bsum_ref[...] = jnp.zeros_like(bsum_ref)

    def rows_at(i):
        return pl.ds(pl.multiple_of(i * size, size), size)

    def forward(i, carry):
        at = rows_at(i)
        attn = bo + x_ref[at, :].astype(F32)
        for t in range(tn):
            attn = attn + nt(ctx_ref[at, t * cols : (t + 1) * cols], wo_ref[t])
        n1, rstd1 = norm_parts(attn)
        n1_ref[at, :] = n1
        rs1_ref[at, :] = rstd1
        hidden = n1 * g1 + s1
        hid = hidden.astype(BF)
        hid_ref[at, :] = hid
        r2 = hidden + bf
        for t in range(tn):
            for c in range(0, units, chunk):
                own = slice(t * units + c, t * units + c + chunk)
                act, gp = gelu_both(nn(hid, wi_ref[t, :, c : c + chunk]) + bi[t][:, c : c + chunk])
                act_ref[at, own] = act.astype(BF)
                gi_ref[at, own] = gp.astype(BF)
        for t in range(tn):
            r2 = r2 + nt(act_ref[at, t * units : (t + 1) * units], wf_ref[t])
        n2, rstd2 = norm_parts(r2)
        n2_ref[at, :] = n2
        rs2_ref[at, :] = rstd2
        out_ref[pl.ds(i * per, per)] = (n2 * g2 + s2).reshape(per, part, width).astype(BF)
        return carry

    def backward(i, carry):
        at = rows_at(i)
        cot = cots_ref[pl.ds(i * per, per)].astype(F32).reshape(size, width)
        n2 = n2_ref[at, :]
        gr2 = norm_back(cot * g2, n2, rs2_ref[at, :])
        vec_ref[5] += fold(cot)
        vec_ref[4] += fold(cot * n2)
        vec_ref[3] += fold(gr2)
        low = gr2.astype(BF)
        gr2_ref[at, :] = low
        for t in range(tn):
            for c in range(0, units, chunk):
                own = slice(t * units + c, t * units + c + chunk)
                gi = nn(low, wf_ref[t, :, c : c + chunk]) * gi_ref[at, own].astype(F32)
                bsum_ref[:, own] += fold(gi)
                gi_ref[at, own] = gi.astype(BF)
        gh = gr2
        for t in range(tn):
            gh = gh + nt(gi_ref[at, t * units : (t + 1) * units], wi_ref[t])
        n1 = n1_ref[at, :]
        gr1 = norm_back(gh * g1, n1, rs1_ref[at, :])
        vec_ref[2] += fold(gh)
        vec_ref[1] += fold(gh * n1)
        vec_ref[0] += fold(gr1)
        low1 = gr1.astype(BF)
        gr1_ref[at, :] = low1
        for t in range(tn):
            dc_ref[at, t * cols : (t + 1) * cols] = nn(low1, wo_ref[t]).astype(BF)
        return carry

    lax.fori_loop(0, length // size, forward, 0)
    start_all(leaving)
    wait_all(arriving)
    lax.fori_loop(0, length // size, backward, 0)

    turn_ref[...] = turn(gr2_ref[...])
    for t in range(tn):
        for c in range(0, units, chunk):
            own = slice(t * units + c, t * units + c + chunk)
            dwf_ref[t, :, c : c + chunk] = nn(turn_ref[...], act_ref[:, own]).astype(BF)
    turn_ref[...] = turn(hid_ref[...])
    for t in range(tn):
        for c in range(0, units, chunk):
            own = slice(t * units + c, t * units + c + chunk)
            dwi_ref[t, :, c : c + chunk] = nn(turn_ref[...], gi_ref[:, own]).astype(BF)
    turn_ref[...] = turn(gr1_ref[...])
    for t in range(tn):
        dwo_ref[t] = nn(turn_ref[...], ctx_ref[:, t * cols : (t + 1) * cols]).astype(BF)
    wait_all(leaving)


def call_feed(dp, x, ctx, wo, wi, wf, vectors, small, cot):
    length, width = x.shape
    tn, _, cols = wo.shape
    units = wi.shape[2]
    s = jax.ShapeDtypeStruct
    big = s((length, width), BF)
    blocks = (dp,) + cot.shape[1:]
    outs = (big, big, s((tn, width, cols), BF), s((tn, width, units), BF), s((tn, width, units), BF),
            s((6, 8, width), F32), s((8, tn * units), F32), s(blocks, BF))
    vm = pltpu.VMEM
    return pl.pallas_call(
        functools.partial(feed, dp),
        out_shape=outs,
        in_specs=[VM] * 12 + [ANY],
        out_specs=tuple([VM] * 7 + [ANY]),
        scratch_shapes=[vm((length, tn * units), BF), vm((length, tn * units), BF), vm((length, width), BF),
                        vm((length, width), BF), vm((width, length), BF), vm((length, width), F32),
                        vm((length, width), F32), vm((length, 1), F32), vm((length, 1), F32), vm(blocks, BF),
                        vm(blocks, BF)] + sems(dp) + sems(dp) + [DMA((2,))],
        compiler_params=params(2, 62),
        name="feed_forward",
    )(x, ctx, wo, wi, wf, *vectors, small, cot)


def attend_backward(dp, x_ref, w_ref, ids_ref, small_ref, q_ref, k_ref, v_ref, near_ref, far_ref, lq_ref, lk_ref, mix_ref,
                    sum_ref, ker_ref, z_ref, a_ref, v2_ref, w2_ref, dc_ref, gr1_ref, dwo_in, dwi_in, dwf_in, half_ref,
                    gtok_ref, dw_ref, vecq_ref, vecv_ref, gtap_ref, go_ref, gi_ref, gf_ref, home_ref,
                    pre_ref, glq_ref, glk_ref, gsum_ref, gz_ref, gk_ref, padv_ref, padc_ref, xt_ref,
                    g_ss, g_rs, y_ss, y_rs, local, *bufs):
    length, width = x_ref.shape
    tn = w_ref.shape[0]
    cols = width // tn
    scale = LAND ** -0.25
    size = length // dp
    pairs = width // 128
    groups = width // 256
    me = Place(dp, tn)
    n = reduce_count(dp)
    half = dwi_in.shape[5] // 2
    plan = [(dwf_in, 0, half, gf_ref), (dwf_in, half, half, gf_ref), (dwi_in, 0, half, gi_ref), (dwi_in, half, half, gi_ref),
            (dwo_in, 0, cols, go_ref)]
    lanes = []
    for k, (src, lo, w, dst) in enumerate(plan):
        lanes.append(reduce_lane(me, src, lo, w, bufs[5 * k : 5 * k + 5], Sub(g_ss, k * n), Sub(g_rs, k * n), local.at[k],
                                 [(dst, lo, 0, w)]))
    quarter = dp // 4
    sides = []
    for k in range(4):
        here, there = pl.ds(k * quarter, quarter), pl.ds(me.t * dp + k * quarter, quarter)
        sides.append(remote(half_ref.at[here], home_ref.at[there], y_ss.at[k], y_rs.at[k], (me.i, 1 - me.t)))
    kept = pltpu.make_async_copy(half_ref, home_ref.at[pl.ds(me.t * dp, dp)], local.at[5])
    greet(me, False)
    for lane in lanes:
        lane[0]()
    kept.start()
    sides[0].start()
    sides[1].start()
    tick = Ticks([lanes[0][1], lanes[1][1], lanes[2][1], lanes[3][1], lanes[4][1], lanes[0][2], lanes[1][2], sides[2].start,
                  lanes[0][3], lanes[2][2], lanes[1][3], lanes[3][2], sides[3].start, lanes[4][2], lanes[2][3], lanes[3][3],
                  lanes[4][3]])
    ids = ids_ref[pl.ds(own_sequence(), 1), :]
    member = jnp.where(lax.broadcasted_iota(jnp.int32, (LAND, length), 0) == ids, 1.0, 0.0).astype(F32)
    count = jnp.sum(member, axis=1, keepdims=True)
    member = member.astype(BF)
    valid = ids < LAND
    eye = pair_eye()

    for g in range(groups):
        own = slice(g * 256, (g + 1) * 256)
        gsum_ref[:, own] = gather_diag(nn(near_ref[own, :], dc_ref[:, own]))
    for p in range(pairs):
        own = slice(p * 128, (p + 1) * 128)
        gmix = gsum_ref[:, own]
        gz_ref[:, own] = pair_nt(gmix, sum_ref[:, own])
        gsum_ref[:, own] = pair_nn(pair_turn(z_ref[ITERS, :, own]), gmix)

    tick(5)
    gk_ref[...] = jnp.zeros_like(gk_ref)

    def iterate(m, carry):
        n = ITERS - 1 - m
        for p in range(pairs):
            own = slice(p * 128, (p + 1) * 128)
            grad = 0.25 * gz_ref[:, own]
            kernel = ker_ref[:, own]
            z = z_ref[n, :, own]
            a = a_ref[n, :, own]
            v2 = v2_ref[n, :, own]
            w2 = w2_ref[n, :, own]
            dw2 = pair_nn(pair_turn(z), grad)
            at = pair_turn(a)
            dv2 = -pair_nn(at, dw2)
            da = -pair_nt(dw2, v2) - pair_nt(dv2, 7.0 * eye - a) + pair_nn(at, dv2)
            gk_ref[:, own] += pair_nt(da, z)
            gz_ref[:, own] = pair_nt(grad, w2) + pair_nn(pair_turn(kernel), da)
        return carry

    lax.fori_loop(0, ITERS // 2, iterate, 0)
    tick(1)
    lax.fori_loop(ITERS // 2, ITERS, iterate, 0)
    tick(2)

    for p in range(pairs):
        own = slice(p * 128, (p + 1) * 128)
        kernel = ker_ref[:, own]
        gz = gz_ref[:, own]
        total = jnp.sum(pair_sum(kernel * kernel), axis=0, keepdims=True)
        kt = pair_turn(kernel)
        back = jnp.sum(pair_sum(gz * kt), axis=0, keepdims=True)
        gk = gk_ref[:, own] + pair_turn(gz) / total - kernel * (2.0 * back / (total * total))
        mid = kernel * (gk - pair_sum(kernel * gk))
        glq_ref[:, own] = pair_nn(mid, lk_ref[:, own].astype(F32))
        glk_ref[:, own] = pair_nn(pair_turn(mid), lq_ref[:, own].astype(F32))

    flip = jnp.where(
        lax.broadcasted_iota(jnp.int32, (256, 256), 0) + lax.broadcasted_iota(jnp.int32, (256, 256), 1) == 255, 1.0, 0.0
    ).astype(BF)
    taps = [reversed_taps(tap_rows(small_ref, t)) for t in range(tn)]
    padv_ref[...] = jnp.zeros_like(padv_ref)
    padc_ref[...] = jnp.zeros_like(padc_ref)
    inner = slice(128, 128 + length)
    for g in range(groups):
        own = slice(g * 256, (g + 1) * 256)
        lk4 = spread(lk_ref[:, own])
        lq4 = spread(lq_ref[:, own])
        near = near_ref[own, :].astype(F32)
        gnear = nt(spread(mix_ref[:, own]), dc_ref[:, own])
        drop = jnp.sum((near * gnear).reshape(4, LAND, length), axis=1, keepdims=True)
        first = (near * (gnear.reshape(4, LAND, length) - drop).reshape(256, length)).astype(BF)
        glk_ref[:, own] += gather_diag(nn(first, q_ref[:, own]))
        gsum4 = spread(gsum_ref[:, own].astype(BF))
        far = far_ref[own, :].astype(F32)
        gfar = nt(gsum4, v_ref[:, own])
        drop = jnp.sum(far * gfar, axis=1, keepdims=True)
        third = (far * (gfar - drop)).astype(BF)
        glq_ref[:, own] += gather_diag(nn(third, k_ref[:, own]))
        glq = turn((glq_ref[:, own] / count).astype(BF))
        glk = turn((glk_ref[:, own] / count).astype(BF))
        dq = (nn(turn(lk4), first) + nn(glq, member)) * scale
        dk = (nn(turn(lq4), third) + nn(glk, member)) * scale
        dv = nn(turn(gsum4), far_ref[own, :])

        vt = turn(v_ref[:, own])
        padv_ref[:, inner] = jnp.where(valid, vt, jnp.zeros_like(vt))
        padc_ref[:, inner] = turn(dc_ref[:, own])
        parts = []
        for h in range(4):
            band = band_of(taps, 4 * g + h)
            parts.append(unblock(nt(blocks_of(padc_ref, h * LAND, 256), band), 256))
            plain = jnp.concatenate(
                [padc_ref[h * LAND : (h + 1) * LAND, 128 + at : 128 + at + 256] for at in range(0, length, 256)], axis=0
            )
            gram = nn(nt(flip, plain).astype(BF), blocks_of(padv_ref, h * LAND, 256))
            gram = pltpu.roll(gram, 0, 1, stride=1, stride_axis=0)
            gtap_ref[4 * g + h : 4 * g + h + 1, :] = jnp.sum(gram, axis=0, keepdims=True)
        dv = dv + jnp.where(valid, jnp.concatenate(parts, axis=0), 0.0)
        vecq_ref[own, :] = jnp.sum(dq, axis=1, keepdims=True)
        vecv_ref[own, :] = jnp.sum(dv, axis=1, keepdims=True)
        for lower in range(0, 256, 128):
            c = g * 256 + lower
            t, r = c // cols, c % cols
            pre_ref[t, r : r + 128, :] = dq[lower : lower + 128].astype(BF)
            pre_ref[t, cols + r : cols + r + 128, :] = dk[lower : lower + 128].astype(BF)
            pre_ref[t, 2 * cols + r : 2 * cols + r + 128, :] = dv[lower : lower + 128].astype(BF)
        tick(2)

    xt_ref[...] = turn(x_ref[...])
    tick(2)
    for t in range(tn):
        dw_ref[t] = nt(xt_ref[...], pre_ref[t]).astype(BF)
    tick(2)
    for at in range(0, length, 256):
        part = nn(w_ref[0], pre_ref[0, :, at : at + 256])
        for t in range(1, tn):
            part = part + nn(w_ref[t], pre_ref[t, :, at : at + 256])
        gtok_ref[at // size : (at + 256) // size] = (
            (gr1_ref[at : at + 256, :].astype(F32) + turn(part)).reshape(256 // size, size, width).astype(BF)
        )
    tick.rest()
    for lane in lanes:
        lane[4]()
    wait_all(sides)
    kept.wait()


def call_attend_backward(dp, x, w, ids, small, saved, dc, gr1, dwo, dwi, dwf, half):
    length, width = x.shape
    tn = w.shape[0]
    cols = width // tn
    s = jax.ShapeDtypeStruct
    depth, units = dwi.shape[4:]
    outs = (s(half.shape, BF), s((tn, width, 3 * cols), BF), s((width, 1), F32), s((width, 1), F32),
            s((width // LAND, 512), F32), s((depth, cols), F32), s((depth, units), F32), s((depth, units), F32),
            s((tn * dp,) + half.shape[1:], BF))
    args = (x, w, ids, small, *saved, dc, gr1, dwo, dwi, dwf, half)
    vm = pltpu.VMEM
    little = vm((LAND, width), F32)
    n = 5 * reduce_count(dp)
    scratch = [vm((tn, 3 * cols, length), BF)] + [little] * 5
    scratch += [vm((256, length + 256), BF), vm((256, length + 256), BF), vm((width, length), BF)]
    scratch += sems(n) + sems(4) + [DMA((6,))]
    for wide in (units // 2,) * 4 + (cols,):
        scratch += reduce_bufs(dp, tn, depth, wide)
    return pl.pallas_call(
        functools.partial(attend_backward, dp),
        out_shape=outs,
        in_specs=[VM] * (len(args) - 4) + [ANY] * 4,
        out_specs=tuple([VM] * 8 + [ANY]),
        scratch_shapes=scratch,
        compiler_params=params(3, 62),
        name="attend_backward",
    )(*args)


def local(tokens, cotangent, landmark_ids, w_query, w_key, w_value, b_query, b_value, conv_taps, w_out, b_out,
          first_gain, first_shift, w_inner, b_inner, w_outer, b_outer, second_gain, second_shift):
    dp = lax.axis_size("dp")
    tn = lax.axis_size("tensor")
    part, width = tokens.shape[1:]
    length = dp * part
    cols = w_query.shape[1]
    units = w_inner.shape[1]
    heads, taps = conv_taps.shape
    row = lambda v: v.reshape(1, -1)
    vectors = [row(v) for v in (b_out, first_gain, first_shift, b_outer, second_gain, second_shift)]

    def join(w):
        return w.reshape(tn, width, w.shape[-1])

    def cut(g):
        return g.reshape(tn, dp // 4, 2, 2, width // dp, g.shape[2])

    rows, wqkv, wout, small = call_bring(
        dp, tn, tokens, w_query, w_key, w_value, w_out, row(b_query), row(b_value), row(b_inner), conv_taps
    )
    rows = rows.reshape(length, width)
    wqkv, wout = join(wqkv), join(wout)
    q, k, v, near, far, ctx, *rest_saved, wi, wf = call_attend_forward(
        dp, rows, wqkv, small, landmark_ids, w_inner, w_outer
    )
    gr1, dc, dwo, dwi, dwf, vec, bsum, half = call_feed(
        dp, rows, ctx, wout, join(wi), join(wf), vectors, small, cotangent
    )
    grad_rows, dwqkv, gbq, gbv, gtap, go, gi, gf, out_home = call_attend_backward(
        dp, rows, wqkv, landmark_ids, small, (q, k, v, near, far, *rest_saved), dc, gr1, cut(dwo), cut(dwi), cut(dwf), half
    )
    share = width // dp
    norms = jnp.sum(vec, axis=1).reshape(6, dp, share).transpose(1, 0, 2).reshape(dp, 6 * share)
    norms = jnp.pad(norms, ((0, 0), (0, 1024 - 6 * share))).reshape(dp, 8, 128)
    rest = jnp.concatenate(
        [gbq.reshape(tn, cols), gbv.reshape(tn, cols), jnp.sum(bsum, axis=0).reshape(tn, units),
         gtap[:, FLIP_AT : FLIP_AT + taps].reshape(tn, heads * taps)], axis=1)
    rest = jnp.pad(rest, ((0, 0), (0, 24 * 128 - rest.shape[1]))).reshape(tn, 24, 128)
    grad_home, gq, gk, gv, nsum, rsum = call_carry_home(dp, tn, grad_rows, cut(dwqkv), norms, rest)
    n = nsum.reshape(-1)[: 6 * share].reshape(6, share)
    r = rsum.reshape(-1)
    at = 2 * cols + units
    return (out_home, grad_home, gq, gk, gv, r[:cols], r[cols : 2 * cols],
            r[at : at + heads * taps].reshape(heads, taps), go, n[0], n[1], n[2], gi, r[2 * cols : at], gf,
            n[3], n[4], n[5])


def solution(mesh):
    return jax.shard_map(
        local,
        mesh=mesh,
        in_specs=(
            P(None, "dp", None),
            P(None, "dp", None),
            P(),
            P("dp", "tensor"),
            P("dp", "tensor"),
            P("dp", "tensor"),
            P("tensor"),
            P("tensor"),
            P("tensor", None),
            P("dp", "tensor"),
            P(),
            P(),
            P(),
            P("dp", "tensor"),
            P("tensor"),
            P("dp", "tensor"),
            P(),
            P(),
            P(),
        ),
        out_specs=(
            P(None, "dp", None),
            P(None, "dp", None),
            P("dp", "tensor"),
            P("dp", "tensor"),
            P("dp", "tensor"),
            P("tensor"),
            P("tensor"),
            P("tensor", None),
            P("dp", "tensor"),
            P("dp"),
            P("dp"),
            P("dp"),
            P("dp", "tensor"),
            P("tensor"),
            P("dp", "tensor"),
            P("dp"),
            P("dp"),
            P("dp"),
        ),
        check_vma=False,
    )
```

```python
import functools

import jax
import jax.numpy as jnp
from jax import lax
from jax.experimental import pallas as pl
from jax.experimental.pallas import tpu as pltpu
from jax.sharding import PartitionSpec as P

F32 = jnp.float32
BF = jnp.bfloat16
MESH = pl.DeviceIdType.MESH
ANY = pl.BlockSpec(memory_space=pl.ANY)
TOP = 62
VM = pl.BlockSpec(memory_space=pltpu.VMEM)
DMA = pltpu.SemaphoreType.DMA
SMALL_ROWS = 32


class Place:
    def __init__(self, dp, tn):
        self.dp, self.tn = dp, tn
        self.nz = dp // 4
        i = lax.axis_index("dp")
        self.i = i
        self.t = lax.axis_index("tensor")
        self.c = lax.rem(i, 2)
        self.x = lax.rem(i // 2, 2)
        self.z = i // 4

    def at(self, z=None, x=None, c=None, t=None):
        z = self.z if z is None else z
        x = self.x if x is None else x
        c = self.c if c is None else c
        t = self.t if t is None else t
        return (z * 4 + x * 2 + c, t)


def greet(me, rows=True):
    bar = pltpu.get_barrier_semaphore()
    if rows:
        peers = [(lax.rem(me.i + k, me.dp), me.t) for k in range(1, me.dp)]
    else:
        peers = [me.at(z=lax.rem(me.z + k, me.nz)) for k in range(1, me.nz)] + [me.at(x=1 - me.x), me.at(c=1 - me.c)]
    peers.append((me.i, 1 - me.t))
    for p in peers:
        pl.semaphore_signal(bar, 1, device_id=p, device_id_type=MESH)
    pl.semaphore_wait(bar, len(peers))


def remote(src, dst, ss, rs, to):
    return pltpu.make_async_remote_copy(
        src_ref=src, dst_ref=dst, send_sem=ss, recv_sem=rs, device_id=to, device_id_type=MESH
    )


def start_all(copies):
    for c in copies:
        c.start()


def wait_all(copies):
    for c in copies:
        c.wait()


def to_owner(me, src, out, ss, rs, local):
    copies = []
    for k in range(1, me.dp):
        j = lax.rem(me.i + k, me.dp)
        copies.append(remote(src.at[me.t * me.dp + j], out.at[me.i], ss.at[k], rs.at[k], (j, me.t)))
    copies.append(pltpu.make_async_copy(src.at[me.t * me.dp + me.i], out.at[me.i], local))
    return copies


def to_home(me, src, out, ss, rs, local):
    copies = []
    for k in range(1, me.dp):
        j = lax.rem(me.i + k, me.dp)
        copies.append(remote(src.at[j], out.at[me.i], ss.at[k], rs.at[k], (j, me.t)))
    copies.append(pltpu.make_async_copy(src.at[me.i], out.at[me.i], local))
    return copies


def gather_lane(me, src, own, out, cols, north_first, ss, rs, local):
    t, z, x, c, n = me.t, me.z, me.x, me.c, me.nz
    px, py, sib = me.at(x=1 - x), me.at(t=1 - t), me.at(c=1 - c)

    def move(ref, k, to):
        return remote(ref, ref, ss.at[k], rs.at[k], to)

    zs = [pltpu.make_async_copy(src.at[:, own], out.at[t, z, x, c, :, cols], local)]
    for k in range(1, n):
        to = me.at(z=lax.rem(z + k, n))
        zs.append(remote(src.at[:, own], out.at[t, z, x, c, :, cols], ss.at[k], rs.at[k], to))
    if north_first:
        first, second = move(out.at[t, :, x, c, :, cols], n, py), move(out.at[:, :, x, c, :, cols], n + 1, px)
        d2, d3 = move(out.at[:, :, x, c, :, cols], n + 2, sib), move(out.at[:, :, 1 - x, c, :, cols], n + 3, sib)
    else:
        first, second = move(out.at[t, :, x, c, :, cols], n, px), move(out.at[t, :, :, c, :, cols], n + 1, py)
        d2, d3 = move(out.at[t, :, :, c, :, cols], n + 2, sib), move(out.at[1 - t, :, :, c, :, cols], n + 3, sib)

    def s0():
        start_all(zs)

    def s1():
        wait_all(zs)
        first.start()

    def s2():
        first.wait()
        second.start()
        d2.start()

    def s3():
        second.wait()
        d3.start()

    def s4():
        d2.wait()
        d3.wait()

    return [s0, s1, s2, s3, s4]


def gather_count(dp):
    return dp // 4 + 4


def add_low(a, b):
    return (a.astype(F32) + b.astype(F32)).astype(BF)


def reduce_lane(me, src, lo, w, bufs, ss, rs, local, puts, north_first=False):
    t, z, x, c, n = me.t, me.z, me.x, me.c, me.nz
    mine, rc, r1, r2, rz = bufs
    cols = pl.ds(lo, w)

    def move(a, b, q, to):
        return remote(a, b, ss.at[q], rs.at[q], to)

    keep = pltpu.make_async_copy(src.at[:, :, :, c, :, cols], mine, local)
    core = move(src.at[:, :, :, 1 - c, :, cols], rc, 0, me.at(c=1 - c))
    px, py = me.at(x=1 - x), me.at(t=1 - t)
    if north_first:
        first = move(rc.at[1 - t], r1, 1, py)
        second = move(r1.at[:, 1 - x], r2, 2, px)
    else:
        first = move(rc.at[:, :, 1 - x], r1, 1, px)
        second = move(r1.at[1 - t], r2, 2, py)
    lines = []
    for q in range(1, n):
        to = lax.rem(z + q, n)
        lines.append(move(r2.at[to], rz.at[q], 2 + q, me.at(z=to)))

    def s0():
        keep.start()
        core.start()

    def s1():
        keep.wait()
        core.wait()
        rc[...] = add_low(rc[...], mine[...])
        first.start()

    def s2():
        first.wait()
        r1[...] = add_low(r1[...], rc[t] if north_first else rc[:, :, x])
        second.start()

    def s3():
        second.wait()
        r2[...] = add_low(r2[...], r1[:, x] if north_first else r1[t])
        start_all(lines)

    def s4():
        total = r2[z].astype(F32)
        wait_all(lines)
        for q in range(1, n):
            total = total + rz[q].astype(F32)
        for dst, at, first_col, width in puts:
            dst[:, at : at + width] = total[:, first_col : first_col + width]

    return [s0, s1, s2, s3, s4]


def reduce_bufs(dp, tn, depth, w, north_first=False):
    nz = dp // 4
    one = (nz, 2) if north_first else (tn, nz)
    return [pltpu.VMEM((tn, nz, 2, depth, w), BF), pltpu.VMEM((tn, nz, 2, depth, w), BF),
            pltpu.VMEM(one + (depth, w), BF), pltpu.VMEM((nz, depth, w), BF), pltpu.VMEM((nz, depth, w), BF)]


def reduce_count(dp):
    return dp // 4 + 2


class Fetch:
    def __init__(self, src, dst, sem):
        self.copy, self.open = pltpu.make_async_copy(src, dst, sem), True

    def start(self):
        self.copy.start()
        return self

    def wait(self):
        if self.open:
            self.copy.wait()
        self.open = False


class Sub:
    def __init__(self, ref, base):
        self.ref, self.base = ref, base

    @property
    def at(self):
        return self

    def __getitem__(self, k):
        return self.ref.at[self.base + k]


class Ticks:
    def __init__(self, stages):
        self.stages = list(stages)

    def __call__(self, count=1):
        for _ in range(min(count, len(self.stages))):
            self.stages.pop(0)()

    def rest(self):
        self(len(self.stages))


def sems(n):
    return [DMA((n,)), DMA((n,))]


def params(cid, mib):
    return pltpu.CompilerParams(collective_id=cid, has_side_effects=True, vmem_limit_bytes=mib * 2**20)


def bring(dp, tn, tok, wq, wk, wv, wo, bq, bv, bi, taps, rows, wqkv, wout, small,
          r_ss, r_rs, g_ss, g_rs, local, piece):
    me = Place(dp, tn)
    cols = wq.shape[1]
    n = gather_count(dp)
    lanes = []
    for k, (src, dst, lo) in enumerate(((wq, wqkv, 0), (wk, wqkv, cols), (wv, wqkv, 2 * cols), (wo, wout, 0))):
        lanes.append(gather_lane(me, src, pl.ds(0, cols), dst, pl.ds(lo, cols), k % 2 == 1,
                                 Sub(g_ss, k * n), Sub(g_rs, k * n), local.at[k]))
    piece[...] = jnp.zeros_like(piece)
    for ref, first in ((bq, ROWS_BQ), (bv, ROWS_BV), (bi, ROWS_BI)):
        line = ref[...].astype(F32).reshape(1, ref.shape[0])
        for r in range(ref.shape[0] // 128):
            piece[first + r : first + r + 1, :] = line[:, r * 128 : (r + 1) * 128]
    heads, width = taps.shape
    tap = taps[...].astype(F32)
    piece[ROWS_TAPS : ROWS_TAPS + heads, :width] = tap
    greet(me)
    for s in (0, 1):
        for lane in lanes[2 * s : 2 * s + 2]:
            lane[0]()
    moved = to_owner(me, tok, rows, r_ss, r_rs, local.at[4])
    start_all(moved)
    side = [remote(piece, small.at[me.t], r_ss.at[0], r_rs.at[0], (me.i, 1 - me.t)),
            pltpu.make_async_copy(piece, small.at[me.t], local.at[5])]
    start_all(side)
    for pair, stage in ((0, 1), (0, 2), (1, 1), (0, 3), (1, 2), (1, 3), (0, 4), (1, 4)):
        for lane in lanes[2 * pair : 2 * pair + 2]:
            lane[stage]()
    wait_all(side)
    wait_all(moved)


def call_bring(dp, tn, tok, wq, wk, wv, wo, bq, bv, bi, taps):
    s = jax.ShapeDtypeStruct
    depth, cols = wq.shape
    lead = (tn, dp // 4, 2, 2, depth)
    outs = (s((dp,) + tok.shape[1:], BF), s(lead + (3 * cols,), BF), s(lead + (cols,), BF), s((tn, SMALL_ROWS, 128), F32))
    return pl.pallas_call(
        functools.partial(bring, dp, tn),
        out_shape=outs,
        in_specs=[ANY] * 5 + [VM] * 4,
        out_specs=(ANY, ANY, ANY, ANY),
        scratch_shapes=sems(dp) + sems(4 * gather_count(dp)) + [DMA((6,)), pltpu.VMEM((SMALL_ROWS, 128), F32)],
        compiler_params=params(0, TOP),
        name="bring",
    )(tok, wq, wk, wv, wo, bq, bv, bi, taps)


def carry_home(dp, tn, g_rows, dwqkv, vec, bsum, vecs, gtap, g_home, gq, gk, gv, gbq, gbv, gtaps, gbi, *refs):
    n_outs, (r_ss, r_rs, v_ss, v_rs, g_ss, g_rs, local, norms, rest, nbuf, rbuf, nall, rall, nsum, rsum) = refs[:6], refs[6:21]
    bufs = refs[21:]
    me = Place(dp, tn)
    cols = gq.shape[1]
    n = reduce_count(dp)
    lanes = []
    for k, dst in enumerate((gq, gk, gv)):
        lanes.append(reduce_lane(me, dwqkv, k * cols, cols, bufs[5 * k : 5 * k + 5], Sub(g_ss, k * n), Sub(g_rs, k * n),
                                 local.at[1 + k], [(dst, 0, 0, cols)]))
    greet(me)
    mine = me.t * dp
    first = []
    for k in range(1, dp):
        j = lax.rem(me.i + k, dp)
        first.append(remote(g_rows.at[j], g_home.at[mine + me.i], r_ss.at[k], r_rs.at[k], (j, me.t)))
    own = pltpu.make_async_copy(g_rows.at[me.i], g_home.at[mine + me.i], local.at[0])
    partner = (me.i, 1 - me.t)
    second = [remote(g_rows.at[me.i], g_home.at[mine + me.i], r_ss.at[dp], r_rs.at[dp], partner)]
    for k in range(1, dp):
        j = mine + lax.rem(me.i + dp - k, dp)
        second.append(remote(g_home.at[j], g_home.at[j], r_ss.at[dp + k], r_rs.at[dp + k], partner))
    v1 = [remote(norms, nbuf, v_ss.at[0], v_rs.at[0], partner),
          remote(rest.at[1 - me.t], rbuf, v_ss.at[1], v_rs.at[1], partner)]
    for lane in lanes:
        lane[0]()
    start_all(first)
    own.start()
    second[0].start()
    share = n_outs[0].shape[0]
    six = jnp.sum(vec[...], axis=1)
    norms[...] = jnp.zeros_like(norms)
    rest[...] = jnp.zeros_like(rest)
    for j in range(dp):
        norms[j, 0:6, :share] = six[:, j * share : (j + 1) * share]
    units = jnp.sum(bsum[...], axis=0, keepdims=True)
    per, taps = gtaps.shape
    for t in range(tn):
        for line, first_row, size in ((vecs[0:1, :], ROWS_BQ, cols), (vecs[1:2, :], ROWS_BV, cols),
                                      (units, ROWS_BI, gbi.shape[0])):
            for r in range(size // 128):
                lo = t * size + r * 128
                rest[t, first_row + r : first_row + r + 1, :] = line[:, lo : lo + 128]
        rest[t, ROWS_TAPS : ROWS_TAPS + per, :taps] = gtap[t * per : (t + 1) * per, FLIP_AT : FLIP_AT + taps]
    start_all(v1)
    for lane in lanes:
        lane[1]()
    wait_all(v1)
    nsum[...] = norms[...] + nbuf[...]
    rsum[...] = rest[me.t] + rbuf[...]
    v2 = []
    for k in range(1, dp):
        j = lax.rem(me.i + k, dp)
        v2.append(remote(nsum.at[j], nall.at[k], v_ss.at[2 * k], v_rs.at[2 * k], (j, me.t)))
        v2.append(remote(rsum, rall.at[k], v_ss.at[2 * k + 1], v_rs.at[2 * k + 1], (j, me.t)))
    start_all(v2)
    todo = list(zip(first, second[1:]))
    stages = [lane[s] for s in (2, 3) for lane in lanes]
    at = [2, 4, 6, 8, 10, 12]
    for k, (a, b) in enumerate(todo):
        while at and k == at[0]:
            at.pop(0)
            stages.pop(0)()
        a.wait()
        b.start()
    for st in stages:
        st()
    wait_all(v2)
    ntot = nsum[me.i]
    rtot = rsum[...]
    for k in range(1, dp):
        ntot = ntot + nall[k]
        rtot = rtot + rall[k]
    for k in range(6):
        n_outs[k][...] = ntot[k, :share]
    for ref, first_row in ((gbq, ROWS_BQ), (gbv, ROWS_BV), (gbi, ROWS_BI)):
        size = ref.shape[0]
        ref[...] = jnp.concatenate([rtot[first_row + r : first_row + r + 1] for r in range(size // 128)], axis=1).reshape(size)
    gtaps[...] = rtot[ROWS_TAPS : ROWS_TAPS + per, :taps]
    for lane in lanes:
        lane[4]()
    own.wait()
    wait_all(second)


def call_carry_home(dp, tn, g_rows, dwqkv, vec, bsum, vecs, gtap, taps):
    s = jax.ShapeDtypeStruct
    r, w = g_rows.shape[1:]
    depth, cols = dwqkv.shape[4], dwqkv.shape[5] // 3
    share = s((depth, cols), F32)
    norms, rest = (dp, 8, 128), (tn, 24, 128)
    outs = (s((tn * dp, r, w), BF), share, share, share, s((cols,), F32), s((cols,), F32), s(taps.shape, F32),
            s((bsum.shape[1] // tn,), F32)) + (s((depth,), F32),) * 6
    scratch = sems(2 * dp) + sems(2 * dp) + sems(3 * reduce_count(dp)) + [DMA((4,))]
    scratch += [pltpu.VMEM(norms, F32), pltpu.VMEM(rest, F32),
                pltpu.VMEM(norms, F32), pltpu.VMEM(rest[1:], F32),
                pltpu.VMEM((dp,) + norms[1:], F32), pltpu.VMEM((dp,) + rest[1:], F32),
                pltpu.VMEM(norms, F32), pltpu.VMEM(rest[1:], F32)]
    for _ in range(3):
        scratch += reduce_bufs(dp, tn, depth, cols)
    return pl.pallas_call(
        functools.partial(carry_home, dp, tn),
        out_shape=outs,
        in_specs=[ANY, ANY] + [VM] * 4,
        out_specs=(ANY,) + (VM,) * 13,
        scratch_shapes=scratch,
        compiler_params=params(4, TOP),
        name="carry_home",
    )(g_rows, dwqkv, vec, bsum, vecs, gtap)


F32 = jnp.float32
BF = jnp.bfloat16
LAND = 64
ITERS = 6
HEADS_HERE = 6
ROWS_BQ, ROWS_BV, ROWS_BI, ROWS_TAPS = 0, 3, 6, 18
EDGE = 112
TAPS = 33
FLIP_AT = 367


def nn(a, b):
    return lax.dot_general(a, b, (((1,), (0,)), ((), ())), preferred_element_type=F32)


def nt(a, b):
    return lax.dot_general(a, b, (((1,), (1,)), ((), ())), preferred_element_type=F32)


def turn(a):
    return jnp.transpose(a, (1, 0))


def same_head(rows, columns):
    left = lax.broadcasted_iota(jnp.int32, (rows, columns), 0) // LAND
    right = lax.broadcasted_iota(jnp.int32, (rows, columns), 1) // LAND
    return left == right


def spread(small):
    n = small.shape[1] // LAND
    tall = jnp.concatenate([small] * n, axis=0)
    return jnp.where(same_head(n * LAND, n * LAND), tall, jnp.zeros_like(tall))


def gather_diag(full):
    n = full.shape[1] // LAND
    lane = lax.broadcasted_iota(jnp.int32, (LAND, full.shape[1]), 1) // LAND
    out = full[:LAND]
    for h in range(1, n):
        out = jnp.where(lane == h, full[h * LAND : (h + 1) * LAND], out)
    return out


def halves(a):
    high = a.astype(BF)
    return high, (a - high.astype(F32)).astype(BF)


def pair_nn(a, b):
    ah, al = halves(a)
    bh, bl = halves(b)
    bh, bl = spread(bh), spread(bl)
    wide = jnp.concatenate([bh, bl], axis=1)
    r = nn(jnp.concatenate([ah, al], axis=1), jnp.concatenate([wide, wide], axis=0))
    return r[:, : 2 * LAND] + r[:, 2 * LAND :]


def pair_nt(a, b):
    ah, al = halves(a)
    bh, bl = halves(b)
    bh, bl = spread(bh), spread(bl)
    tall = jnp.concatenate([bh, bl], axis=0)
    r = nt(jnp.concatenate([ah, al], axis=1), jnp.concatenate([tall, tall], axis=1))
    return r[:, : 2 * LAND] + r[:, 2 * LAND :]


def pair_turn(a):
    t = turn(a)
    return jnp.concatenate([t[:LAND], t[LAND:]], axis=1)


def pair_sum(a):
    left = lax.broadcasted_iota(jnp.int32, a.shape, 1) < LAND
    low = jnp.sum(jnp.where(left, a, 0.0), axis=1, keepdims=True)
    high = jnp.sum(jnp.where(left, 0.0, a), axis=1, keepdims=True)
    return jnp.where(left, low, high)


def pair_softmax(a):
    left = lax.broadcasted_iota(jnp.int32, a.shape, 1) < LAND
    low = jnp.max(jnp.where(left, a, -1e30), axis=1, keepdims=True)
    high = jnp.max(jnp.where(left, -1e30, a), axis=1, keepdims=True)
    e = jnp.exp(a - jnp.where(left, low, high))
    return e / pair_sum(e)


def pair_eye():
    r = lax.broadcasted_iota(jnp.int32, (LAND, 2 * LAND), 0)
    c = lax.broadcasted_iota(jnp.int32, (LAND, 2 * LAND), 1) % LAND
    return jnp.where(r == c, 1.0, 0.0).astype(F32)


def toeplitz(row, size, width):
    return pltpu.roll(jnp.broadcast_to(row, (size, width)), 0, 1, stride=1, stride_axis=0)


def blocks_of(ref, lower, block):
    length = ref.shape[1] - 256
    return jnp.concatenate(
        [ref[lower : lower + LAND, at : at + block + 256] for at in range(0, length, block)], axis=0
    )


def unblock(stacked, block):
    n = stacked.shape[0] // LAND
    return jnp.concatenate([stacked[i * LAND : (i + 1) * LAND] for i in range(n)], axis=1)


def own_sequence():
    return lax.axis_index("tensor") * lax.axis_size("dp") + lax.axis_index("dp")


def side_row(small_ref, t, first, count):
    return jnp.concatenate([small_ref[t, r : r + 1, :] for r in range(first, first + count)], axis=1)


def band_of(rows, head):
    h = head % HEADS_HERE
    row = jnp.concatenate([rows[head // HEADS_HERE][h : h + 1, :], jnp.zeros((1, 384), F32)], axis=1)
    return toeplitz(pltpu.roll(row, EDGE, 1), 256, 512).astype(BF)


def tap_rows(small_ref, t):
    return small_ref[t, ROWS_TAPS : ROWS_TAPS + 8, :]


def reversed_taps(rows):
    turned = jnp.where(
        lax.broadcasted_iota(jnp.int32, (128, 128), 0) + lax.broadcasted_iota(jnp.int32, (128, 128), 1) == TAPS - 1, 1.0, 0.0
    ).astype(BF)
    return nn(rows.astype(BF), turned)


def attend_forward(dp, x_in, w_in, small_ref, ids_ref, wi_ref, wf_ref, cot_ref,
                   q_out, k_out, v_out, near_out, far_out, ctx_out, lq_ref, lk_ref, mix_ref, sum_ref, ker_ref,
                   z_out, a_out, v2_out, w2_out, wi_all, wf_all, cota_ref, pad_ref, x_ref, w_ref, q_ref, k_ref, v_ref,
                   near_ref, far_ref, ctx_ref, z_ref, a_ref, v2_ref, w2_ref, g_ss, g_rs, c_ss, c_rs, local, move):
    length, width = x_ref.shape
    tn = w_ref.shape[0]
    loads = [Fetch(x_in, x_ref, move.at[0]).start(), Fetch(w_in, w_ref, move.at[1]).start()]
    q_w, k_w, v_w, near_w, far_w, ctx_w, z_w, a_w, v2_w, w2_w = writes = [
        Fetch(a, b, move.at[2 + k]) for k, (a, b) in enumerate((
            (q_ref, q_out), (k_ref, k_out), (v_ref, v_out), (near_ref, near_out), (far_ref, far_out), (ctx_ref, ctx_out),
            (z_ref, z_out), (a_ref, a_out), (v2_ref, v2_out), (w2_ref, w2_out)))]
    cols = width // tn
    scale = LAND ** -0.25
    rows_at = 256
    pairs = width // 128
    groups = width // 256
    me = Place(dp, tn)
    n = gather_count(dp)
    half = wi_ref.shape[1] // 2
    lanes = []
    for p, (src, dst) in enumerate(((wi_ref, wi_all), (wf_ref, wf_all))):
        for h in range(2):
            own, k = pl.ds(h * half, half), 2 * p + h
            lanes.append(gather_lane(me, src, own, dst, own, h == 1, Sub(g_ss, k * n), Sub(g_rs, k * n), local.at[k]))

    def stage(pair, s):
        def run():
            for lane in lanes[2 * pair : 2 * pair + 2]:
                lane[s]()
        return run

    greet(me)
    stage(0, 0)()
    stage(1, 0)()
    arriving = []
    for k in range(1, early_blocks(dp) + 1):
        j = lax.rem(me.i + k, dp)
        arriving.append(remote(cot_ref.at[me.t * dp + j], cota_ref.at[me.i], c_ss.at[k], c_rs.at[k], (j, me.t)))
    start_all(arriving)
    tick = Ticks([stage(0, 1), stage(0, 2), stage(1, 1), stage(0, 3), stage(1, 2), stage(1, 3), stage(0, 4), stage(1, 4)])
    bq = [side_row(small_ref, t, ROWS_BQ, 3) for t in range(tn)]
    bv = [side_row(small_ref, t, ROWS_BV, 3) for t in range(tn)]

    def project(i, carry):
        at = pl.ds(pl.multiple_of(i * rows_at, rows_at), rows_at)
        for t in range(tn):
            out = nn(x_ref[at, :], w_ref[t])
            own = slice(t * cols, (t + 1) * cols)
            q_ref[at, own] = ((out[:, :cols] + bq[t]) * scale).astype(BF)
            k_ref[at, own] = (out[:, cols : 2 * cols] * scale).astype(BF)
            v_ref[at, own] = (out[:, 2 * cols :] + bv[t]).astype(BF)
        return carry

    wait_all(loads)
    lax.fori_loop(0, length // rows_at, project, 0)
    start_all([q_w, k_w, v_w])

    ids = ids_ref[pl.ds(own_sequence(), 1), :]
    member = jnp.where(lax.broadcasted_iota(jnp.int32, (LAND, length), 0) == ids, 1.0, 0.0).astype(F32)
    count = jnp.sum(member, axis=1, keepdims=True)
    member = member.astype(BF)
    valid = ids < LAND
    lq_ref[...] = (nn(member, q_ref[...]) / count).astype(BF)
    lk_ref[...] = (nn(member, k_ref[...]) / count).astype(BF)

    eye = pair_eye()
    for p in range(pairs):
        own = slice(p * 128, (p + 1) * 128)
        scores = nt(lq_ref[:, own], spread(lk_ref[:, own]))
        kernel = pair_softmax(scores)
        ker_ref[:, own] = kernel
        left = lax.broadcasted_iota(jnp.int32, kernel.shape, 1) < LAND
        total = jnp.sum(pair_sum(kernel * kernel), axis=0, keepdims=True)
        z_ref[0, :, own] = pair_turn(kernel) / total
    tick()

    for g in range(groups):
        own = slice(g * 256, (g + 1) * 256)
        scores = nt(spread(lk_ref[:, own]), q_ref[:, own]).reshape(4, LAND, length)
        scores = jnp.exp(scores - jnp.max(scores, axis=1, keepdims=True))
        scores = scores / jnp.sum(scores, axis=1, keepdims=True)
        near_ref[own, :] = scores.reshape(256, length).astype(BF)
        scores = nt(spread(lq_ref[:, own]), k_ref[:, own])
        scores = jnp.where(valid, scores, -1e30)
        scores = jnp.exp(scores - jnp.max(scores, axis=1, keepdims=True))
        scores = scores / jnp.sum(scores, axis=1, keepdims=True)
        far_ref[own, :] = scores.astype(BF)
        sum_ref[:, own] = gather_diag(nn(far_ref[own, :], v_ref[:, own]))
    tick()
    start_all([near_w, far_w])

    def iterate(n, carry):
        for p in range(pairs):
            own = slice(p * 128, (p + 1) * 128)
            z = z_ref[n, :, own]
            a = pair_nn(ker_ref[:, own], z)
            v2 = 15.0 * eye - pair_nn(a, 7.0 * eye - a)
            w2 = 13.0 * eye - pair_nn(a, v2)
            a_ref[n, :, own] = a
            v2_ref[n, :, own] = v2
            w2_ref[n, :, own] = w2
            z_ref[n + 1, :, own] = 0.25 * pair_nn(z, w2)
        return carry

    lax.fori_loop(0, ITERS // 2, iterate, 0)
    tick()
    lax.fori_loop(ITERS // 2, ITERS, iterate, 0)
    start_all([z_w, a_w, v2_w, w2_w])

    for p in range(pairs):
        own = slice(p * 128, (p + 1) * 128)
        mix_ref[:, own] = pair_nn(z_ref[ITERS, :, own], sum_ref[:, own]).astype(BF)

    pad_ref[...] = jnp.zeros_like(pad_ref)
    taps = [tap_rows(small_ref, t) for t in range(tn)]
    for g in range(groups):
        own = slice(g * 256, (g + 1) * 256)
        att = nn(turn(spread(mix_ref[:, own])), near_ref[own, :])
        vt = turn(v_ref[:, own])
        pad_ref[:, 128 : 128 + length] = jnp.where(valid, vt, jnp.zeros_like(vt))
        parts = []
        for h in range(4):
            band = band_of(taps, 4 * g + h)
            parts.append(unblock(nt(blocks_of(pad_ref, h * LAND, 256), band), 256))
        att = (att + jnp.concatenate(parts, axis=0)).astype(BF)
        ctx_ref[:, own] = turn(att)
    ctx_w.start()
    tick.rest()
    wait_all(arriving)
    wait_all(writes)


def early_blocks(dp):
    return dp // 2


def call_attend_forward(dp, x, w, small, ids, wi, wf, cot):
    length, width = x.shape
    s = jax.ShapeDtypeStruct
    big = s((length, width), BF)
    tall = s((width, length), BF)
    low = s((LAND, width), BF)
    wide = s((LAND, width), F32)
    steps = s((ITERS, LAND, width), F32)
    tn = w.shape[0]
    depth, units = wi.shape
    whole = s((tn, dp // 4, 2, 2, depth, units), BF)
    outs = (big, big, big, tall, tall, big, low, low, low, wide, wide, s((ITERS + 1, LAND, width), F32), steps, steps, steps,
            whole, whole, s((dp,) + cot.shape[1:], BF))
    vm = pltpu.VMEM
    return pl.pallas_call(
        functools.partial(attend_forward, dp),
        out_shape=outs,
        in_specs=[ANY] * 2 + [VM] * 2 + [ANY] * 3,
        out_specs=tuple([ANY] * 6 + [VM] * 5 + [ANY] * 7),
        scratch_shapes=[vm((256, length + 256), BF)] + [vm(o.shape, o.dtype) for o in (x, w) + outs[:6] + outs[11:15]]
        + sems(4 * gather_count(dp)) + sems(dp) + [DMA((4,)), DMA((12,))],
        compiler_params=params(1, TOP),
        name="attend_forward",
    )(x, w, small, ids, wi, wf, cot)


ROOT_HALF = 0.7071067811865476
P_ERF = 0.3275911
C_ERF = (0.254829592, -0.284496736, 1.421413741, -1.453152027, 1.061405429)


def gelu_both(u):
    x = jnp.abs(u) * ROOT_HALF
    e = jnp.exp(-0.5 * u * u)
    t = 1.0 / (1.0 + P_ERF * x)
    poly = C_ERF[4]
    for c in (C_ERF[3], C_ERF[2], C_ERF[1], C_ERF[0]):
        poly = poly * t + c
    tail = 0.5 * poly * t * e
    phi = jnp.where(u < 0.0, tail, 1.0 - tail)
    return u * phi, phi + u * e * 0.3989422804014327


def norm_parts(r):
    n = r.shape[1]
    center = r - jnp.sum(r, axis=1, keepdims=True) * (1.0 / n)
    spread_ = jnp.sum(center * center, axis=1, keepdims=True) * (1.0 / n)
    rstd = lax.rsqrt(spread_ + 1e-05)
    return center * rstd, rstd


def norm_back(e, normed, rstd):
    n = e.shape[1]
    mean_e = jnp.sum(e, axis=1, keepdims=True) * (1.0 / n)
    mean_en = jnp.sum(e * normed, axis=1, keepdims=True) * (1.0 / n)
    return rstd * (e - mean_e - normed * mean_en)


def fold(a):
    return jnp.sum(a.reshape(a.shape[0] // 8, 8, a.shape[1]), axis=0)


def feed(dp, x_in, ctx_in, wo_in, wi_in, wf_in, bo_in, g1_in, s1_in, bf_in, g2_in, s2_in, small_ref, cot_ref, cota_ref,
         gr1_out, dc_out, dwo_out, dwi_out, dwf_out, vec_ref, bsum_ref, home_ref,
         act_ref, gi_ref, hid_ref, gr2_ref, turn_ref, n1_ref, n2_ref, rs1_ref, rs2_ref, out_ref, cots_ref,
         x_ref, ctx_ref, wo_ref, wi_ref, wf_ref, gr1_ref, dc_ref, dwo_ref, dwi_ref, dwf_ref,
         c_ss, c_rs, h_ss, h_rs, f_ss, f_rs, local, move):
    length, width = x_ref.shape
    tn = wo_ref.shape[0]
    cols = width // tn
    units = wi_ref.shape[2]
    size = 256
    chunk = 512
    part = length // dp
    per = size // part
    me = Place(dp, tn)
    x_l, ctx_l, wo_l, wi_l, wf_l = loads = [
        Fetch(a, b, move.at[k]).start() for k, (a, b) in enumerate((
            (x_in, x_ref), (ctx_in, ctx_ref), (wo_in, wo_ref), (wi_in, wi_ref), (wf_in, wf_ref)))]
    greet(me)
    mine = me.t * dp
    early = early_blocks(dp)
    arriving = [pltpu.make_async_copy(cot_ref.at[mine + me.i], cots_ref.at[me.i], local.at[0])]
    leaving, passing = [], []
    partner = (me.i, 1 - me.t)
    for k in range(1, dp):
        j, back = lax.rem(me.i + k, dp), lax.rem(me.i + dp - k, dp)
        if k <= early:
            arriving.append(pltpu.make_async_copy(cota_ref.at[back], cots_ref.at[back], c_ss.at[k]))
        else:
            arriving.append(remote(cot_ref.at[mine + j], cots_ref.at[me.i], c_ss.at[k], c_rs.at[k], (j, me.t)))
        leaving.append(remote(out_ref.at[j], home_ref.at[mine + me.i], h_ss.at[k], h_rs.at[k], (j, me.t)))
        if k < late_blocks(dp):
            passing.append(remote(home_ref.at[mine + back], home_ref.at[mine + back], f_ss.at[k], f_rs.at[k], partner))
    kept = pltpu.make_async_copy(out_ref.at[me.i], home_ref.at[mine + me.i], local.at[1])
    across = remote(out_ref.at[me.i], home_ref.at[mine + me.i], f_ss.at[0], f_rs.at[0], partner)
    start_all(arriving)
    bo, g1, s1, bf, g2, s2 = [
        r[...].astype(F32).reshape(1, width) for r in (bo_in, g1_in, s1_in, bf_in, g2_in, s2_in)]
    bi = [side_row(small_ref, t, ROWS_BI, units // 128) for t in range(tn)]
    vec_ref[...] = jnp.zeros_like(vec_ref)
    bsum_ref[...] = jnp.zeros_like(bsum_ref)

    def rows_at(i):
        return pl.ds(pl.multiple_of(i * size, size), size)

    def forward(i, carry):
        at = rows_at(i)
        attn = bo + x_ref[at, :].astype(F32)
        for t in range(tn):
            attn = attn + nt(ctx_ref[at, t * cols : (t + 1) * cols], wo_ref[t])
        n1, rstd1 = norm_parts(attn)
        n1_ref[at, :] = n1
        rs1_ref[at, :] = rstd1
        hidden = n1 * g1 + s1
        hid = hidden.astype(BF)
        hid_ref[at, :] = hid
        r2 = hidden + bf
        for t in range(tn):
            for c in range(0, units, chunk):
                own = slice(t * units + c, t * units + c + chunk)
                act, gp = gelu_both(nn(hid, wi_ref[t, :, c : c + chunk]) + bi[t][:, c : c + chunk])
                act_ref[at, own] = act.astype(BF)
                gi_ref[at, own] = gp.astype(BF)
        for t in range(tn):
            r2 = r2 + nt(act_ref[at, t * units : (t + 1) * units], wf_ref[t])
        n2, rstd2 = norm_parts(r2)
        n2_ref[at, :] = n2
        rs2_ref[at, :] = rstd2
        out_ref[pl.ds(i * per, per)] = (n2 * g2 + s2).reshape(per, part, width).astype(BF)
        return carry

    def backward(i, carry):
        at = rows_at(i)
        cot = cots_ref[pl.ds(i * per, per)].astype(F32).reshape(size, width)
        n2 = n2_ref[at, :]
        gr2 = norm_back(cot * g2, n2, rs2_ref[at, :])
        vec_ref[5] += fold(cot)
        vec_ref[4] += fold(cot * n2)
        vec_ref[3] += fold(gr2)
        low = gr2.astype(BF)
        gr2_ref[at, :] = low
        for t in range(tn):
            for c in range(0, units, chunk):
                own = slice(t * units + c, t * units + c + chunk)
                gi = nn(low, wf_ref[t, :, c : c + chunk]) * gi_ref[at, own].astype(F32)
                bsum_ref[:, own] += fold(gi)
                gi_ref[at, own] = gi.astype(BF)
        gh = gr2
        for t in range(tn):
            gh = gh + nt(gi_ref[at, t * units : (t + 1) * units], wi_ref[t])
        n1 = n1_ref[at, :]
        gr1 = norm_back(gh * g1, n1, rs1_ref[at, :])
        vec_ref[2] += fold(gh)
        vec_ref[1] += fold(gh * n1)
        vec_ref[0] += fold(gr1)
        low1 = gr1.astype(BF)
        gr1_ref[at, :] = low1
        for t in range(tn):
            dc_ref[at, t * cols : (t + 1) * cols] = nn(low1, wo_ref[t]).astype(BF)
        return carry

    wait_all(loads)
    lax.fori_loop(0, length // size, forward, 0)
    start_all(leaving)
    kept.start()
    across.start()
    wait_all(arriving)
    n_back = length // size
    done = 0
    for i in range(n_back):
        backward(i, 0)
        upto = len(passing) * (i + 1) // n_back
        for k in range(done, upto):
            leaving[k].wait()
            passing[k].start()
        done = upto

    outs = [Fetch(gr1_ref, gr1_out, move.at[5]).start(), Fetch(dc_ref, dc_out, move.at[6]).start()]
    turn_ref[...] = turn(gr2_ref[...])
    for t in range(tn):
        for c in range(0, units, chunk):
            own = slice(t * units + c, t * units + c + chunk)
            dwf_ref[t, :, c : c + chunk] = nn(turn_ref[...], act_ref[:, own]).astype(BF)
    outs.append(Fetch(dwf_ref, dwf_out, move.at[7]).start())
    turn_ref[...] = turn(hid_ref[...])
    for t in range(tn):
        for c in range(0, units, chunk):
            own = slice(t * units + c, t * units + c + chunk)
            dwi_ref[t, :, c : c + chunk] = nn(turn_ref[...], gi_ref[:, own]).astype(BF)
    outs.append(Fetch(dwi_ref, dwi_out, move.at[8]).start())
    turn_ref[...] = turn(gr1_ref[...])
    for t in range(tn):
        dwo_ref[t] = nn(turn_ref[...], ctx_ref[:, t * cols : (t + 1) * cols]).astype(BF)
    outs.append(Fetch(dwo_ref, dwo_out, move.at[9]).start())
    wait_all(leaving[done:])
    kept.wait()
    across.wait()
    wait_all(passing)
    wait_all(outs)


def late_blocks(dp):
    return dp // 2


def call_feed(dp, x, ctx, wo, wi, wf, vectors, small, cot, cota):
    length, width = x.shape
    tn, _, cols = wo.shape
    units = wi.shape[2]
    s = jax.ShapeDtypeStruct
    big = s((length, width), BF)
    blocks = (dp,) + cot.shape[1:]
    outs = (big, big, s((tn, width, cols), BF), s((tn, width, units), BF), s((tn, width, units), BF),
            s((6, 8, width), F32), s((8, tn * units), F32), s((tn * dp,) + blocks[1:], BF))
    vm = pltpu.VMEM
    return pl.pallas_call(
        functools.partial(feed, dp),
        out_shape=outs,
        in_specs=[ANY] * 5 + [VM] * 7 + [ANY] * 2,
        out_specs=tuple([ANY] * 5 + [VM] * 2 + [ANY]),
        scratch_shapes=[vm((length, tn * units), BF), vm((length, tn * units), BF), vm((length, width), BF),
                        vm((length, width), BF), vm((width, length), BF), vm((length, width), F32),
                        vm((length, width), F32), vm((length, 1), F32), vm((length, 1), F32), vm(blocks, BF),
                        vm(blocks, BF)] + [vm(o.shape, o.dtype) for o in (x, ctx, wo, wi, wf) + outs[:5]]
        + sems(dp) * 3 + [DMA((2,)), DMA((10,))],
        compiler_params=params(2, TOP),
        name="feed_forward",
    )(x, ctx, wo, wi, wf, *vectors, small, cot, cota)


NORTH_LANE = 3


def row_of(column):
    return turn(jnp.broadcast_to(column, (column.shape[0], 128)))[0:1, :]


def attend_backward(dp, ids_ref, small_ref, lq_ref, lk_ref, mix_ref, sum_ref, ker_ref,
                    x_in, w_in, q_in, k_in, v_in, near_in, far_in, z_in, a_in, v2_in, w2_in, dc_in, gr1_in,
                    dwo_in, dwi_in, dwf_in, home_in,
                    gtok_ref, dw_ref, vecs_ref, gtap_ref, go_ref, gi_ref, gf_ref, home_ref,
                    x_ref, w_ref, q_ref, k_ref, v_ref, near_ref, far_ref, z_ref, a_ref, v2_ref, w2_ref, dc_ref, gr1_ref,
                    pre_ref, glq_ref, glk_ref, gsum_ref, gz_ref, gk_ref, padv_ref, padc_ref, xt_ref,
                    g_ss, g_rs, y_ss, y_rs, local, move, *bufs):
    near_l, dc_l, z_l, a_l, v2_l, w2_l, far_l, q_l, k_l, v_l, x_l, w_l, gr1_l = [
        Fetch(a, b, move.at[k]).start() for k, (a, b) in enumerate((
            (near_in, near_ref), (dc_in, dc_ref), (z_in, z_ref), (a_in, a_ref), (v2_in, v2_ref), (w2_in, w2_ref),
            (far_in, far_ref), (q_in, q_ref), (k_in, k_ref), (v_in, v_ref), (x_in, x_ref), (w_in, w_ref), (gr1_in, gr1_ref)))]
    length, width = x_ref.shape
    tn = w_ref.shape[0]
    cols = width // tn
    scale = LAND ** -0.25
    size = length // dp
    pairs = width // 128
    groups = width // 256
    me = Place(dp, tn)
    n = reduce_count(dp)
    half = dwi_in.shape[5] // 2
    plan = [(dwf_in, 0, half, gf_ref), (dwf_in, half, half, gf_ref), (dwi_in, 0, half, gi_ref), (dwi_in, half, half, gi_ref),
            (dwo_in, 0, cols, go_ref)]
    lanes = []
    for k, (src, lo, w, dst) in enumerate(plan):
        lanes.append(reduce_lane(me, src, lo, w, bufs[5 * k : 5 * k + 5], Sub(g_ss, k * n), Sub(g_rs, k * n), local.at[k],
                                 [(dst, lo, 0, w)], k == NORTH_LANE))
    sides = []
    for k in range(late_blocks(dp), dp):
        j = me.t * dp + lax.rem(me.i + dp - k, dp)
        sides.append(remote(home_ref.at[j], home_ref.at[j], y_ss.at[k], y_rs.at[k], (me.i, 1 - me.t)))
    greet(me, False)
    for k in (3, 0, 1, 2, 4):
        lanes[k][0]()
    tick = Ticks([lanes[3][1], lanes[0][1], lanes[1][1], lanes[2][1], lanes[4][1]] + [c.start for c in sides]
                 + [lanes[0][2], lanes[3][2], lanes[1][2], lanes[0][3], lanes[2][2], lanes[1][3], lanes[3][3], lanes[4][2],
                    lanes[2][3], lanes[4][3]])
    ids = ids_ref[pl.ds(own_sequence(), 1), :]
    member = jnp.where(lax.broadcasted_iota(jnp.int32, (LAND, length), 0) == ids, 1.0, 0.0).astype(F32)
    count = jnp.sum(member, axis=1, keepdims=True)
    member = member.astype(BF)
    valid = ids < LAND
    eye = pair_eye()

    near_l.wait()
    dc_l.wait()
    for g in range(groups):
        own = slice(g * 256, (g + 1) * 256)
        gsum_ref[:, own] = gather_diag(nn(near_ref[own, :], dc_ref[:, own]))
    tick(5 + len(sides))
    wait_all([z_l, a_l, v2_l, w2_l])
    for p in range(pairs):
        own = slice(p * 128, (p + 1) * 128)
        gmix = gsum_ref[:, own]
        gz_ref[:, own] = pair_nt(gmix, sum_ref[:, own])
        gsum_ref[:, own] = pair_nn(pair_turn(z_ref[ITERS, :, own]), gmix)

    gk_ref[...] = jnp.zeros_like(gk_ref)

    def iterate(m, carry):
        n = ITERS - 1 - m
        for p in range(pairs):
            own = slice(p * 128, (p + 1) * 128)
            grad = 0.25 * gz_ref[:, own]
            kernel = ker_ref[:, own]
            z = z_ref[n, :, own]
            a = a_ref[n, :, own]
            v2 = v2_ref[n, :, own]
            w2 = w2_ref[n, :, own]
            dw2 = pair_nn(pair_turn(z), grad)
            at = pair_turn(a)
            dv2 = -pair_nn(at, dw2)
            da = -pair_nt(dw2, v2) - pair_nt(dv2, 7.0 * eye - a) + pair_nn(at, dv2)
            gk_ref[:, own] += pair_nt(da, z)
            gz_ref[:, own] = pair_nt(grad, w2) + pair_nn(pair_turn(kernel), da)
        return carry

    lax.fori_loop(0, ITERS, iterate, 0)
    tick(1)
    wait_all([far_l, q_l, k_l, v_l])

    for p in range(pairs):
        own = slice(p * 128, (p + 1) * 128)
        kernel = ker_ref[:, own]
        gz = gz_ref[:, own]
        total = jnp.sum(pair_sum(kernel * kernel), axis=0, keepdims=True)
        kt = pair_turn(kernel)
        back = jnp.sum(pair_sum(gz * kt), axis=0, keepdims=True)
        gk = gk_ref[:, own] + pair_turn(gz) / total - kernel * (2.0 * back / (total * total))
        mid = kernel * (gk - pair_sum(kernel * gk))
        glq_ref[:, own] = pair_nn(mid, lk_ref[:, own].astype(F32))
        glk_ref[:, own] = pair_nn(pair_turn(mid), lq_ref[:, own].astype(F32))

    flip = jnp.where(
        lax.broadcasted_iota(jnp.int32, (256, 256), 0) + lax.broadcasted_iota(jnp.int32, (256, 256), 1) == 255, 1.0, 0.0
    ).astype(BF)
    taps = [reversed_taps(tap_rows(small_ref, t)) for t in range(tn)]
    padv_ref[...] = jnp.zeros_like(padv_ref)
    padc_ref[...] = jnp.zeros_like(padc_ref)
    inner = slice(128, 128 + length)
    for g in range(groups):
        own = slice(g * 256, (g + 1) * 256)
        lk4 = spread(lk_ref[:, own])
        lq4 = spread(lq_ref[:, own])
        near = near_ref[own, :].astype(F32)
        gnear = nt(spread(mix_ref[:, own]), dc_ref[:, own])
        drop = jnp.sum((near * gnear).reshape(4, LAND, length), axis=1, keepdims=True)
        first = (near * (gnear.reshape(4, LAND, length) - drop).reshape(256, length)).astype(BF)
        glk_ref[:, own] += gather_diag(nn(first, q_ref[:, own]))
        gsum4 = spread(gsum_ref[:, own].astype(BF))
        far = far_ref[own, :].astype(F32)
        gfar = nt(gsum4, v_ref[:, own])
        drop = jnp.sum(far * gfar, axis=1, keepdims=True)
        third = (far * (gfar - drop)).astype(BF)
        glq_ref[:, own] += gather_diag(nn(third, k_ref[:, own]))
        glq = turn((glq_ref[:, own] / count).astype(BF))
        glk = turn((glk_ref[:, own] / count).astype(BF))
        dq = (nn(turn(lk4), first) + nn(glq, member)) * scale
        dk = (nn(turn(lq4), third) + nn(glk, member)) * scale
        dv = nn(turn(gsum4), far_ref[own, :])

        vt = turn(v_ref[:, own])
        padv_ref[:, inner] = jnp.where(valid, vt, jnp.zeros_like(vt))
        padc_ref[:, inner] = turn(dc_ref[:, own])
        parts = []
        for h in range(4):
            band = band_of(taps, 4 * g + h)
            parts.append(unblock(nt(blocks_of(padc_ref, h * LAND, 256), band), 256))
            plain = jnp.concatenate(
                [padc_ref[h * LAND : (h + 1) * LAND, 128 + at : 128 + at + 256] for at in range(0, length, 256)], axis=0
            )
            gram = nn(nt(flip, plain).astype(BF), blocks_of(padv_ref, h * LAND, 256))
            gram = pltpu.roll(gram, 0, 1, stride=1, stride_axis=0)
            gtap_ref[4 * g + h : 4 * g + h + 1, :] = jnp.sum(gram, axis=0, keepdims=True)
        dv = dv + jnp.where(valid, jnp.concatenate(parts, axis=0), 0.0)
        vecs_ref[0:1, own] = row_of(jnp.sum(dq, axis=1, keepdims=True))
        vecs_ref[1:2, own] = row_of(jnp.sum(dv, axis=1, keepdims=True))
        for lower in range(0, 256, 128):
            c = g * 256 + lower
            t, r = c // cols, c % cols
            pre_ref[t, r : r + 128, :] = dq[lower : lower + 128].astype(BF)
            pre_ref[t, cols + r : cols + r + 128, :] = dk[lower : lower + 128].astype(BF)
            pre_ref[t, 2 * cols + r : 2 * cols + r + 128, :] = dv[lower : lower + 128].astype(BF)
        if g > 0:
            tick(1)

    wait_all([x_l, w_l, gr1_l])
    xt_ref[...] = turn(x_ref[...])
    tick(1)
    for t in range(tn):
        dw_ref[t] = nt(xt_ref[...], pre_ref[t]).astype(BF)
    tick(2)
    for at in range(0, length, 256):
        part = nn(w_ref[0], pre_ref[0, :, at : at + 256])
        for t in range(1, tn):
            part = part + nn(w_ref[t], pre_ref[t, :, at : at + 256])
        gtok_ref[at // size : (at + 256) // size] = (
            (gr1_ref[at : at + 256, :].astype(F32) + turn(part)).reshape(256 // size, size, width).astype(BF)
        )
    tick.rest()
    for lane in lanes:
        lane[4]()
    wait_all(sides)


def call_attend_backward(dp, x, w, ids, small, saved, dc, gr1, dwo, dwi, dwf, home):
    q, k, v, near, far, lq, lk, mix, summ, ker, z, a, v2, w2 = saved
    length, width = x.shape
    tn = w.shape[0]
    cols = width // tn
    s = jax.ShapeDtypeStruct
    depth, units = dwi.shape[4:]
    outs = (s((dp,) + home.shape[1:], BF), s((tn, width, 3 * cols), BF), s((8, width), F32),
            s((width // LAND, 512), F32), s((depth, cols), F32), s((depth, units), F32), s((depth, units), F32),
            s(home.shape, BF))
    little = (ids, small, lq, lk, mix, summ, ker)
    large = (x, w, q, k, v, near, far, z, a, v2, w2, dc, gr1)
    args = little + large + (dwo, dwi, dwf, home)
    vm = pltpu.VMEM
    mini = vm((LAND, width), F32)
    n = 5 * reduce_count(dp)
    scratch = [vm(b.shape, b.dtype) for b in large] + [vm((tn, 3 * cols, length), BF)] + [mini] * 5
    scratch += [vm((256, length + 256), BF), vm((256, length + 256), BF), vm((width, length), BF)]
    scratch += sems(n) + sems(dp) + [DMA((5,)), DMA((len(large),))]
    for k, wide in enumerate((units // 2,) * 4 + (cols,)):
        scratch += reduce_bufs(dp, tn, depth, wide, k == NORTH_LANE)
    return pl.pallas_call(
        functools.partial(attend_backward, dp),
        out_shape=outs,
        in_specs=[VM] * len(little) + [ANY] * (len(args) - len(little)),
        out_specs=tuple([VM] * 7 + [ANY]),
        scratch_shapes=scratch,
        input_output_aliases={len(args) - 1: 7},
        compiler_params=params(3, TOP),
        name="attend_backward",
    )(*args)


def local(tokens, cotangent, landmark_ids, w_query, w_key, w_value, b_query, b_value, conv_taps, w_out, b_out,
          first_gain, first_shift, w_inner, b_inner, w_outer, b_outer, second_gain, second_shift):
    dp = lax.axis_size("dp")
    tn = lax.axis_size("tensor")
    part, width = tokens.shape[1:]
    length = dp * part
    cols = w_query.shape[1]
    vectors = [b_out, first_gain, first_shift, b_outer, second_gain, second_shift]

    def join(w):
        return w.reshape(tn, width, w.shape[-1])

    def cut(g):
        return g.reshape(tn, dp // 4, 2, 2, width // dp, g.shape[2])

    rows, wqkv, wout, small = call_bring(
        dp, tn, tokens, w_query, w_key, w_value, w_out, b_query, b_value, b_inner, conv_taps
    )
    rows = rows.reshape(length, width)
    wqkv, wout = join(wqkv), join(wout)
    q, k, v, near, far, ctx, *rest_saved, wi, wf, cota = call_attend_forward(
        dp, rows, wqkv, small, landmark_ids, w_inner, w_outer, cotangent
    )
    gr1, dc, dwo, dwi, dwf, vec, bsum, home = call_feed(
        dp, rows, ctx, wout, join(wi), join(wf), vectors, small, cotangent, cota
    )
    grad_rows, dwqkv, vecs, gtap, go, gi, gf, out_home = call_attend_backward(
        dp, rows, wqkv, landmark_ids, small, (q, k, v, near, far, *rest_saved), dc, gr1, cut(dwo), cut(dwi), cut(dwf), home
    )
    grad_home, gq, gk, gv, gbq, gbv, gtaps, gbi, gbo, gg1, gs1, gbf, gg2, gs2 = call_carry_home(
        dp, tn, grad_rows, cut(dwqkv), vec, bsum, vecs, gtap, conv_taps
    )
    return (out_home, grad_home, gq, gk, gv, gbq, gbv, gtaps, go, gbo, gg1, gs1, gi, gbi, gf, gbf, gg2, gs2)


def solution(mesh):
    return jax.shard_map(
        local,
        mesh=mesh,
        in_specs=(
            P(None, "dp", None),
            P(None, "dp", None),
            P(),
            P("dp", "tensor"),
            P("dp", "tensor"),
            P("dp", "tensor"),
            P("tensor"),
            P("tensor"),
            P("tensor", None),
            P("dp", "tensor"),
            P(),
            P(),
            P(),
            P("dp", "tensor"),
            P("tensor"),
            P("dp", "tensor"),
            P(),
            P(),
            P(),
        ),
        out_specs=(
            P(None, "dp", None),
            P(None, "dp", None),
            P("dp", "tensor"),
            P("dp", "tensor"),
            P("dp", "tensor"),
            P("tensor"),
            P("tensor"),
            P("tensor", None),
            P("dp", "tensor"),
            P("dp"),
            P("dp"),
            P("dp"),
            P("dp", "tensor"),
            P("tensor"),
            P("dp", "tensor"),
            P("dp"),
            P("dp"),
            P("dp"),
        ),
        check_vma=False,
    )
```

```python
import functools

import jax
import jax.numpy as jnp
from jax import lax
from jax.experimental import pallas as pl
from jax.experimental.pallas import tpu as pltpu
from jax.sharding import PartitionSpec as P

F32 = jnp.float32
BF = jnp.bfloat16
MESH = pl.DeviceIdType.MESH
ANY = pl.BlockSpec(memory_space=pl.ANY)
TOP = 62
VM = pl.BlockSpec(memory_space=pltpu.VMEM)
DMA = pltpu.SemaphoreType.DMA
SMALL_ROWS = 32


class Place:
    def __init__(self, dp, tn):
        self.dp, self.tn = dp, tn
        self.nz = dp // 4
        i = lax.axis_index("dp")
        self.i = i
        self.t = lax.axis_index("tensor")
        self.c = lax.rem(i, 2)
        self.x = lax.rem(i // 2, 2)
        self.z = i // 4

    def at(self, z=None, x=None, c=None, t=None):
        z = self.z if z is None else z
        x = self.x if x is None else x
        c = self.c if c is None else c
        t = self.t if t is None else t
        return (z * 4 + x * 2 + c, t)


def greet(me, rows=True):
    bar = pltpu.get_barrier_semaphore()
    if rows:
        peers = [(lax.rem(me.i + k, me.dp), me.t) for k in range(1, me.dp)]
    else:
        peers = [me.at(z=lax.rem(me.z + k, me.nz)) for k in range(1, me.nz)] + [me.at(x=1 - me.x), me.at(c=1 - me.c)]
    peers.append((me.i, 1 - me.t))
    for p in peers:
        pl.semaphore_signal(bar, 1, device_id=p, device_id_type=MESH)
    pl.semaphore_wait(bar, len(peers))


def remote(src, dst, ss, rs, to):
    return pltpu.make_async_remote_copy(
        src_ref=src, dst_ref=dst, send_sem=ss, recv_sem=rs, device_id=to, device_id_type=MESH
    )


def start_all(copies):
    for c in copies:
        c.start()


def wait_all(copies):
    for c in copies:
        c.wait()


def to_owner(me, src, out, ss, rs, local):
    copies = []
    for k in range(1, me.dp):
        j = lax.rem(me.i + k, me.dp)
        copies.append(remote(src.at[me.t * me.dp + j], out.at[me.i], ss.at[k], rs.at[k], (j, me.t)))
    copies.append(pltpu.make_async_copy(src.at[me.t * me.dp + me.i], out.at[me.i], local))
    return copies


def to_home(me, src, out, ss, rs, local):
    copies = []
    for k in range(1, me.dp):
        j = lax.rem(me.i + k, me.dp)
        copies.append(remote(src.at[j], out.at[me.i], ss.at[k], rs.at[k], (j, me.t)))
    copies.append(pltpu.make_async_copy(src.at[me.i], out.at[me.i], local))
    return copies


def gather_lane(me, src, own, out, cols, north_first, ss, rs, local):
    t, z, x, c, n = me.t, me.z, me.x, me.c, me.nz
    px, py, sib = me.at(x=1 - x), me.at(t=1 - t), me.at(c=1 - c)

    def move(ref, k, to):
        return remote(ref, ref, ss.at[k], rs.at[k], to)

    zs = [pltpu.make_async_copy(src.at[:, own], out.at[t, z, x, c, :, cols], local)]
    for k in range(1, n):
        to = me.at(z=lax.rem(z + k, n))
        zs.append(remote(src.at[:, own], out.at[t, z, x, c, :, cols], ss.at[k], rs.at[k], to))
    if north_first:
        first, second = move(out.at[t, :, x, c, :, cols], n, py), move(out.at[:, :, x, c, :, cols], n + 1, px)
        d2, d3 = move(out.at[:, :, x, c, :, cols], n + 2, sib), move(out.at[:, :, 1 - x, c, :, cols], n + 3, sib)
    else:
        first, second = move(out.at[t, :, x, c, :, cols], n, px), move(out.at[t, :, :, c, :, cols], n + 1, py)
        d2, d3 = move(out.at[t, :, :, c, :, cols], n + 2, sib), move(out.at[1 - t, :, :, c, :, cols], n + 3, sib)

    def s0():
        start_all(zs)

    def s1():
        wait_all(zs)
        first.start()

    def s2():
        first.wait()
        second.start()
        d2.start()

    def s3():
        second.wait()
        d3.start()

    def s4():
        d2.wait()
        d3.wait()

    return [s0, s1, s2, s3, s4]


def gather_count(dp):
    return dp // 4 + 4


def add_low(a, b):
    return (a.astype(F32) + b.astype(F32)).astype(BF)


def reduce_lane(me, src, lo, w, bufs, ss, rs, local, puts, north_first=False):
    t, z, x, c, n = me.t, me.z, me.x, me.c, me.nz
    mine, rc, r1, r2, rz = bufs
    cols = pl.ds(lo, w)

    def move(a, b, q, to):
        return remote(a, b, ss.at[q], rs.at[q], to)

    keep = pltpu.make_async_copy(src.at[:, :, :, c, :, cols], mine, local)
    core = move(src.at[:, :, :, 1 - c, :, cols], rc, 0, me.at(c=1 - c))
    px, py = me.at(x=1 - x), me.at(t=1 - t)
    if north_first:
        first = move(rc.at[1 - t], r1, 1, py)
        second = move(r1.at[:, 1 - x], r2, 2, px)
    else:
        first = move(rc.at[:, :, 1 - x], r1, 1, px)
        second = move(r1.at[1 - t], r2, 2, py)
    lines = []
    for q in range(1, n):
        to = lax.rem(z + q, n)
        lines.append(move(r2.at[to], rz.at[q], 2 + q, me.at(z=to)))

    def s0():
        keep.start()
        core.start()

    def s1():
        keep.wait()
        core.wait()
        rc[...] = add_low(rc[...], mine[...])
        first.start()

    def s2():
        first.wait()
        r1[...] = add_low(r1[...], rc[t] if north_first else rc[:, :, x])
        second.start()

    def s3():
        second.wait()
        r2[...] = add_low(r2[...], r1[:, x] if north_first else r1[t])
        start_all(lines)

    def s4():
        total = r2[z].astype(F32)
        wait_all(lines)
        for q in range(1, n):
            total = total + rz[q].astype(F32)
        for dst, at, first_col, width in puts:
            dst[:, at : at + width] = total[:, first_col : first_col + width]

    return [s0, s1, s2, s3, s4]


def reduce_bufs(dp, tn, depth, w, north_first=False):
    nz = dp // 4
    one = (nz, 2) if north_first else (tn, nz)
    return [pltpu.VMEM((tn, nz, 2, depth, w), BF), pltpu.VMEM((tn, nz, 2, depth, w), BF),
            pltpu.VMEM(one + (depth, w), BF), pltpu.VMEM((nz, depth, w), BF), pltpu.VMEM((nz, depth, w), BF)]


def reduce_count(dp):
    return dp // 4 + 2


class Fetch:
    def __init__(self, src, dst, sem):
        self.copy, self.open = pltpu.make_async_copy(src, dst, sem), True

    def start(self):
        self.copy.start()
        return self

    def wait(self):
        if self.open:
            self.copy.wait()
        self.open = False


class Sub:
    def __init__(self, ref, base):
        self.ref, self.base = ref, base

    @property
    def at(self):
        return self

    def __getitem__(self, k):
        return self.ref.at[self.base + k]


def together(functions):
    def run():
        for f in functions:
            f()
    return run


class Ticks:
    def __init__(self, stages):
        self.stages = list(stages)

    def __call__(self, count=1):
        for _ in range(min(count, len(self.stages))):
            self.stages.pop(0)()

    def rest(self):
        self(len(self.stages))


def sems(n):
    return [DMA((n,)), DMA((n,))]


def params(cid, mib):
    return pltpu.CompilerParams(collective_id=cid, has_side_effects=True, vmem_limit_bytes=mib * 2**20)


def fill_piece(piece, bq, bv, bi, taps):
    piece[...] = jnp.zeros_like(piece)
    for ref, first in ((bq, ROWS_BQ), (bv, ROWS_BV), (bi, ROWS_BI)):
        line = ref[...].astype(F32).reshape(1, ref.shape[0])
        for r in range(ref.shape[0] // 128):
            piece[first + r : first + r + 1, :] = line[:, r * 128 : (r + 1) * 128]
    heads, width = taps.shape
    tap = taps[...].astype(F32)
    piece[ROWS_TAPS : ROWS_TAPS + heads, :width] = tap


def bring(dp, tn, tok, wq, wk, wv, wo, bq, bv, bi, taps, rows, wqkv, wout, small,
          r_ss, r_rs, g_ss, g_rs, local, piece):
    me = Place(dp, tn)
    cols = wq.shape[1]
    n = gather_count(dp)
    lanes = []
    for k, (src, dst, lo) in enumerate(((wq, wqkv, 0), (wk, wqkv, cols), (wv, wqkv, 2 * cols), (wo, wout, 0))):
        lanes.append(gather_lane(me, src, pl.ds(0, cols), dst, pl.ds(lo, cols), k % 2 == 1,
                                 Sub(g_ss, k * n), Sub(g_rs, k * n), local.at[k]))
    fill_piece(piece, bq, bv, bi, taps)
    greet(me)
    for s in (0, 1):
        for lane in lanes[2 * s : 2 * s + 2]:
            lane[0]()
    moved = to_owner(me, tok, rows, r_ss, r_rs, local.at[4])
    start_all(moved)
    side = [remote(piece, small.at[me.t], r_ss.at[0], r_rs.at[0], (me.i, 1 - me.t)),
            pltpu.make_async_copy(piece, small.at[me.t], local.at[5])]
    start_all(side)
    for pair, stage in ((0, 1), (0, 2), (1, 1), (0, 3), (1, 2), (1, 3), (0, 4), (1, 4)):
        for lane in lanes[2 * pair : 2 * pair + 2]:
            lane[stage]()
    wait_all(side)
    wait_all(moved)


def call_bring(dp, tn, tok, wq, wk, wv, wo, bq, bv, bi, taps):
    s = jax.ShapeDtypeStruct
    depth, cols = wq.shape
    lead = (tn, dp // 4, 2, 2, depth)
    outs = (s((dp,) + tok.shape[1:], BF), s(lead + (3 * cols,), BF), s(lead + (cols,), BF), s((tn, SMALL_ROWS, 128), F32))
    return pl.pallas_call(
        functools.partial(bring, dp, tn),
        out_shape=outs,
        in_specs=[ANY] * 5 + [VM] * 4,
        out_specs=(ANY, ANY, ANY, ANY),
        scratch_shapes=sems(dp) + sems(4 * gather_count(dp)) + [DMA((6,)), pltpu.VMEM((SMALL_ROWS, 128), F32)],
        compiler_params=params(0, TOP),
        name="bring",
    )(tok, wq, wk, wv, wo, bq, bv, bi, taps)


def carry_home(dp, tn, g_rows, dwqkv, vec, bsum, vecs, gtap, g_home, gq, gk, gv, gbq, gbv, gtaps, gbi, *refs):
    n_outs, (r_ss, r_rs, v_ss, v_rs, g_ss, g_rs, local, norms, rest, nbuf, rbuf, nall, rall, nsum, rsum) = refs[:6], refs[6:21]
    bufs = refs[21:]
    me = Place(dp, tn)
    greet(me)
    c = Carry(me, g_rows, dwqkv, vec, bsum, vecs, gtap, g_home, gq, gk, gv, gbq, gbv, gtaps, gbi, n_outs, r_ss, r_rs, v_ss, v_rs,
              g_ss, g_rs, local, norms, rest, nbuf, rbuf, nall, rall, nsum, rsum, bufs)
    c.send_rows()
    c.send_grads()
    c.pack()
    c.finish([])


class Carry:
    def __init__(self, me, g_rows, dwqkv, vec, bsum, vecs, gtap, g_home, gq, gk, gv, gbq, gbv, gtaps, gbi, n_outs, r_ss, r_rs,
                 v_ss, v_rs, g_ss, g_rs, local, norms, rest, nbuf, rbuf, nall, rall, nsum, rsum, bufs):
        self.me, self.sources = me, (vec, bsum, vecs, gtap)
        self.results = (gbq, gbv, gtaps, gbi, n_outs)
        self.v = (v_ss, v_rs, norms, rest, nbuf, rbuf, nall, rall, nsum, rsum)
        self.cols = cols = gq.shape[1]
        dp, n = me.dp, reduce_count(me.dp)
        self.lanes = []
        for k, dst in enumerate((gq, gk, gv)):
            self.lanes.append(reduce_lane(me, dwqkv, k * cols, cols, bufs[5 * k : 5 * k + 5], Sub(g_ss, k * n),
                                          Sub(g_rs, k * n), local.at[1 + k], [(dst, 0, 0, cols)]))
        mine = me.t * dp
        self.partner = partner = (me.i, 1 - me.t)
        self.first = []
        for k in range(1, dp):
            j = lax.rem(me.i + k, dp)
            self.first.append(remote(g_rows.at[j], g_home.at[mine + me.i], r_ss.at[k], r_rs.at[k], (j, me.t)))
        self.own = pltpu.make_async_copy(g_rows.at[me.i], g_home.at[mine + me.i], local.at[0])
        self.second = [remote(g_rows.at[me.i], g_home.at[mine + me.i], r_ss.at[dp], r_rs.at[dp], partner)]
        for k in range(1, dp):
            j = mine + lax.rem(me.i + dp - k, dp)
            self.second.append(remote(g_home.at[j], g_home.at[j], r_ss.at[dp + k], r_rs.at[dp + k], partner))

    def send_rows(self):
        start_all(self.first)
        self.own.start()
        self.second[0].start()

    def send_grads(self):
        for lane in self.lanes:
            lane[0]()

    def pack(self):
        me = self.me
        dp, tn, cols = me.dp, me.tn, self.cols
        vec, bsum, vecs, gtap = self.sources
        gbq, gbv, gtaps, gbi, n_outs = self.results
        v_ss, v_rs, norms, rest, nbuf, rbuf, nall, rall, nsum, rsum = self.v
        share = n_outs[0].shape[0]
        six = jnp.sum(vec[...], axis=1)
        norms[...] = jnp.zeros_like(norms)
        rest[...] = jnp.zeros_like(rest)
        for j in range(dp):
            norms[j, 0:6, :share] = six[:, j * share : (j + 1) * share]
        units = jnp.sum(bsum[...], axis=0, keepdims=True)
        per, taps = gtaps.shape
        for t in range(tn):
            for line, first_row, size in ((vecs[0:1, :], ROWS_BQ, cols), (vecs[1:2, :], ROWS_BV, cols),
                                          (units, ROWS_BI, gbi.shape[0])):
                for r in range(size // 128):
                    lo = t * size + r * 128
                    rest[t, first_row + r : first_row + r + 1, :] = line[:, lo : lo + 128]
            rest[t, ROWS_TAPS : ROWS_TAPS + per, :taps] = gtap[t * per : (t + 1) * per, FLIP_AT : FLIP_AT + taps]
        self.v1 = [remote(norms, nbuf, v_ss.at[0], v_rs.at[0], self.partner),
                   remote(rest.at[1 - me.t], rbuf, v_ss.at[1], v_rs.at[1], self.partner)]
        start_all(self.v1)

    def finish(self, others):
        me = self.me
        dp = me.dp
        gbq, gbv, gtaps, gbi, n_outs = self.results
        v_ss, v_rs, norms, rest, nbuf, rbuf, nall, rall, nsum, rsum = self.v
        for lane in self.lanes:
            lane[1]()
        wait_all(self.v1)
        nsum[...] = norms[...] + nbuf[...]
        rsum[...] = rest[me.t] + rbuf[...]
        v2 = []
        for k in range(1, dp):
            j = lax.rem(me.i + k, dp)
            v2.append(remote(nsum.at[j], nall.at[k], v_ss.at[2 * k], v_rs.at[2 * k], (j, me.t)))
            v2.append(remote(rsum, rall.at[k], v_ss.at[2 * k + 1], v_rs.at[2 * k + 1], (j, me.t)))
        start_all(v2)
        stages = list(others) + [lane[s] for s in (2, 3) for lane in self.lanes]
        todo = list(zip(self.first, self.second[1:]))
        for k, (a, b) in enumerate(todo):
            left = len(todo) - k
            for _ in range(-(-len(stages) // left) if k > 0 else 0):
                stages.pop(0)()
            a.wait()
            b.start()
        for st in stages:
            st()
        wait_all(v2)
        ntot = nsum[me.i]
        rtot = rsum[...]
        for k in range(1, dp):
            ntot = ntot + nall[k]
            rtot = rtot + rall[k]
        share = n_outs[0].shape[0]
        per, taps = gtaps.shape
        for k in range(6):
            n_outs[k][...] = ntot[k, :share]
        for ref, first_row in ((gbq, ROWS_BQ), (gbv, ROWS_BV), (gbi, ROWS_BI)):
            size = ref.shape[0]
            ref[...] = jnp.concatenate(
                [rtot[first_row + r : first_row + r + 1] for r in range(size // 128)], axis=1).reshape(size)
        gtaps[...] = rtot[ROWS_TAPS : ROWS_TAPS + per, :taps]
        for lane in self.lanes:
            lane[4]()
        self.own.wait()
        wait_all(self.second)


def carry_scratch(dp, tn, depth, cols):
    norms, rest = (dp, 8, 128), (tn, 24, 128)
    scratch = sems(2 * dp) + sems(2 * dp) + sems(3 * reduce_count(dp)) + [DMA((4,))]
    scratch += [pltpu.VMEM(norms, F32), pltpu.VMEM(rest, F32),
                pltpu.VMEM(norms, F32), pltpu.VMEM(rest[1:], F32),
                pltpu.VMEM((dp,) + norms[1:], F32), pltpu.VMEM((dp,) + rest[1:], F32),
                pltpu.VMEM(norms, F32), pltpu.VMEM(rest[1:], F32)]
    for _ in range(3):
        scratch += reduce_bufs(dp, tn, depth, cols)
    return scratch


def call_carry_home(dp, tn, g_rows, dwqkv, vec, bsum, vecs, gtap, taps):
    s = jax.ShapeDtypeStruct
    r, w = g_rows.shape[1:]
    depth, cols = dwqkv.shape[4], dwqkv.shape[5] // 3
    share = s((depth, cols), F32)
    outs = (s((tn * dp, r, w), BF), share, share, share, s((cols,), F32), s((cols,), F32), s(taps.shape, F32),
            s((bsum.shape[1] // tn,), F32)) + (s((depth,), F32),) * 6
    scratch = carry_scratch(dp, tn, depth, cols)
    return pl.pallas_call(
        functools.partial(carry_home, dp, tn),
        out_shape=outs,
        in_specs=[ANY, ANY] + [VM] * 4,
        out_specs=(ANY,) + (VM,) * 13,
        scratch_shapes=scratch,
        compiler_params=params(4, TOP),
        name="carry_home",
    )(g_rows, dwqkv, vec, bsum, vecs, gtap)


F32 = jnp.float32
BF = jnp.bfloat16
LAND = 64
ITERS = 6
HEADS_HERE = 6
ROWS_BQ, ROWS_BV, ROWS_BI, ROWS_TAPS = 0, 3, 6, 18
EDGE = 112
TAPS = 33
FLIP_AT = 367


def nn(a, b):
    return lax.dot_general(a, b, (((1,), (0,)), ((), ())), preferred_element_type=F32)


def nt(a, b):
    return lax.dot_general(a, b, (((1,), (1,)), ((), ())), preferred_element_type=F32)


def turn(a):
    return jnp.transpose(a, (1, 0))


def same_head(rows, columns):
    left = lax.broadcasted_iota(jnp.int32, (rows, columns), 0) // LAND
    right = lax.broadcasted_iota(jnp.int32, (rows, columns), 1) // LAND
    return left == right


def spread(small):
    n = small.shape[1] // LAND
    tall = jnp.concatenate([small] * n, axis=0)
    return jnp.where(same_head(n * LAND, n * LAND), tall, jnp.zeros_like(tall))


def gather_diag(full):
    n = full.shape[1] // LAND
    lane = lax.broadcasted_iota(jnp.int32, (LAND, full.shape[1]), 1) // LAND
    out = full[:LAND]
    for h in range(1, n):
        out = jnp.where(lane == h, full[h * LAND : (h + 1) * LAND], out)
    return out


def halves(a):
    high = a.astype(BF)
    return high, (a - high.astype(F32)).astype(BF)


def pair_nn(a, b):
    ah, al = halves(a)
    bh, bl = halves(b)
    bh, bl = spread(bh), spread(bl)
    wide = jnp.concatenate([bh, bl], axis=1)
    r = nn(jnp.concatenate([ah, al], axis=1), jnp.concatenate([wide, wide], axis=0))
    return r[:, : 2 * LAND] + r[:, 2 * LAND :]


def pair_nt(a, b):
    ah, al = halves(a)
    bh, bl = halves(b)
    bh, bl = spread(bh), spread(bl)
    tall = jnp.concatenate([bh, bl], axis=0)
    r = nt(jnp.concatenate([ah, al], axis=1), jnp.concatenate([tall, tall], axis=1))
    return r[:, : 2 * LAND] + r[:, 2 * LAND :]


def pair_turn(a):
    t = turn(a)
    return jnp.concatenate([t[:LAND], t[LAND:]], axis=1)


def pair_sum(a):
    left = lax.broadcasted_iota(jnp.int32, a.shape, 1) < LAND
    low = jnp.sum(jnp.where(left, a, 0.0), axis=1, keepdims=True)
    high = jnp.sum(jnp.where(left, 0.0, a), axis=1, keepdims=True)
    return jnp.where(left, low, high)


def pair_softmax(a):
    left = lax.broadcasted_iota(jnp.int32, a.shape, 1) < LAND
    low = jnp.max(jnp.where(left, a, -1e30), axis=1, keepdims=True)
    high = jnp.max(jnp.where(left, -1e30, a), axis=1, keepdims=True)
    e = jnp.exp(a - jnp.where(left, low, high))
    return e / pair_sum(e)


def pair_eye():
    r = lax.broadcasted_iota(jnp.int32, (LAND, 2 * LAND), 0)
    c = lax.broadcasted_iota(jnp.int32, (LAND, 2 * LAND), 1) % LAND
    return jnp.where(r == c, 1.0, 0.0).astype(F32)


def toeplitz(row, size, width):
    return pltpu.roll(jnp.broadcast_to(row, (size, width)), 0, 1, stride=1, stride_axis=0)


def blocks_of(ref, lower, block):
    length = ref.shape[1] - 256
    return jnp.concatenate(
        [ref[lower : lower + LAND, at : at + block + 256] for at in range(0, length, block)], axis=0
    )


def unblock(stacked, block):
    n = stacked.shape[0] // LAND
    return jnp.concatenate([stacked[i * LAND : (i + 1) * LAND] for i in range(n)], axis=1)


def own_sequence():
    return lax.axis_index("tensor") * lax.axis_size("dp") + lax.axis_index("dp")


def side_row(small_ref, t, first, count):
    return jnp.concatenate([small_ref[t, r : r + 1, :] for r in range(first, first + count)], axis=1)


def band_of(rows, head):
    h = head % HEADS_HERE
    row = jnp.concatenate([rows[head // HEADS_HERE][h : h + 1, :], jnp.zeros((1, 384), F32)], axis=1)
    return toeplitz(pltpu.roll(row, EDGE, 1), 256, 512).astype(BF)


def tap_rows(small_ref, t):
    return small_ref[t, ROWS_TAPS : ROWS_TAPS + 8, :]


def reversed_taps(rows):
    turned = jnp.where(
        lax.broadcasted_iota(jnp.int32, (128, 128), 0) + lax.broadcasted_iota(jnp.int32, (128, 128), 1) == TAPS - 1, 1.0, 0.0
    ).astype(BF)
    return nn(rows.astype(BF), turned)


def forward_core(rows_of, weight_of, tn, small_ref, ids_ref, q_ref, k_ref, v_ref, near_ref, far_ref, ctx_ref,
                 lq_ref, lk_ref, mix_ref, sum_ref, ker_ref, z_ref, a_ref, v2_ref, w2_ref, pad_ref, tick, ready, writes):
    length, width = q_ref.shape
    cols = width // tn
    scale = LAND ** -0.25
    rows_at = 256
    pairs = width // 128
    groups = width // 256
    q_w, k_w, v_w, near_w, far_w, ctx_w, z_w, a_w, v2_w, w2_w = writes
    ready()
    bq = [side_row(small_ref, t, ROWS_BQ, 3) for t in range(tn)]
    bv = [side_row(small_ref, t, ROWS_BV, 3) for t in range(tn)]

    def project(i, carry):
        at = pl.ds(pl.multiple_of(i * rows_at, rows_at), rows_at)
        for t in range(tn):
            out = nn(rows_of(at, i), weight_of(t))
            own = slice(t * cols, (t + 1) * cols)
            q_ref[at, own] = ((out[:, :cols] + bq[t]) * scale).astype(BF)
            k_ref[at, own] = (out[:, cols : 2 * cols] * scale).astype(BF)
            v_ref[at, own] = (out[:, 2 * cols :] + bv[t]).astype(BF)
        return carry

    lax.fori_loop(0, length // rows_at, project, 0)
    start_all([q_w, k_w, v_w])
    tick()

    ids = ids_ref[pl.ds(own_sequence(), 1), :]
    member = jnp.where(lax.broadcasted_iota(jnp.int32, (LAND, length), 0) == ids, 1.0, 0.0).astype(F32)
    count = jnp.sum(member, axis=1, keepdims=True)
    member = member.astype(BF)
    valid = ids < LAND
    lq_ref[...] = (nn(member, q_ref[...]) / count).astype(BF)
    lk_ref[...] = (nn(member, k_ref[...]) / count).astype(BF)

    eye = pair_eye()
    for p in range(pairs):
        own = slice(p * 128, (p + 1) * 128)
        scores = nt(lq_ref[:, own], spread(lk_ref[:, own]))
        kernel = pair_softmax(scores)
        ker_ref[:, own] = kernel
        left = lax.broadcasted_iota(jnp.int32, kernel.shape, 1) < LAND
        total = jnp.sum(pair_sum(kernel * kernel), axis=0, keepdims=True)
        z_ref[0, :, own] = pair_turn(kernel) / total
    tick()

    for g in range(groups):
        own = slice(g * 256, (g + 1) * 256)
        scores = nt(spread(lk_ref[:, own]), q_ref[:, own]).reshape(4, LAND, length)
        scores = jnp.exp(scores - jnp.max(scores, axis=1, keepdims=True))
        scores = scores / jnp.sum(scores, axis=1, keepdims=True)
        near_ref[own, :] = scores.reshape(256, length).astype(BF)
        scores = nt(spread(lq_ref[:, own]), k_ref[:, own])
        scores = jnp.where(valid, scores, -1e30)
        scores = jnp.exp(scores - jnp.max(scores, axis=1, keepdims=True))
        scores = scores / jnp.sum(scores, axis=1, keepdims=True)
        far_ref[own, :] = scores.astype(BF)
        sum_ref[:, own] = gather_diag(nn(far_ref[own, :], v_ref[:, own]))
        tick()
    start_all([near_w, far_w])

    def iterate(n, carry):
        for p in range(pairs):
            own = slice(p * 128, (p + 1) * 128)
            z = z_ref[n, :, own]
            a = pair_nn(ker_ref[:, own], z)
            v2 = 15.0 * eye - pair_nn(a, 7.0 * eye - a)
            w2 = 13.0 * eye - pair_nn(a, v2)
            a_ref[n, :, own] = a
            v2_ref[n, :, own] = v2
            w2_ref[n, :, own] = w2
            z_ref[n + 1, :, own] = 0.25 * pair_nn(z, w2)
        return carry

    lax.fori_loop(0, ITERS // 2, iterate, 0)
    tick()
    lax.fori_loop(ITERS // 2, ITERS, iterate, 0)
    start_all([z_w, a_w, v2_w, w2_w])
    tick()

    for p in range(pairs):
        own = slice(p * 128, (p + 1) * 128)
        mix_ref[:, own] = pair_nn(z_ref[ITERS, :, own], sum_ref[:, own]).astype(BF)

    pad_ref[...] = jnp.zeros_like(pad_ref)
    taps = [tap_rows(small_ref, t) for t in range(tn)]
    for g in range(groups):
        own = slice(g * 256, (g + 1) * 256)
        att = nn(turn(spread(mix_ref[:, own])), near_ref[own, :])
        vt = turn(v_ref[:, own])
        pad_ref[:, 128 : 128 + length] = jnp.where(valid, vt, jnp.zeros_like(vt))
        parts = []
        for h in range(4):
            band = band_of(taps, 4 * g + h)
            parts.append(unblock(nt(blocks_of(pad_ref, h * LAND, 256), band), 256))
        att = (att + jnp.concatenate(parts, axis=0)).astype(BF)
        ctx_ref[:, own] = turn(att)
        tick()


def attend_forward(dp, x_in, w_in, small_ref, ids_ref, wi_ref, wf_ref, cot_ref,
                   q_out, k_out, v_out, near_out, far_out, ctx_out, lq_ref, lk_ref, mix_ref, sum_ref, ker_ref,
                   z_out, a_out, v2_out, w2_out, wi_all, wf_all, cota_ref, pad_ref, x_ref, w_ref, q_ref, k_ref, v_ref,
                   near_ref, far_ref, ctx_ref, z_ref, a_ref, v2_ref, w2_ref, g_ss, g_rs, c_ss, c_rs, local, move):
    length, width = x_ref.shape
    tn = w_ref.shape[0]
    loads = [Fetch(x_in, x_ref, move.at[0]).start(), Fetch(w_in, w_ref, move.at[1]).start()]
    writes = [
        Fetch(a, b, move.at[2 + k]) for k, (a, b) in enumerate((
            (q_ref, q_out), (k_ref, k_out), (v_ref, v_out), (near_ref, near_out), (far_ref, far_out), (ctx_ref, ctx_out),
            (z_ref, z_out), (a_ref, a_out), (v2_ref, v2_out), (w2_ref, w2_out)))]
    me = Place(dp, tn)
    n = gather_count(dp)
    half = wi_ref.shape[1] // 2
    lanes = []
    for p, (src, dst) in enumerate(((wi_ref, wi_all), (wf_ref, wf_all))):
        for h in range(2):
            own, k = pl.ds(h * half, half), 2 * p + h
            lanes.append(gather_lane(me, src, own, dst, own, h == 1, Sub(g_ss, k * n), Sub(g_rs, k * n), local.at[k]))

    def stage(pair, s):
        def run():
            for lane in lanes[2 * pair : 2 * pair + 2]:
                lane[s]()
        return run

    greet(me)
    stage(0, 0)()
    stage(1, 0)()
    arriving = []
    for k in range(1, early_blocks(dp) + 1):
        j = lax.rem(me.i + k, dp)
        arriving.append(remote(cot_ref.at[me.t * dp + j], cota_ref.at[me.i], c_ss.at[k], c_rs.at[k], (j, me.t)))
    start_all(arriving)
    tick = Ticks([stage(0, 1), stage(0, 2), stage(1, 1), stage(0, 3), stage(1, 2), stage(1, 3), stage(0, 4), stage(1, 4)])
    forward_core(lambda at, i: x_ref[at, :], lambda t: w_ref[t], tn, small_ref, ids_ref, q_ref, k_ref, v_ref, near_ref,
                 far_ref, ctx_ref, lq_ref, lk_ref, mix_ref, sum_ref, ker_ref, z_ref, a_ref, v2_ref, w2_ref, pad_ref,
                 tick, lambda: wait_all(loads), writes)
    writes[5].start()
    tick.rest()
    wait_all(arriving)
    wait_all(writes)


def begin(dp, tn, tok, wq, wk, wv, wo, bq, bv, bi, taps, ids_ref, wi_ref, wf_ref, cot_ref,
          rows_out, wqkv_out, wout, small_out, q_out, k_out, v_out, near_out, far_out, ctx_out,
          lq_ref, lk_ref, mix_ref, sum_ref, ker_ref, z_out, a_out, v2_out, w2_out, wi_all, wf_all, cota_ref,
          x_ref, w_ref, small_ref, piece, pad_ref, q_ref, k_ref, v_ref, near_ref, far_ref, ctx_ref, z_ref, a_ref, v2_ref, w2_ref,
          r_ss, r_rs, p_ss, p_rs, g_ss, g_rs, c_ss, c_rs, local, move):
    me = Place(dp, tn)
    cols = wq.shape[1]
    n = gather_count(dp)
    first = []
    for k, (src, dst, lo) in enumerate(((wq, w_ref, 0), (wk, w_ref, cols), (wv, w_ref, 2 * cols), (wo, wout, 0))):
        first.append(gather_lane(me, src, pl.ds(0, cols), dst, pl.ds(lo, cols), k % 2 == 1,
                                 Sub(p_ss, k * n), Sub(p_rs, k * n), local.at[k]))
    lanes = []
    parts = wi_ref.shape[1] // FORWARD_CUT
    for p, (src, dst) in enumerate(((wi_ref, wi_all), (wf_ref, wf_all))):
        for h in range(parts):
            own, k = pl.ds(h * FORWARD_CUT, FORWARD_CUT), parts * p + h
            lanes.append(gather_lane(me, src, own, dst, own, h % 2 == 1, Sub(g_ss, k * n), Sub(g_rs, k * n), local.at[6 + k]))

    def stage(pair, s):
        def run():
            for lane in lanes[2 * pair : 2 * pair + 2]:
                lane[s]()
        return run

    fill_piece(piece, bq, bv, bi, taps)
    greet(me)
    for lane in first:
        lane[0]()
    moved = to_owner(me, tok, x_ref, r_ss, r_rs, local.at[4])
    start_all(moved)
    side = [remote(piece, small_ref.at[me.t], r_ss.at[0], r_rs.at[0], (me.i, 1 - me.t)),
            pltpu.make_async_copy(piece, small_ref.at[me.t], local.at[5])]
    start_all(side)
    arriving = []
    for k in range(1, early_blocks(dp) + 1):
        j = lax.rem(me.i + k, dp)
        arriving.append(remote(cot_ref.at[me.t * dp + j], cota_ref.at[me.i], c_ss.at[k], c_rs.at[k], (j, me.t)))
    pairs = len(lanes) // 2
    for pair, st in ((0, 1), (0, 2), (1, 1), (1, 2)):
        for lane in first[2 * pair : 2 * pair + 2]:
            lane[st]()
    for pair in range(FORWARD_EARLY):
        stage(pair, 0)()
    for lane in first:
        lane[3]()
    for pair in range(FORWARD_EARLY):
        stage(pair, 1)()
        stage(pair + FORWARD_EARLY, 0)()
        stage(pair, 2)()
    for lane in first:
        lane[4]()
    wait_all(side)
    wait_all(moved)
    rolled = 2 * FORWARD_EARLY
    while rolled < FORWARD_EARLY + FORWARD_AHEAD:
        stage(rolled, 0)()
        rolled += 1
    keep = [Fetch(x_ref, rows_out, move.at[0]).start(), Fetch(w_ref, wqkv_out, move.at[1]).start(),
            Fetch(small_ref, small_out, move.at[12]).start()]
    writes = [
        Fetch(a, b, move.at[2 + k]) for k, (a, b) in enumerate((
            (q_ref, q_out), (k_ref, k_out), (v_ref, v_out), (near_ref, near_out), (far_ref, far_out), (ctx_ref, ctx_out),
            (z_ref, z_out), (a_ref, a_out), (v2_ref, v2_out), (w2_ref, w2_out)))]
    todo = []
    for pair in range(FORWARD_EARLY, pairs):
        steps = [stage(pair, 1)]
        if rolled < pairs:
            steps.append(stage(rolled, 0))
            rolled += 1
        if rolled == pairs:
            steps.append(lambda: start_all(arriving))
            rolled += 1
        todo += [together(steps), stage(pair, 2)]
    todo += [stage(pair, 3) for pair in range(pairs)] + [stage(pair, 4) for pair in range(pairs)]
    tick = Ticks(todo)
    width = q_ref.shape[1]
    part = x_ref.shape[1]
    per = 256 // part
    forward_core(lambda at, i: x_ref[pl.ds(i * per, per)].reshape(256, width), lambda t: w_ref[t].reshape(width, 3 * cols),
                 tn, small_ref, ids_ref, q_ref, k_ref, v_ref, near_ref, far_ref, ctx_ref, lq_ref, lk_ref, mix_ref, sum_ref,
                 ker_ref, z_ref, a_ref, v2_ref, w2_ref, pad_ref, tick, lambda: None, writes)
    writes[5].start()
    tick.rest()
    wait_all(arriving)
    wait_all(writes)
    wait_all(keep)


FORWARD_CUT = 384
FORWARD_EARLY = 1
FORWARD_AHEAD = 2


def call_begin(dp, tn, tok, wq, wk, wv, wo, bq, bv, bi, taps, ids, wi, wf, cot):
    s = jax.ShapeDtypeStruct
    vm = pltpu.VMEM
    depth, cols = wq.shape
    units = wi.shape[1]
    part, width = tok.shape[1:]
    length = dp * part
    lead = (tn, dp // 4, 2, 2, depth)
    big, tall = s((length, width), BF), s((width, length), BF)
    low, wide = s((LAND, width), BF), s((LAND, width), F32)
    steps, steps1 = s((ITERS, LAND, width), F32), s((ITERS + 1, LAND, width), F32)
    whole = s(lead + (units,), BF)
    blocks = s((dp, part, width), BF)
    small = s((tn, SMALL_ROWS, 128), F32)
    wqkv = s(lead + (3 * cols,), BF)
    outs = (blocks, wqkv, s(lead + (cols,), BF), small,
            big, big, big, tall, tall, big, low, low, low, wide, wide, steps1, steps, steps, steps, whole, whole, blocks)
    n_lanes = 2 * (units // FORWARD_CUT)
    return pl.pallas_call(
        functools.partial(begin, dp, tn),
        out_shape=outs,
        in_specs=[ANY] * 5 + [VM] * 5 + [ANY] * 3,
        out_specs=tuple([ANY] * 10 + [VM] * 5 + [ANY] * 7),
        scratch_shapes=[vm(o.shape, o.dtype) for o in (blocks, wqkv, small)]
        + [vm((SMALL_ROWS, 128), F32), vm((256, length + 256), BF)]
        + [vm(o.shape, o.dtype) for o in outs[4:10] + outs[15:19]]
        + sems(dp) + sems(4 * gather_count(dp)) + sems(n_lanes * gather_count(dp)) + sems(dp)
        + [DMA((6 + n_lanes,)), DMA((13,))],
        compiler_params=params(5, TOP),
        name="begin",
    )(tok, wq, wk, wv, wo, bq, bv, bi, taps, ids, wi, wf, cot)


def early_blocks(dp):
    return dp // 2


def call_attend_forward(dp, x, w, small, ids, wi, wf, cot):
    length, width = x.shape
    s = jax.ShapeDtypeStruct
    big = s((length, width), BF)
    tall = s((width, length), BF)
    low = s((LAND, width), BF)
    wide = s((LAND, width), F32)
    steps = s((ITERS, LAND, width), F32)
    tn = w.shape[0]
    depth, units = wi.shape
    whole = s((tn, dp // 4, 2, 2, depth, units), BF)
    outs = (big, big, big, tall, tall, big, low, low, low, wide, wide, s((ITERS + 1, LAND, width), F32), steps, steps, steps,
            whole, whole, s((dp,) + cot.shape[1:], BF))
    vm = pltpu.VMEM
    return pl.pallas_call(
        functools.partial(attend_forward, dp),
        out_shape=outs,
        in_specs=[ANY] * 2 + [VM] * 2 + [ANY] * 3,
        out_specs=tuple([ANY] * 6 + [VM] * 5 + [ANY] * 7),
        scratch_shapes=[vm((256, length + 256), BF)] + [vm(o.shape, o.dtype) for o in (x, w) + outs[:6] + outs[11:15]]
        + sems(4 * gather_count(dp)) + sems(dp) + [DMA((4,)), DMA((12,))],
        compiler_params=params(1, TOP),
        name="attend_forward",
    )(x, w, small, ids, wi, wf, cot)


ROOT_HALF = 0.7071067811865476
P_ERF = 0.3275911
C_ERF = (0.254829592, -0.284496736, 1.421413741, -1.453152027, 1.061405429)


def gelu_both(u):
    x = jnp.abs(u) * ROOT_HALF
    e = jnp.exp(-0.5 * u * u)
    t = 1.0 / (1.0 + P_ERF * x)
    poly = C_ERF[4]
    for c in (C_ERF[3], C_ERF[2], C_ERF[1], C_ERF[0]):
        poly = poly * t + c
    tail = 0.5 * poly * t * e
    phi = jnp.where(u < 0.0, tail, 1.0 - tail)
    return u * phi, phi + u * e * 0.3989422804014327


def norm_parts(r):
    n = r.shape[1]
    center = r - jnp.sum(r, axis=1, keepdims=True) * (1.0 / n)
    spread_ = jnp.sum(center * center, axis=1, keepdims=True) * (1.0 / n)
    rstd = lax.rsqrt(spread_ + 1e-05)
    return center * rstd, rstd


def norm_back(e, normed, rstd):
    n = e.shape[1]
    mean_e = jnp.sum(e, axis=1, keepdims=True) * (1.0 / n)
    mean_en = jnp.sum(e * normed, axis=1, keepdims=True) * (1.0 / n)
    return rstd * (e - mean_e - normed * mean_en)


def fold(a):
    return jnp.sum(a.reshape(a.shape[0] // 8, 8, a.shape[1]), axis=0)


def feed(dp, x_in, ctx_in, wo_in, wi_in, wf_in, bo_in, g1_in, s1_in, bf_in, g2_in, s2_in, small_ref, cot_ref, cota_ref,
         gr1_out, dc_out, dwo_out, dwi_out, dwf_out, vec_ref, bsum_ref, home_ref,
         act_ref, gi_ref, hid_ref, gr2_ref, turn_ref, n1_ref, n2_ref, rs1_ref, rs2_ref, out_ref, cots_ref,
         x_ref, ctx_ref, wo_ref, wi_ref, wf_ref, gr1_ref, dc_ref, dwo_ref, dwi_ref, dwf_ref,
         c_ss, c_rs, h_ss, h_rs, f_ss, f_rs, local, move):
    length, width = x_ref.shape
    tn = wo_ref.shape[0]
    cols = width // tn
    units = wi_ref.shape[2]
    size = 256
    chunk = 512
    part = length // dp
    per = size // part
    me = Place(dp, tn)
    x_l, ctx_l, wo_l, wi_l, wf_l = loads = [
        Fetch(a, b, move.at[k]).start() for k, (a, b) in enumerate((
            (x_in, x_ref), (ctx_in, ctx_ref), (wo_in, wo_ref), (wi_in, wi_ref), (wf_in, wf_ref)))]
    greet(me)
    mine = me.t * dp
    early = early_blocks(dp)
    arriving = [pltpu.make_async_copy(cot_ref.at[mine + me.i], cots_ref.at[me.i], local.at[0])]
    leaving, passing = [], []
    partner = (me.i, 1 - me.t)
    for k in range(1, dp):
        j, back = lax.rem(me.i + k, dp), lax.rem(me.i + dp - k, dp)
        if k <= early:
            arriving.append(pltpu.make_async_copy(cota_ref.at[back], cots_ref.at[back], c_ss.at[k]))
        else:
            arriving.append(remote(cot_ref.at[mine + j], cots_ref.at[me.i], c_ss.at[k], c_rs.at[k], (j, me.t)))
        leaving.append(remote(out_ref.at[j], home_ref.at[mine + me.i], h_ss.at[k], h_rs.at[k], (j, me.t)))
        if k < late_blocks(dp):
            passing.append(remote(home_ref.at[mine + back], home_ref.at[mine + back], f_ss.at[k], f_rs.at[k], partner))
    kept = pltpu.make_async_copy(out_ref.at[me.i], home_ref.at[mine + me.i], local.at[1])
    across = remote(out_ref.at[me.i], home_ref.at[mine + me.i], f_ss.at[0], f_rs.at[0], partner)
    start_all(arriving)
    bo, g1, s1, bf, g2, s2 = [
        r[...].astype(F32).reshape(1, width) for r in (bo_in, g1_in, s1_in, bf_in, g2_in, s2_in)]
    bi = [side_row(small_ref, t, ROWS_BI, units // 128) for t in range(tn)]
    vec_ref[...] = jnp.zeros_like(vec_ref)
    bsum_ref[...] = jnp.zeros_like(bsum_ref)

    def rows_at(i):
        return pl.ds(pl.multiple_of(i * size, size), size)

    def forward(i, carry):
        at = rows_at(i)
        attn = bo + x_ref[at, :].astype(F32)
        for t in range(tn):
            attn = attn + nt(ctx_ref[at, t * cols : (t + 1) * cols], wo_ref[t])
        n1, rstd1 = norm_parts(attn)
        n1_ref[at, :] = n1
        rs1_ref[at, :] = rstd1
        hidden = n1 * g1 + s1
        hid = hidden.astype(BF)
        hid_ref[at, :] = hid
        r2 = hidden + bf
        for t in range(tn):
            for c in range(0, units, chunk):
                own = slice(t * units + c, t * units + c + chunk)
                act, gp = gelu_both(nn(hid, wi_ref[t, :, c : c + chunk]) + bi[t][:, c : c + chunk])
                act_ref[at, own] = act.astype(BF)
                gi_ref[at, own] = gp.astype(BF)
        for t in range(tn):
            r2 = r2 + nt(act_ref[at, t * units : (t + 1) * units], wf_ref[t])
        n2, rstd2 = norm_parts(r2)
        n2_ref[at, :] = n2
        rs2_ref[at, :] = rstd2
        out_ref[pl.ds(i * per, per)] = (n2 * g2 + s2).reshape(per, part, width).astype(BF)
        return carry

    def backward(i, carry):
        at = rows_at(i)
        cot = cots_ref[pl.ds(i * per, per)].astype(F32).reshape(size, width)
        n2 = n2_ref[at, :]
        gr2 = norm_back(cot * g2, n2, rs2_ref[at, :])
        vec_ref[5] += fold(cot)
        vec_ref[4] += fold(cot * n2)
        vec_ref[3] += fold(gr2)
        low = gr2.astype(BF)
        gr2_ref[at, :] = low
        for t in range(tn):
            for c in range(0, units, chunk):
                own = slice(t * units + c, t * units + c + chunk)
                gi = nn(low, wf_ref[t, :, c : c + chunk]) * gi_ref[at, own].astype(F32)
                bsum_ref[:, own] += fold(gi)
                gi_ref[at, own] = gi.astype(BF)
        gh = gr2
        for t in range(tn):
            gh = gh + nt(gi_ref[at, t * units : (t + 1) * units], wi_ref[t])
        n1 = n1_ref[at, :]
        gr1 = norm_back(gh * g1, n1, rs1_ref[at, :])
        vec_ref[2] += fold(gh)
        vec_ref[1] += fold(gh * n1)
        vec_ref[0] += fold(gr1)
        low1 = gr1.astype(BF)
        gr1_ref[at, :] = low1
        for t in range(tn):
            dc_ref[at, t * cols : (t + 1) * cols] = nn(low1, wo_ref[t]).astype(BF)
        return carry

    wait_all(loads)
    lax.fori_loop(0, length // size, forward, 0)
    start_all(leaving)
    kept.start()
    across.start()
    wait_all(arriving)
    n_back = length // size
    done = 0
    for i in range(n_back):
        backward(i, 0)
        upto = len(passing) * (i + 1) // n_back
        for k in range(done, upto):
            leaving[k].wait()
            passing[k].start()
        done = upto

    outs = [Fetch(gr1_ref, gr1_out, move.at[5]).start(), Fetch(dc_ref, dc_out, move.at[6]).start()]
    turn_ref[...] = turn(gr2_ref[...])
    for t in range(tn):
        for c in range(0, units, chunk):
            own = slice(t * units + c, t * units + c + chunk)
            dwf_ref[t, :, c : c + chunk] = nn(turn_ref[...], act_ref[:, own]).astype(BF)
    outs.append(Fetch(dwf_ref, dwf_out, move.at[7]).start())
    turn_ref[...] = turn(hid_ref[...])
    for t in range(tn):
        for c in range(0, units, chunk):
            own = slice(t * units + c, t * units + c + chunk)
            dwi_ref[t, :, c : c + chunk] = nn(turn_ref[...], gi_ref[:, own]).astype(BF)
    outs.append(Fetch(dwi_ref, dwi_out, move.at[8]).start())
    turn_ref[...] = turn(gr1_ref[...])
    for t in range(tn):
        dwo_ref[t] = nn(turn_ref[...], ctx_ref[:, t * cols : (t + 1) * cols]).astype(BF)
    outs.append(Fetch(dwo_ref, dwo_out, move.at[9]).start())
    wait_all(leaving[done:])
    kept.wait()
    across.wait()
    wait_all(passing)
    wait_all(outs)


def late_blocks(dp):
    return dp // 2


def call_feed(dp, x, ctx, wo, wi, wf, vectors, small, cot, cota):
    length, width = x.shape
    tn, _, cols = wo.shape
    units = wi.shape[2]
    s = jax.ShapeDtypeStruct
    big = s((length, width), BF)
    blocks = (dp,) + cot.shape[1:]
    outs = (big, big, s((tn, width, cols), BF), s((tn, width, units), BF), s((tn, width, units), BF),
            s((6, 8, width), F32), s((8, tn * units), F32), s((tn * dp,) + blocks[1:], BF))
    vm = pltpu.VMEM
    return pl.pallas_call(
        functools.partial(feed, dp),
        out_shape=outs,
        in_specs=[ANY] * 5 + [VM] * 7 + [ANY] * 2,
        out_specs=tuple([ANY] * 5 + [VM] * 2 + [ANY]),
        scratch_shapes=[vm((length, tn * units), BF), vm((length, tn * units), BF), vm((length, width), BF),
                        vm((length, width), BF), vm((width, length), BF), vm((length, width), F32),
                        vm((length, width), F32), vm((length, 1), F32), vm((length, 1), F32), vm(blocks, BF),
                        vm(blocks, BF)] + [vm(o.shape, o.dtype) for o in (x, ctx, wo, wi, wf) + outs[:5]]
        + sems(dp) * 3 + [DMA((2,)), DMA((10,))],
        compiler_params=params(2, TOP),
        name="feed_forward",
    )(x, ctx, wo, wi, wf, *vectors, small, cot, cota)


NORTH_LANES = (1, 3, 5)
BACK_CUT = 384
BACK_LAG = 4
SIDE_FIRST = 4
BACK_TICKS = (4, 0, 0, 2, 2, 2, 2, 1)


def staggered(lanes, lag):
    steps = []
    for step in range(len(lanes) + 2 * lag):
        todo = []
        for stage in (3, 2, 1):
            k = step - (stage - 1) * lag
            if 0 <= k < len(lanes):
                todo.append(lanes[k][stage])
        steps.append(todo)
    return steps


def row_of(column):
    return turn(jnp.broadcast_to(column, (column.shape[0], 128)))[0:1, :]


def attend_backward(dp, ids_ref, small_ref, lq_ref, lk_ref, mix_ref, sum_ref, ker_ref,
                    x_in, w_in, q_in, k_in, v_in, near_in, far_in, z_in, a_in, v2_in, w2_in, dc_in, gr1_in,
                    dwo_in, dwi_in, dwf_in, home_in,
                    gtok_ref, dw_ref, vecs_ref, gtap_ref, go_ref, gi_ref, gf_ref, home_ref,
                    x_ref, w_ref, q_ref, k_ref, v_ref, near_ref, far_ref, z_ref, a_ref, v2_ref, w2_ref, dc_ref, gr1_ref,
                    pre_ref, glq_ref, glk_ref, gsum_ref, gz_ref, gk_ref, padv_ref, padc_ref, xt_ref,
                    g_ss, g_rs, y_ss, y_rs, local, move, *bufs, carry=None):
    near_l, dc_l, z_l, a_l, v2_l, w2_l, far_l, q_l, k_l, v_l, x_l, w_l, gr1_l = [
        Fetch(a, b, move.at[k]).start() for k, (a, b) in enumerate((
            (near_in, near_ref), (dc_in, dc_ref), (z_in, z_ref), (a_in, a_ref), (v2_in, v2_ref), (w2_in, w2_ref),
            (far_in, far_ref), (q_in, q_ref), (k_in, k_ref), (v_in, v_ref), (x_in, x_ref), (w_in, w_ref), (gr1_in, gr1_ref)))]
    length, width = x_ref.shape
    tn = w_ref.shape[0]
    cols = width // tn
    scale = LAND ** -0.25
    size = length // dp
    pairs = width // 128
    groups = width // 256
    me = Place(dp, tn)
    n = reduce_count(dp)
    plan = []
    for src, dst in ((dwf_in, gf_ref), (dwi_in, gi_ref), (dwo_in, go_ref)):
        plan += [(src, lo, BACK_CUT, dst) for lo in range(0, src.shape[5], BACK_CUT)]
    lanes = []
    for k, (src, lo, w, dst) in enumerate(plan):
        lanes.append(reduce_lane(me, src, lo, w, bufs[5 * k : 5 * k + 5], Sub(g_ss, k * n), Sub(g_rs, k * n), local.at[k],
                                 [(dst, lo, 0, w)], k in NORTH_LANES))
    sides = []
    for k in range(late_blocks(dp), dp):
        j = me.t * dp + lax.rem(me.i + dp - k, dp)
        sides.append(remote(home_ref.at[j], home_ref.at[j], y_ss.at[k], y_rs.at[k], (me.i, 1 - me.t)))
    greet(me, carry is not None)
    for lane in lanes:
        lane[0]()
    steps = staggered(lanes, BACK_LAG)
    for k, side in enumerate(sides):
        steps[min(SIDE_FIRST + k, len(steps) - 1)].append(side.start)
    tick = Ticks([together(step) for step in steps])
    ids = ids_ref[pl.ds(own_sequence(), 1), :]
    member = jnp.where(lax.broadcasted_iota(jnp.int32, (LAND, length), 0) == ids, 1.0, 0.0).astype(F32)
    count = jnp.sum(member, axis=1, keepdims=True)
    member = member.astype(BF)
    valid = ids < LAND
    eye = pair_eye()

    near_l.wait()
    dc_l.wait()
    for g in range(groups):
        own = slice(g * 256, (g + 1) * 256)
        gsum_ref[:, own] = gather_diag(nn(near_ref[own, :], dc_ref[:, own]))
    tick(BACK_TICKS[0])
    wait_all([z_l, a_l, v2_l, w2_l])
    for p in range(pairs):
        own = slice(p * 128, (p + 1) * 128)
        gmix = gsum_ref[:, own]
        gz_ref[:, own] = pair_nt(gmix, sum_ref[:, own])
        gsum_ref[:, own] = pair_nn(pair_turn(z_ref[ITERS, :, own]), gmix)

    tick(BACK_TICKS[1])
    gk_ref[...] = jnp.zeros_like(gk_ref)

    def iterate(m, carry):
        n = ITERS - 1 - m
        for p in range(pairs):
            own = slice(p * 128, (p + 1) * 128)
            grad = 0.25 * gz_ref[:, own]
            kernel = ker_ref[:, own]
            z = z_ref[n, :, own]
            a = a_ref[n, :, own]
            v2 = v2_ref[n, :, own]
            w2 = w2_ref[n, :, own]
            dw2 = pair_nn(pair_turn(z), grad)
            at = pair_turn(a)
            dv2 = -pair_nn(at, dw2)
            da = -pair_nt(dw2, v2) - pair_nt(dv2, 7.0 * eye - a) + pair_nn(at, dv2)
            gk_ref[:, own] += pair_nt(da, z)
            gz_ref[:, own] = pair_nt(grad, w2) + pair_nn(pair_turn(kernel), da)
        return carry

    lax.fori_loop(0, ITERS // 2, iterate, 0)
    tick(BACK_TICKS[2])
    lax.fori_loop(ITERS // 2, ITERS, iterate, 0)
    tick(BACK_TICKS[3])
    wait_all([far_l, q_l, k_l, v_l])

    for p in range(pairs):
        own = slice(p * 128, (p + 1) * 128)
        kernel = ker_ref[:, own]
        gz = gz_ref[:, own]
        total = jnp.sum(pair_sum(kernel * kernel), axis=0, keepdims=True)
        kt = pair_turn(kernel)
        back = jnp.sum(pair_sum(gz * kt), axis=0, keepdims=True)
        gk = gk_ref[:, own] + pair_turn(gz) / total - kernel * (2.0 * back / (total * total))
        mid = kernel * (gk - pair_sum(kernel * gk))
        glq_ref[:, own] = pair_nn(mid, lk_ref[:, own].astype(F32))
        glk_ref[:, own] = pair_nn(pair_turn(mid), lq_ref[:, own].astype(F32))

    flip = jnp.where(
        lax.broadcasted_iota(jnp.int32, (256, 256), 0) + lax.broadcasted_iota(jnp.int32, (256, 256), 1) == 255, 1.0, 0.0
    ).astype(BF)
    taps = [reversed_taps(tap_rows(small_ref, t)) for t in range(tn)]
    padv_ref[...] = jnp.zeros_like(padv_ref)
    padc_ref[...] = jnp.zeros_like(padc_ref)
    inner = slice(128, 128 + length)
    for g in range(groups):
        own = slice(g * 256, (g + 1) * 256)
        lk4 = spread(lk_ref[:, own])
        lq4 = spread(lq_ref[:, own])
        near = near_ref[own, :].astype(F32)
        gnear = nt(spread(mix_ref[:, own]), dc_ref[:, own])
        drop = jnp.sum((near * gnear).reshape(4, LAND, length), axis=1, keepdims=True)
        first = (near * (gnear.reshape(4, LAND, length) - drop).reshape(256, length)).astype(BF)
        glk_ref[:, own] += gather_diag(nn(first, q_ref[:, own]))
        gsum4 = spread(gsum_ref[:, own].astype(BF))
        far = far_ref[own, :].astype(F32)
        gfar = nt(gsum4, v_ref[:, own])
        drop = jnp.sum(far * gfar, axis=1, keepdims=True)
        third = (far * (gfar - drop)).astype(BF)
        glq_ref[:, own] += gather_diag(nn(third, k_ref[:, own]))
        glq = turn((glq_ref[:, own] / count).astype(BF))
        glk = turn((glk_ref[:, own] / count).astype(BF))
        dq = (nn(turn(lk4), first) + nn(glq, member)) * scale
        dk = (nn(turn(lq4), third) + nn(glk, member)) * scale
        dv = nn(turn(gsum4), far_ref[own, :])

        vt = turn(v_ref[:, own])
        padv_ref[:, inner] = jnp.where(valid, vt, jnp.zeros_like(vt))
        padc_ref[:, inner] = turn(dc_ref[:, own])
        parts = []
        for h in range(4):
            band = band_of(taps, 4 * g + h)
            parts.append(unblock(nt(blocks_of(padc_ref, h * LAND, 256), band), 256))
            plain = jnp.concatenate(
                [padc_ref[h * LAND : (h + 1) * LAND, 128 + at : 128 + at + 256] for at in range(0, length, 256)], axis=0
            )
            gram = nn(nt(flip, plain).astype(BF), blocks_of(padv_ref, h * LAND, 256))
            gram = pltpu.roll(gram, 0, 1, stride=1, stride_axis=0)
            gtap_ref[4 * g + h : 4 * g + h + 1, :] = jnp.sum(gram, axis=0, keepdims=True)
        dv = dv + jnp.where(valid, jnp.concatenate(parts, axis=0), 0.0)
        vecs_ref[0:1, own] = row_of(jnp.sum(dq, axis=1, keepdims=True))
        vecs_ref[1:2, own] = row_of(jnp.sum(dv, axis=1, keepdims=True))
        for lower in range(0, 256, 128):
            c = g * 256 + lower
            t, r = c // cols, c % cols
            pre_ref[t, r : r + 128, :] = dq[lower : lower + 128].astype(BF)
            pre_ref[t, cols + r : cols + r + 128, :] = dk[lower : lower + 128].astype(BF)
            pre_ref[t, 2 * cols + r : 2 * cols + r + 128, :] = dv[lower : lower + 128].astype(BF)
        tick(BACK_TICKS[4 + g])

    wait_all([x_l, w_l, gr1_l])

    def weight_grads():
        xt_ref[...] = turn(x_ref[...])
        for t in range(tn):
            dw = nt(xt_ref[...], pre_ref[t])
            if carry:
                dw = dw.reshape(dw_ref.shape[1:])
            dw_ref[t] = dw.astype(BF)

    def token_grads():
        for at in range(0, length, 256):
            part = nn(w_ref[0], pre_ref[0, :, at : at + 256])
            for t in range(1, tn):
                part = part + nn(w_ref[t], pre_ref[t, :, at : at + 256])
            gtok_ref[at // size : (at + 256) // size] = (
                (gr1_ref[at : at + 256, :].astype(F32) + turn(part)).reshape(256 // size, size, width).astype(BF)
            )

    if carry:
        token_grads()
        carry.send_rows()
        tick(BACK_TICKS[7])
        weight_grads()
        carry.send_grads()
        carry.pack()
        carry.finish(tick.stages)
    else:
        weight_grads()
        tick(1)
        token_grads()
        tick.rest()
    for lane in lanes:
        lane[4]()
    wait_all(sides)


def end(dp, *refs):
    ins, refs = refs[:26], refs[26:]
    vec, bsum = ins[24:]
    go, gi, gf, home, g_home, gq, gk, gv, gbq, gbv, gtaps, gbi, *refs = refs
    n_outs, refs = refs[:6], refs[6:]
    gtok, dw, vecs, gtap, *refs = refs
    count = 13 + 9 + 6
    own, refs = refs[:count], refs[count:]
    n_bufs = len(refs) - 15 - 15
    bufs, refs = refs[:n_bufs], refs[n_bufs:]
    me = Place(dp, gtap.shape[0] // HEADS_HERE)
    carry = Carry(me, gtok, dw, vec, bsum, vecs, gtap, g_home, gq, gk, gv, gbq, gbv, gtaps, gbi, n_outs, *refs[:15], refs[15:])
    attend_backward(dp, *ins[:24], gtok, dw, vecs, gtap, go, gi, gf, home, *own, *bufs, carry=carry)


def call_end(dp, x, w, ids, small, saved, dc, gr1, dwo, dwi, dwf, home, vec, bsum, taps):
    q, k, v, near, far, lq, lk, mix, summ, ker, z, a, v2, w2 = saved
    length, width = x.shape
    tn = w.shape[0]
    cols = width // tn
    s = jax.ShapeDtypeStruct
    vm = pltpu.VMEM
    depth, units = dwi.shape[4:]
    share = s((depth, cols), F32)
    outs = (share, s((depth, units), F32), s((depth, units), F32), s(home.shape, BF), s(home.shape, BF), share, share, share,
            s((cols,), F32), s((cols,), F32), s(taps.shape, F32), s((units,), F32)) + (s((depth,), F32),) * 6
    little = (ids, small, lq, lk, mix, summ, ker)
    large = (x, w, q, k, v, near, far, z, a, v2, w2, dc, gr1)
    args = little + large + (dwo, dwi, dwf, home, vec, bsum)
    mini = vm((LAND, width), F32)
    n_lanes = (2 * units + cols) // BACK_CUT
    n = n_lanes * reduce_count(dp)
    scratch = [vm((dp,) + home.shape[1:], BF), vm((tn, dp // 4, 2, 2, depth, 3 * cols), BF), vm((8, width), F32),
               vm((width // LAND, 512), F32)]
    scratch += [vm(b.shape, b.dtype) for b in large] + [vm((tn, 3 * cols, length), BF)] + [mini] * 5
    scratch += [vm((256, length + 256), BF), vm((256, length + 256), BF), vm((width, length), BF)]
    scratch += sems(n) + sems(dp) + [DMA((n_lanes,)), DMA((len(large),))]
    for k in range(n_lanes):
        scratch += reduce_bufs(dp, tn, depth, BACK_CUT, k in NORTH_LANES)
    scratch += carry_scratch(dp, tn, depth, cols)
    return pl.pallas_call(
        functools.partial(end, dp),
        out_shape=outs,
        in_specs=[VM] * len(little) + [ANY] * (len(large) + 4) + [VM] * 2,
        out_specs=tuple([VM] * 3 + [ANY] * 2 + [VM] * 13),
        scratch_shapes=scratch,
        input_output_aliases={len(args) - 3: 3},
        compiler_params=params(6, TOP),
        name="end",
    )(*args)


def call_attend_backward(dp, x, w, ids, small, saved, dc, gr1, dwo, dwi, dwf, home):
    q, k, v, near, far, lq, lk, mix, summ, ker, z, a, v2, w2 = saved
    length, width = x.shape
    tn = w.shape[0]
    cols = width // tn
    s = jax.ShapeDtypeStruct
    depth, units = dwi.shape[4:]
    outs = (s((dp,) + home.shape[1:], BF), s((tn, width, 3 * cols), BF), s((8, width), F32),
            s((width // LAND, 512), F32), s((depth, cols), F32), s((depth, units), F32), s((depth, units), F32),
            s(home.shape, BF))
    little = (ids, small, lq, lk, mix, summ, ker)
    large = (x, w, q, k, v, near, far, z, a, v2, w2, dc, gr1)
    args = little + large + (dwo, dwi, dwf, home)
    vm = pltpu.VMEM
    mini = vm((LAND, width), F32)
    n_lanes = (2 * units + cols) // BACK_CUT
    n = n_lanes * reduce_count(dp)
    scratch = [vm(b.shape, b.dtype) for b in large] + [vm((tn, 3 * cols, length), BF)] + [mini] * 5
    scratch += [vm((256, length + 256), BF), vm((256, length + 256), BF), vm((width, length), BF)]
    scratch += sems(n) + sems(dp) + [DMA((n_lanes,)), DMA((len(large),))]
    for k in range(n_lanes):
        scratch += reduce_bufs(dp, tn, depth, BACK_CUT, k in NORTH_LANES)
    return pl.pallas_call(
        functools.partial(attend_backward, dp),
        out_shape=outs,
        in_specs=[VM] * len(little) + [ANY] * (len(args) - len(little)),
        out_specs=tuple([VM] * 7 + [ANY]),
        scratch_shapes=scratch,
        input_output_aliases={len(args) - 1: 7},
        compiler_params=params(3, TOP),
        name="attend_backward",
    )(*args)


def finish(n, *refs):
    ins, outs, held, sem = refs[:n], refs[n : 2 * n], refs[2 * n : 3 * n], refs[3 * n]
    loads = [pltpu.make_async_copy(a, b, sem.at[k]) for k, (a, b) in enumerate(zip(ins, held))]
    writes = [pltpu.make_async_copy(a, b, sem.at[n + k]) for k, (a, b) in enumerate(zip(held, outs))]
    start_all(loads)
    for a, b in zip(loads, writes):
        a.wait()
        b.start()
    wait_all(writes)


def call_finish(arrays):
    n = len(arrays)
    return pl.pallas_call(
        functools.partial(finish, n),
        out_shape=tuple(jax.ShapeDtypeStruct(a.shape, a.dtype) for a in arrays),
        in_specs=[ANY] * n,
        out_specs=(ANY,) * n,
        scratch_shapes=[pltpu.VMEM(a.shape, a.dtype) for a in arrays] + [DMA((2 * n,))],
        compiler_params=pltpu.CompilerParams(vmem_limit_bytes=TOP * 2**20),
        name="finish",
    )(*arrays)


def local(tokens, cotangent, landmark_ids, w_query, w_key, w_value, b_query, b_value, conv_taps, w_out, b_out,
          first_gain, first_shift, w_inner, b_inner, w_outer, b_outer, second_gain, second_shift):
    dp = lax.axis_size("dp")
    tn = lax.axis_size("tensor")
    part, width = tokens.shape[1:]
    length = dp * part
    cols = w_query.shape[1]
    vectors = [b_out, first_gain, first_shift, b_outer, second_gain, second_shift]

    def join(w):
        return w.reshape(tn, width, w.shape[-1])

    def cut(g):
        return g.reshape(tn, dp // 4, 2, 2, width // dp, g.shape[2])

    joined = width // dp % 16 == 0 and part % 16 == 0
    if joined:
        rows, wqkv, wout, small, *done = call_begin(
            dp, tn, tokens, w_query, w_key, w_value, w_out, b_query, b_value, b_inner, conv_taps,
            landmark_ids, w_inner, w_outer, cotangent)
    else:
        rows, wqkv, wout, small = call_bring(
            dp, tn, tokens, w_query, w_key, w_value, w_out, b_query, b_value, b_inner, conv_taps)
        done = call_attend_forward(
            dp, rows.reshape(length, width), join(wqkv), small, landmark_ids, w_inner, w_outer, cotangent)
    rows = rows.reshape(length, width)
    wqkv, wout = join(wqkv), join(wout)
    q, k, v, near, far, ctx, *rest_saved, wi, wf, cota = done
    gr1, dc, dwo, dwi, dwf, vec, bsum, home = call_feed(
        dp, rows, ctx, wout, join(wi), join(wf), vectors, small, cotangent, cota
    )
    back = (dp, rows, wqkv, landmark_ids, small, (q, k, v, near, far, *rest_saved), dc, gr1, cut(dwo), cut(dwi), cut(dwf), home)
    if joined:
        go, gi, gf, out_home, *ends = call_end(*back, vec, bsum, conv_taps)
    else:
        grad_rows, dwqkv, vecs, gtap, go, gi, gf, out_home = call_attend_backward(*back)
        ends = call_carry_home(dp, tn, grad_rows, cut(dwqkv), vec, bsum, vecs, gtap, conv_taps)
    grad_home, gq, gk, gv, gbq, gbv, gtaps, gbi, gbo, gg1, gs1, gbf, gg2, gs2 = ends
    return call_finish((out_home, grad_home, gq, gk, gv, gbq, gbv, gtaps, go, gbo, gg1, gs1, gi, gbi, gf, gbf, gg2, gs2))


def solution(mesh):
    return jax.shard_map(
        local,
        mesh=mesh,
        in_specs=(
            P(None, "dp", None),
            P(None, "dp", None),
            P(),
            P("dp", "tensor"),
            P("dp", "tensor"),
            P("dp", "tensor"),
            P("tensor"),
            P("tensor"),
            P("tensor", None),
            P("dp", "tensor"),
            P(),
            P(),
            P(),
            P("dp", "tensor"),
            P("tensor"),
            P("dp", "tensor"),
            P(),
            P(),
            P(),
        ),
        out_specs=(
            P(None, "dp", None),
            P(None, "dp", None),
            P("dp", "tensor"),
            P("dp", "tensor"),
            P("dp", "tensor"),
            P("tensor"),
            P("tensor"),
            P("tensor", None),
            P("dp", "tensor"),
            P("dp"),
            P("dp"),
            P("dp"),
            P("dp", "tensor"),
            P("tensor"),
            P("dp", "tensor"),
            P("dp"),
            P("dp"),
            P("dp"),
        ),
        check_vma=False,
    )
```

```python
import functools

import jax
import jax.numpy as jnp
from jax import lax
from jax.experimental import pallas as pl
from jax.experimental.pallas import tpu as pltpu
from jax.sharding import PartitionSpec as P

F32 = jnp.float32
BF = jnp.bfloat16
MESH = pl.DeviceIdType.MESH
ANY = pl.BlockSpec(memory_space=pl.ANY)
TOP = 62
VM = pl.BlockSpec(memory_space=pltpu.VMEM)
DMA = pltpu.SemaphoreType.DMA
SMALL_ROWS = 32


class Place:
    def __init__(self, dp, tn):
        self.dp, self.tn = dp, tn
        self.nz = dp // 4
        i = lax.axis_index("dp")
        self.i = i
        self.t = lax.axis_index("tensor")
        self.c = lax.rem(i, 2)
        self.x = lax.rem(i // 2, 2)
        self.z = i // 4

    def at(self, z=None, x=None, c=None, t=None):
        z = self.z if z is None else z
        x = self.x if x is None else x
        c = self.c if c is None else c
        t = self.t if t is None else t
        return (z * 4 + x * 2 + c, t)


def greet(me, rows=True):
    bar = pltpu.get_barrier_semaphore()
    if rows:
        peers = [(lax.rem(me.i + k, me.dp), me.t) for k in range(1, me.dp)]
    else:
        peers = [me.at(z=lax.rem(me.z + k, me.nz)) for k in range(1, me.nz)] + [me.at(x=1 - me.x), me.at(c=1 - me.c)]
    peers.append((me.i, 1 - me.t))
    for p in peers:
        pl.semaphore_signal(bar, 1, device_id=p, device_id_type=MESH)
    pl.semaphore_wait(bar, len(peers))


def remote(src, dst, ss, rs, to):
    return pltpu.make_async_remote_copy(
        src_ref=src, dst_ref=dst, send_sem=ss, recv_sem=rs, device_id=to, device_id_type=MESH
    )


def start_all(copies):
    for c in copies:
        c.start()


def wait_all(copies):
    for c in copies:
        c.wait()


def to_owner(me, src, out, ss, rs, local):
    copies = []
    for k in range(1, me.dp):
        j = lax.rem(me.i + k, me.dp)
        copies.append(remote(src.at[me.t * me.dp + j], out.at[me.i], ss.at[k], rs.at[k], (j, me.t)))
    copies.append(pltpu.make_async_copy(src.at[me.t * me.dp + me.i], out.at[me.i], local))
    return copies


def to_home(me, src, out, ss, rs, local):
    copies = []
    for k in range(1, me.dp):
        j = lax.rem(me.i + k, me.dp)
        copies.append(remote(src.at[j], out.at[me.i], ss.at[k], rs.at[k], (j, me.t)))
    copies.append(pltpu.make_async_copy(src.at[me.i], out.at[me.i], local))
    return copies


def gather_lane(me, src, own, out, cols, north_first, ss, rs, local):
    t, z, x, c, n = me.t, me.z, me.x, me.c, me.nz
    px, py, sib = me.at(x=1 - x), me.at(t=1 - t), me.at(c=1 - c)

    def move(ref, k, to):
        return remote(ref, ref, ss.at[k], rs.at[k], to)

    zs = [pltpu.make_async_copy(src.at[:, own], out.at[t, z, x, c, :, cols], local)]
    for k in range(1, n):
        to = me.at(z=lax.rem(z + k, n))
        zs.append(remote(src.at[:, own], out.at[t, z, x, c, :, cols], ss.at[k], rs.at[k], to))
    if north_first:
        first, second = move(out.at[t, :, x, c, :, cols], n, py), move(out.at[:, :, x, c, :, cols], n + 1, px)
        d2, d3 = move(out.at[:, :, x, c, :, cols], n + 2, sib), move(out.at[:, :, 1 - x, c, :, cols], n + 3, sib)
    else:
        first, second = move(out.at[t, :, x, c, :, cols], n, px), move(out.at[t, :, :, c, :, cols], n + 1, py)
        d2, d3 = move(out.at[t, :, :, c, :, cols], n + 2, sib), move(out.at[1 - t, :, :, c, :, cols], n + 3, sib)

    def s0():
        start_all(zs)

    def s1():
        wait_all(zs)
        first.start()

    def s2():
        first.wait()
        second.start()
        d2.start()

    def s3():
        second.wait()
        d3.start()

    def s4():
        d2.wait()
        d3.wait()

    return [s0, s1, s2, s3, s4]


def gather_count(dp):
    return dp // 4 + 4


def add_low(a, b):
    return (a.astype(F32) + b.astype(F32)).astype(BF)


def reduce_lane(me, src, lo, w, bufs, ss, rs, local, puts, north_first=False):
    t, z, x, c, n = me.t, me.z, me.x, me.c, me.nz
    mine, rc, r1, r2, rz = bufs
    cols = pl.ds(lo, w)

    def move(a, b, q, to):
        return remote(a, b, ss.at[q], rs.at[q], to)

    keep = pltpu.make_async_copy(src.at[:, :, :, c, :, cols], mine, local)
    core = move(src.at[:, :, :, 1 - c, :, cols], rc, 0, me.at(c=1 - c))
    px, py = me.at(x=1 - x), me.at(t=1 - t)
    if north_first:
        first = move(rc.at[1 - t], r1, 1, py)
        second = move(r1.at[:, 1 - x], r2, 2, px)
    else:
        first = move(rc.at[:, :, 1 - x], r1, 1, px)
        second = move(r1.at[1 - t], r2, 2, py)
    lines = []
    for q in range(1, n):
        to = lax.rem(z + q, n)
        lines.append(move(r2.at[to], rz.at[q], 2 + q, me.at(z=to)))

    def s0():
        keep.start()
        core.start()

    def s1():
        keep.wait()
        core.wait()
        rc[...] = add_low(rc[...], mine[...])
        first.start()

    def s2():
        first.wait()
        r1[...] = add_low(r1[...], rc[t] if north_first else rc[:, :, x])
        second.start()

    def s3():
        second.wait()
        r2[...] = add_low(r2[...], r1[:, x] if north_first else r1[t])
        start_all(lines)

    def s4():
        total = r2[z].astype(F32)
        wait_all(lines)
        for q in range(1, n):
            total = total + rz[q].astype(F32)
        for dst, at, first_col, width in puts:
            dst[:, at : at + width] = total[:, first_col : first_col + width]

    return [s0, s1, s2, s3, s4]


def reduce_bufs(dp, tn, depth, w, north_first=False):
    nz = dp // 4
    one = (nz, 2) if north_first else (tn, nz)
    return [pltpu.VMEM((tn, nz, 2, depth, w), BF), pltpu.VMEM((tn, nz, 2, depth, w), BF),
            pltpu.VMEM(one + (depth, w), BF), pltpu.VMEM((nz, depth, w), BF), pltpu.VMEM((nz, depth, w), BF)]


def reduce_count(dp):
    return dp // 4 + 2


class Fetch:
    def __init__(self, src, dst, sem):
        self.copy, self.open = pltpu.make_async_copy(src, dst, sem), True

    def start(self):
        self.copy.start()
        return self

    def wait(self):
        if self.open:
            self.copy.wait()
        self.open = False


class Sub:
    def __init__(self, ref, base):
        self.ref, self.base = ref, base

    @property
    def at(self):
        return self

    def __getitem__(self, k):
        return self.ref.at[self.base + k]


def together(functions):
    def run():
        for f in functions:
            f()
    return run


class Ticks:
    def __init__(self, stages):
        self.stages = list(stages)

    def __call__(self, count=1):
        for _ in range(min(count, len(self.stages))):
            self.stages.pop(0)()

    def rest(self):
        self(len(self.stages))


def sems(n):
    return [DMA((n,)), DMA((n,))]


def params(cid, mib):
    return pltpu.CompilerParams(collective_id=cid, has_side_effects=True, vmem_limit_bytes=mib * 2**20)


def fill_piece(piece, bq, bv, bi, taps):
    piece[...] = jnp.zeros_like(piece)
    for ref, first in ((bq, ROWS_BQ), (bv, ROWS_BV), (bi, ROWS_BI)):
        line = ref[...].astype(F32).reshape(1, ref.shape[0])
        for r in range(ref.shape[0] // 128):
            piece[first + r : first + r + 1, :] = line[:, r * 128 : (r + 1) * 128]
    heads, width = taps.shape
    tap = taps[...].astype(F32)
    piece[ROWS_TAPS : ROWS_TAPS + heads, :width] = tap


def bring(dp, tn, tok, wq, wk, wv, wo, bq, bv, bi, taps, rows, wqkv, wout, small,
          r_ss, r_rs, g_ss, g_rs, local, piece):
    me = Place(dp, tn)
    cols = wq.shape[1]
    n = gather_count(dp)
    lanes = []
    for k, (src, dst, lo) in enumerate(((wq, wqkv, 0), (wk, wqkv, cols), (wv, wqkv, 2 * cols), (wo, wout, 0))):
        lanes.append(gather_lane(me, src, pl.ds(0, cols), dst, pl.ds(lo, cols), k % 2 == 1,
                                 Sub(g_ss, k * n), Sub(g_rs, k * n), local.at[k]))
    fill_piece(piece, bq, bv, bi, taps)
    greet(me)
    for s in (0, 1):
        for lane in lanes[2 * s : 2 * s + 2]:
            lane[0]()
    moved = to_owner(me, tok, rows, r_ss, r_rs, local.at[4])
    start_all(moved)
    side = [remote(piece, small.at[me.t], r_ss.at[0], r_rs.at[0], (me.i, 1 - me.t)),
            pltpu.make_async_copy(piece, small.at[me.t], local.at[5])]
    start_all(side)
    for pair, stage in ((0, 1), (0, 2), (1, 1), (0, 3), (1, 2), (1, 3), (0, 4), (1, 4)):
        for lane in lanes[2 * pair : 2 * pair + 2]:
            lane[stage]()
    wait_all(side)
    wait_all(moved)


def call_bring(dp, tn, tok, wq, wk, wv, wo, bq, bv, bi, taps):
    s = jax.ShapeDtypeStruct
    depth, cols = wq.shape
    lead = (tn, dp // 4, 2, 2, depth)
    outs = (s((dp,) + tok.shape[1:], BF), s(lead + (3 * cols,), BF), s(lead + (cols,), BF), s((tn, SMALL_ROWS, 128), F32))
    return pl.pallas_call(
        functools.partial(bring, dp, tn),
        out_shape=outs,
        in_specs=[ANY] * 5 + [VM] * 4,
        out_specs=(ANY, ANY, ANY, ANY),
        scratch_shapes=sems(dp) + sems(4 * gather_count(dp)) + [DMA((6,)), pltpu.VMEM((SMALL_ROWS, 128), F32)],
        compiler_params=params(0, TOP),
        name="bring",
    )(tok, wq, wk, wv, wo, bq, bv, bi, taps)


def carry_home(dp, tn, g_rows, dwqkv, vec, bsum, vecs, gtap, g_home, gq, gk, gv, gbq, gbv, gtaps, gbi, *refs):
    n_outs, (r_ss, r_rs, v_ss, v_rs, g_ss, g_rs, local, norms, rest, nbuf, rbuf, nall, rall, nsum, rsum) = refs[:6], refs[6:21]
    bufs = refs[21:]
    me = Place(dp, tn)
    greet(me)
    c = Carry(me, g_rows, dwqkv, vec, bsum, vecs, gtap, g_home, gq, gk, gv, gbq, gbv, gtaps, gbi, n_outs, r_ss, r_rs, v_ss, v_rs,
              g_ss, g_rs, local, norms, rest, nbuf, rbuf, nall, rall, nsum, rsum, bufs)
    c.send_rows()
    c.send_grads()
    c.pack()
    c.finish([])


class Carry:
    def __init__(self, me, g_rows, dwqkv, vec, bsum, vecs, gtap, g_home, gq, gk, gv, gbq, gbv, gtaps, gbi, n_outs, r_ss, r_rs,
                 v_ss, v_rs, g_ss, g_rs, local, norms, rest, nbuf, rbuf, nall, rall, nsum, rsum, bufs):
        self.me, self.sources = me, (vec, bsum, vecs, gtap)
        self.results = (gbq, gbv, gtaps, gbi, n_outs)
        self.v = (v_ss, v_rs, norms, rest, nbuf, rbuf, nall, rall, nsum, rsum)
        self.cols = cols = gq.shape[1]
        dp, n = me.dp, reduce_count(me.dp)
        self.lanes = []
        for k, dst in enumerate((gq, gk, gv)):
            self.lanes.append(reduce_lane(me, dwqkv, k * cols, cols, bufs[5 * k : 5 * k + 5], Sub(g_ss, k * n),
                                          Sub(g_rs, k * n), local.at[1 + k], [(dst, 0, 0, cols)]))
        mine = me.t * dp
        self.partner = partner = (me.i, 1 - me.t)
        self.first = []
        for k in range(1, dp):
            j = lax.rem(me.i + k, dp)
            self.first.append(remote(g_rows.at[j], g_home.at[mine + me.i], r_ss.at[k], r_rs.at[k], (j, me.t)))
        self.own = pltpu.make_async_copy(g_rows.at[me.i], g_home.at[mine + me.i], local.at[0])
        self.second = [remote(g_rows.at[me.i], g_home.at[mine + me.i], r_ss.at[dp], r_rs.at[dp], partner)]
        for k in range(1, dp):
            j = mine + lax.rem(me.i + dp - k, dp)
            self.second.append(remote(g_home.at[j], g_home.at[j], r_ss.at[dp + k], r_rs.at[dp + k], partner))

    def send_rows(self):
        self.turns = waves(self.me.dp)
        for k in self.turns[0] + self.turns[1]:
            self.first[k - 1].start()
        self.own.start()
        self.second[0].start()

    def send_grads(self):
        for lane in self.lanes:
            lane[0]()

    def pack(self):
        me = self.me
        dp, tn, cols = me.dp, me.tn, self.cols
        vec, bsum, vecs, gtap = self.sources
        gbq, gbv, gtaps, gbi, n_outs = self.results
        v_ss, v_rs, norms, rest, nbuf, rbuf, nall, rall, nsum, rsum = self.v
        share = n_outs[0].shape[0]
        six = jnp.sum(vec[...], axis=1)
        norms[...] = jnp.zeros_like(norms)
        rest[...] = jnp.zeros_like(rest)
        for j in range(dp):
            norms[j, 0:6, :share] = six[:, j * share : (j + 1) * share]
        units = jnp.sum(bsum[...], axis=0, keepdims=True)
        per, taps = gtaps.shape
        for t in range(tn):
            for line, first_row, size in ((vecs[0:1, :], ROWS_BQ, cols), (vecs[1:2, :], ROWS_BV, cols),
                                          (units, ROWS_BI, gbi.shape[0])):
                for r in range(size // 128):
                    lo = t * size + r * 128
                    rest[t, first_row + r : first_row + r + 1, :] = line[:, lo : lo + 128]
            rest[t, ROWS_TAPS : ROWS_TAPS + per, :taps] = gtap[t * per : (t + 1) * per, FLIP_AT : FLIP_AT + taps]
        self.v1 = [remote(norms, nbuf, v_ss.at[0], v_rs.at[0], self.partner),
                   remote(rest.at[1 - me.t], rbuf, v_ss.at[1], v_rs.at[1], self.partner)]
        start_all(self.v1)

    def finish(self, others):
        me = self.me
        dp = me.dp
        gbq, gbv, gtaps, gbi, n_outs = self.results
        v_ss, v_rs, norms, rest, nbuf, rbuf, nall, rall, nsum, rsum = self.v
        for lane in self.lanes:
            lane[1]()
        wait_all(self.v1)
        nsum[...] = norms[...] + nbuf[...]
        rsum[...] = rest[me.t] + rbuf[...]
        v2 = []
        for k in range(1, dp):
            j = lax.rem(me.i + k, dp)
            v2.append(remote(nsum.at[j], nall.at[k], v_ss.at[2 * k], v_rs.at[2 * k], (j, me.t)))
            v2.append(remote(rsum, rall.at[k], v_ss.at[2 * k + 1], v_rs.at[2 * k + 1], (j, me.t)))
        start_all(v2)
        stages = list(others) + [lane[s] for s in (2, 3) for lane in self.lanes]
        n = len(self.turns)
        for w, turn_ in enumerate(self.turns):
            for k in turn_:
                self.first[k - 1].wait()
                self.second[k].start()
            if w + 2 < n:
                start_all([self.first[k - 1] for k in self.turns[w + 2]])
            for _ in range(-(-len(stages) // (n - w))):
                stages.pop(0)()
        for st in stages:
            st()
        wait_all(v2)
        ntot = nsum[me.i]
        rtot = rsum[...]
        for k in range(1, dp):
            ntot = ntot + nall[k]
            rtot = rtot + rall[k]
        share = n_outs[0].shape[0]
        per, taps = gtaps.shape
        for k in range(6):
            n_outs[k][...] = ntot[k, :share]
        for ref, first_row in ((gbq, ROWS_BQ), (gbv, ROWS_BV), (gbi, ROWS_BI)):
            size = ref.shape[0]
            ref[...] = jnp.concatenate(
                [rtot[first_row + r : first_row + r + 1] for r in range(size // 128)], axis=1).reshape(size)
        gtaps[...] = rtot[ROWS_TAPS : ROWS_TAPS + per, :taps]
        for lane in self.lanes:
            lane[4]()
        self.own.wait()
        wait_all(self.second)


def carry_scratch(dp, tn, depth, cols):
    norms, rest = (dp, 8, 128), (tn, 24, 128)
    scratch = sems(2 * dp) + sems(2 * dp) + sems(3 * reduce_count(dp)) + [DMA((4,))]
    scratch += [pltpu.VMEM(norms, F32), pltpu.VMEM(rest, F32),
                pltpu.VMEM(norms, F32), pltpu.VMEM(rest[1:], F32),
                pltpu.VMEM((dp,) + norms[1:], F32), pltpu.VMEM((dp,) + rest[1:], F32),
                pltpu.VMEM(norms, F32), pltpu.VMEM(rest[1:], F32)]
    for _ in range(3):
        scratch += reduce_bufs(dp, tn, depth, cols)
    return scratch


def call_carry_home(dp, tn, g_rows, dwqkv, vec, bsum, vecs, gtap, taps):
    s = jax.ShapeDtypeStruct
    r, w = g_rows.shape[1:]
    depth, cols = dwqkv.shape[4], dwqkv.shape[5] // 3
    share = s((depth, cols), F32)
    outs = (s((tn * dp, r, w), BF), share, share, share, s((cols,), F32), s((cols,), F32), s(taps.shape, F32),
            s((bsum.shape[1] // tn,), F32)) + (s((depth,), F32),) * 6
    scratch = carry_scratch(dp, tn, depth, cols)
    return pl.pallas_call(
        functools.partial(carry_home, dp, tn),
        out_shape=outs,
        in_specs=[ANY, ANY] + [VM] * 4,
        out_specs=(ANY,) + (VM,) * 13,
        scratch_shapes=scratch,
        compiler_params=params(4, TOP),
        name="carry_home",
    )(g_rows, dwqkv, vec, bsum, vecs, gtap)


F32 = jnp.float32
BF = jnp.bfloat16
LAND = 64
ITERS = 6
HEADS_HERE = 6
ROWS_BQ, ROWS_BV, ROWS_BI, ROWS_TAPS = 0, 3, 6, 18
EDGE = 112
TAPS = 33
FLIP_AT = 367


def nn(a, b):
    return lax.dot_general(a, b, (((1,), (0,)), ((), ())), preferred_element_type=F32)


def nt(a, b):
    return lax.dot_general(a, b, (((1,), (1,)), ((), ())), preferred_element_type=F32)


def turn(a):
    return jnp.transpose(a, (1, 0))


def same_head(rows, columns):
    left = lax.broadcasted_iota(jnp.int32, (rows, columns), 0) // LAND
    right = lax.broadcasted_iota(jnp.int32, (rows, columns), 1) // LAND
    return left == right


def spread(small):
    n = small.shape[1] // LAND
    tall = jnp.concatenate([small] * n, axis=0)
    return jnp.where(same_head(n * LAND, n * LAND), tall, jnp.zeros_like(tall))


def gather_diag(full):
    n = full.shape[1] // LAND
    lane = lax.broadcasted_iota(jnp.int32, (LAND, full.shape[1]), 1) // LAND
    out = full[:LAND]
    for h in range(1, n):
        out = jnp.where(lane == h, full[h * LAND : (h + 1) * LAND], out)
    return out


def halves(a):
    high = a.astype(BF)
    return high, (a - high.astype(F32)).astype(BF)


def pair_nn(a, b):
    ah, al = halves(a)
    bh, bl = halves(b)
    bh, bl = spread(bh), spread(bl)
    wide = jnp.concatenate([bh, bl], axis=1)
    r = nn(jnp.concatenate([ah, al], axis=1), jnp.concatenate([wide, wide], axis=0))
    return r[:, : 2 * LAND] + r[:, 2 * LAND :]


def pair_nt(a, b):
    ah, al = halves(a)
    bh, bl = halves(b)
    bh, bl = spread(bh), spread(bl)
    tall = jnp.concatenate([bh, bl], axis=0)
    r = nt(jnp.concatenate([ah, al], axis=1), jnp.concatenate([tall, tall], axis=1))
    return r[:, : 2 * LAND] + r[:, 2 * LAND :]


def pair_turn(a):
    t = turn(a)
    return jnp.concatenate([t[:LAND], t[LAND:]], axis=1)


def pair_sum(a):
    left = lax.broadcasted_iota(jnp.int32, a.shape, 1) < LAND
    low = jnp.sum(jnp.where(left, a, 0.0), axis=1, keepdims=True)
    high = jnp.sum(jnp.where(left, 0.0, a), axis=1, keepdims=True)
    return jnp.where(left, low, high)


def pair_softmax(a):
    left = lax.broadcasted_iota(jnp.int32, a.shape, 1) < LAND
    low = jnp.max(jnp.where(left, a, -1e30), axis=1, keepdims=True)
    high = jnp.max(jnp.where(left, -1e30, a), axis=1, keepdims=True)
    e = jnp.exp(a - jnp.where(left, low, high))
    return e / pair_sum(e)


def pair_eye():
    r = lax.broadcasted_iota(jnp.int32, (LAND, 2 * LAND), 0)
    c = lax.broadcasted_iota(jnp.int32, (LAND, 2 * LAND), 1) % LAND
    return jnp.where(r == c, 1.0, 0.0).astype(F32)


def toeplitz(row, size, width):
    return pltpu.roll(jnp.broadcast_to(row, (size, width)), 0, 1, stride=1, stride_axis=0)


def blocks_of(ref, lower, block):
    length = ref.shape[1] - 256
    return jnp.concatenate(
        [ref[lower : lower + LAND, at : at + block + 256] for at in range(0, length, block)], axis=0
    )


def unblock(stacked, block):
    n = stacked.shape[0] // LAND
    return jnp.concatenate([stacked[i * LAND : (i + 1) * LAND] for i in range(n)], axis=1)


def own_sequence():
    return lax.axis_index("tensor") * lax.axis_size("dp") + lax.axis_index("dp")


def side_row(small_ref, t, first, count):
    return jnp.concatenate([small_ref[t, r : r + 1, :] for r in range(first, first + count)], axis=1)


def band_of(rows, head):
    h = head % HEADS_HERE
    row = jnp.concatenate([rows[head // HEADS_HERE][h : h + 1, :], jnp.zeros((1, 384), F32)], axis=1)
    return toeplitz(pltpu.roll(row, EDGE, 1), 256, 512).astype(BF)


def tap_rows(small_ref, t):
    return small_ref[t, ROWS_TAPS : ROWS_TAPS + 8, :]


def reversed_taps(rows):
    turned = jnp.where(
        lax.broadcasted_iota(jnp.int32, (128, 128), 0) + lax.broadcasted_iota(jnp.int32, (128, 128), 1) == TAPS - 1, 1.0, 0.0
    ).astype(BF)
    return nn(rows.astype(BF), turned)


def forward_core(rows_of, weight_of, tn, small_ref, ids_ref, q_ref, k_ref, v_ref, near_ref, far_ref, ctx_ref,
                 lq_ref, lk_ref, mix_ref, sum_ref, ker_ref, z_ref, a_ref, v2_ref, w2_ref, pad_ref, tick, ready, writes):
    length, width = q_ref.shape
    cols = width // tn
    scale = LAND ** -0.25
    rows_at = 256
    pairs = width // 128
    groups = width // 256
    q_w, k_w, v_w, near_w, far_w, ctx_w, z_w, a_w, v2_w, w2_w = writes
    ready()
    bq = [side_row(small_ref, t, ROWS_BQ, 3) for t in range(tn)]
    bv = [side_row(small_ref, t, ROWS_BV, 3) for t in range(tn)]

    def project(i, carry):
        at = pl.ds(pl.multiple_of(i * rows_at, rows_at), rows_at)
        for t in range(tn):
            out = nn(rows_of(at, i), weight_of(t))
            own = slice(t * cols, (t + 1) * cols)
            q_ref[at, own] = ((out[:, :cols] + bq[t]) * scale).astype(BF)
            k_ref[at, own] = (out[:, cols : 2 * cols] * scale).astype(BF)
            v_ref[at, own] = (out[:, 2 * cols :] + bv[t]).astype(BF)
        return carry

    lax.fori_loop(0, length // rows_at, project, 0)
    start_all([q_w, k_w, v_w])
    tick()

    ids = ids_ref[pl.ds(own_sequence(), 1), :]
    member = jnp.where(lax.broadcasted_iota(jnp.int32, (LAND, length), 0) == ids, 1.0, 0.0).astype(F32)
    count = jnp.sum(member, axis=1, keepdims=True)
    member = member.astype(BF)
    valid = ids < LAND
    lq_ref[...] = (nn(member, q_ref[...]) / count).astype(BF)
    lk_ref[...] = (nn(member, k_ref[...]) / count).astype(BF)

    eye = pair_eye()
    for p in range(pairs):
        own = slice(p * 128, (p + 1) * 128)
        scores = nt(lq_ref[:, own], spread(lk_ref[:, own]))
        kernel = pair_softmax(scores)
        ker_ref[:, own] = kernel
        left = lax.broadcasted_iota(jnp.int32, kernel.shape, 1) < LAND
        total = jnp.sum(pair_sum(kernel * kernel), axis=0, keepdims=True)
        z_ref[0, :, own] = pair_turn(kernel) / total
    tick()

    for g in range(groups):
        own = slice(g * 256, (g + 1) * 256)
        scores = nt(spread(lk_ref[:, own]), q_ref[:, own]).reshape(4, LAND, length)
        scores = jnp.exp(scores - jnp.max(scores, axis=1, keepdims=True))
        scores = scores / jnp.sum(scores, axis=1, keepdims=True)
        near_ref[own, :] = scores.reshape(256, length).astype(BF)
        scores = nt(spread(lq_ref[:, own]), k_ref[:, own])
        scores = jnp.where(valid, scores, -1e30)
        scores = jnp.exp(scores - jnp.max(scores, axis=1, keepdims=True))
        scores = scores / jnp.sum(scores, axis=1, keepdims=True)
        far_ref[own, :] = scores.astype(BF)
        sum_ref[:, own] = gather_diag(nn(far_ref[own, :], v_ref[:, own]))
        tick()
    start_all([near_w, far_w])

    def iterate(n, carry):
        for p in range(pairs):
            own = slice(p * 128, (p + 1) * 128)
            z = z_ref[n, :, own]
            a = pair_nn(ker_ref[:, own], z)
            v2 = 15.0 * eye - pair_nn(a, 7.0 * eye - a)
            w2 = 13.0 * eye - pair_nn(a, v2)
            a_ref[n, :, own] = a
            v2_ref[n, :, own] = v2
            w2_ref[n, :, own] = w2
            z_ref[n + 1, :, own] = 0.25 * pair_nn(z, w2)
        return carry

    lax.fori_loop(0, ITERS // 2, iterate, 0)
    tick()
    lax.fori_loop(ITERS // 2, ITERS, iterate, 0)
    start_all([z_w, a_w, v2_w, w2_w])
    tick()

    for p in range(pairs):
        own = slice(p * 128, (p + 1) * 128)
        mix_ref[:, own] = pair_nn(z_ref[ITERS, :, own], sum_ref[:, own]).astype(BF)

    pad_ref[...] = jnp.zeros_like(pad_ref)
    taps = [tap_rows(small_ref, t) for t in range(tn)]
    for g in range(groups):
        own = slice(g * 256, (g + 1) * 256)
        att = nn(turn(spread(mix_ref[:, own])), near_ref[own, :])
        vt = turn(v_ref[:, own])
        pad_ref[:, 128 : 128 + length] = jnp.where(valid, vt, jnp.zeros_like(vt))
        parts = []
        for h in range(4):
            band = band_of(taps, 4 * g + h)
            parts.append(unblock(nt(blocks_of(pad_ref, h * LAND, 256), band), 256))
        att = (att + jnp.concatenate(parts, axis=0)).astype(BF)
        ctx_ref[:, own] = turn(att)
        tick()


def attend_forward(dp, x_in, w_in, small_ref, ids_ref, wi_ref, wf_ref, cot_ref,
                   q_out, k_out, v_out, near_out, far_out, ctx_out, lq_ref, lk_ref, mix_ref, sum_ref, ker_ref,
                   z_out, a_out, v2_out, w2_out, wi_all, wf_all, cota_ref, pad_ref, x_ref, w_ref, q_ref, k_ref, v_ref,
                   near_ref, far_ref, ctx_ref, z_ref, a_ref, v2_ref, w2_ref, g_ss, g_rs, c_ss, c_rs, local, move):
    length, width = x_ref.shape
    tn = w_ref.shape[0]
    loads = [Fetch(x_in, x_ref, move.at[0]).start(), Fetch(w_in, w_ref, move.at[1]).start()]
    writes = [
        Fetch(a, b, move.at[2 + k]) for k, (a, b) in enumerate((
            (q_ref, q_out), (k_ref, k_out), (v_ref, v_out), (near_ref, near_out), (far_ref, far_out), (ctx_ref, ctx_out),
            (z_ref, z_out), (a_ref, a_out), (v2_ref, v2_out), (w2_ref, w2_out)))]
    me = Place(dp, tn)
    n = gather_count(dp)
    half = wi_ref.shape[1] // 2
    lanes = []
    for p, (src, dst) in enumerate(((wi_ref, wi_all), (wf_ref, wf_all))):
        for h in range(2):
            own, k = pl.ds(h * half, half), 2 * p + h
            lanes.append(gather_lane(me, src, own, dst, own, h == 1, Sub(g_ss, k * n), Sub(g_rs, k * n), local.at[k]))

    def stage(pair, s):
        def run():
            for lane in lanes[2 * pair : 2 * pair + 2]:
                lane[s]()
        return run

    greet(me)
    stage(0, 0)()
    stage(1, 0)()
    arriving = []
    for k in range(1, early_blocks(dp) + 1):
        j = lax.rem(me.i + k, dp)
        arriving.append(remote(cot_ref.at[me.t * dp + j], cota_ref.at[me.i], c_ss.at[k], c_rs.at[k], (j, me.t)))
    start_all(arriving)
    tick = Ticks([stage(0, 1), stage(0, 2), stage(1, 1), stage(0, 3), stage(1, 2), stage(1, 3), stage(0, 4), stage(1, 4)])
    forward_core(lambda at, i: x_ref[at, :], lambda t: w_ref[t], tn, small_ref, ids_ref, q_ref, k_ref, v_ref, near_ref,
                 far_ref, ctx_ref, lq_ref, lk_ref, mix_ref, sum_ref, ker_ref, z_ref, a_ref, v2_ref, w2_ref, pad_ref,
                 tick, lambda: wait_all(loads), writes)
    writes[5].start()
    tick.rest()
    wait_all(arriving)
    wait_all(writes)


def begin(dp, tn, tok, wq, wk, wv, wo, bq, bv, bi, taps, ids_ref, wi_ref, wf_ref, cot_ref,
          rows_out, wqkv_out, wout, small_out, q_out, k_out, v_out, near_out, far_out, ctx_out,
          lq_ref, lk_ref, mix_ref, sum_ref, ker_ref, z_out, a_out, v2_out, w2_out, wi_all, wf_all, cota_ref,
          x_ref, w_ref, small_ref, piece, pad_ref, q_ref, k_ref, v_ref, near_ref, far_ref, ctx_ref, z_ref, a_ref, v2_ref, w2_ref,
          r_ss, r_rs, p_ss, p_rs, g_ss, g_rs, c_ss, c_rs, local, move):
    me = Place(dp, tn)
    cols = wq.shape[1]
    n = gather_count(dp)
    first = []
    for k, (src, dst, lo) in enumerate(((wq, w_ref, 0), (wk, w_ref, cols), (wv, w_ref, 2 * cols), (wo, wout, 0))):
        first.append(gather_lane(me, src, pl.ds(0, cols), dst, pl.ds(lo, cols), k % 2 == 1,
                                 Sub(p_ss, k * n), Sub(p_rs, k * n), local.at[k]))
    lanes = []
    parts = wi_ref.shape[1] // FORWARD_CUT
    for p, (src, dst) in enumerate(((wi_ref, wi_all), (wf_ref, wf_all))):
        for h in range(parts):
            own, k = pl.ds(h * FORWARD_CUT, FORWARD_CUT), parts * p + h
            lanes.append(gather_lane(me, src, own, dst, own, h % 2 == 1, Sub(g_ss, k * n), Sub(g_rs, k * n), local.at[6 + k]))

    def stage(pair, s):
        def run():
            for lane in lanes[2 * pair : 2 * pair + 2]:
                lane[s]()
        return run

    fill_piece(piece, bq, bv, bi, taps)
    greet(me)
    for lane in first:
        lane[0]()
    moved = to_owner(me, tok, x_ref, r_ss, r_rs, local.at[4])
    start_all(moved)
    side = [remote(piece, small_ref.at[me.t], r_ss.at[0], r_rs.at[0], (me.i, 1 - me.t)),
            pltpu.make_async_copy(piece, small_ref.at[me.t], local.at[5])]
    start_all(side)
    arriving = []
    for k in range(1, early_blocks(dp) + 1):
        j = lax.rem(me.i + k, dp)
        arriving.append(remote(cot_ref.at[me.t * dp + j], cota_ref.at[me.i], c_ss.at[k], c_rs.at[k], (j, me.t)))
    pairs = len(lanes) // 2
    for pair, st in ((0, 1), (0, 2), (1, 1), (1, 2)):
        for lane in first[2 * pair : 2 * pair + 2]:
            lane[st]()
    for pair in range(FORWARD_EARLY):
        stage(pair, 0)()
    for lane in first:
        lane[3]()
    for pair in range(FORWARD_EARLY):
        stage(pair, 1)()
        stage(pair + FORWARD_EARLY, 0)()
        stage(pair, 2)()
    for lane in first:
        lane[4]()
    wait_all(side)
    wait_all(moved)
    rolled = 2 * FORWARD_EARLY
    while rolled < FORWARD_EARLY + FORWARD_AHEAD:
        stage(rolled, 0)()
        rolled += 1
    keep = [Fetch(x_ref, rows_out, move.at[0]).start(), Fetch(w_ref, wqkv_out, move.at[1]).start(),
            Fetch(small_ref, small_out, move.at[12]).start()]
    writes = [
        Fetch(a, b, move.at[2 + k]) for k, (a, b) in enumerate((
            (q_ref, q_out), (k_ref, k_out), (v_ref, v_out), (near_ref, near_out), (far_ref, far_out), (ctx_ref, ctx_out),
            (z_ref, z_out), (a_ref, a_out), (v2_ref, v2_out), (w2_ref, w2_out)))]
    todo = []
    for pair in range(FORWARD_EARLY, pairs):
        steps = [stage(pair, 1)]
        if rolled < pairs:
            steps.append(stage(rolled, 0))
            rolled += 1
        if rolled == pairs:
            steps.append(lambda: start_all(arriving))
            rolled += 1
        todo += [together(steps), stage(pair, 2)]
    todo += [stage(pair, 3) for pair in range(pairs)] + [stage(pair, 4) for pair in range(pairs)]
    tick = Ticks(todo)
    width = q_ref.shape[1]
    part = x_ref.shape[1]
    per = 256 // part
    forward_core(lambda at, i: x_ref[pl.ds(i * per, per)].reshape(256, width), lambda t: w_ref[t].reshape(width, 3 * cols),
                 tn, small_ref, ids_ref, q_ref, k_ref, v_ref, near_ref, far_ref, ctx_ref, lq_ref, lk_ref, mix_ref, sum_ref,
                 ker_ref, z_ref, a_ref, v2_ref, w2_ref, pad_ref, tick, lambda: None, writes)
    writes[5].start()
    tick.rest()
    wait_all(arriving)
    wait_all(writes)
    wait_all(keep)


FORWARD_CUT = 384
FORWARD_EARLY = 1
FORWARD_AHEAD = 2


def call_begin(dp, tn, tok, wq, wk, wv, wo, bq, bv, bi, taps, ids, wi, wf, cot):
    s = jax.ShapeDtypeStruct
    vm = pltpu.VMEM
    depth, cols = wq.shape
    units = wi.shape[1]
    part, width = tok.shape[1:]
    length = dp * part
    lead = (tn, dp // 4, 2, 2, depth)
    big, tall = s((length, width), BF), s((width, length), BF)
    low, wide = s((LAND, width), BF), s((LAND, width), F32)
    steps, steps1 = s((ITERS, LAND, width), F32), s((ITERS + 1, LAND, width), F32)
    whole = s(lead + (units,), BF)
    blocks = s((dp, part, width), BF)
    small = s((tn, SMALL_ROWS, 128), F32)
    wqkv = s(lead + (3 * cols,), BF)
    outs = (blocks, wqkv, s(lead + (cols,), BF), small,
            big, big, big, tall, tall, big, low, low, low, wide, wide, steps1, steps, steps, steps, whole, whole, blocks)
    n_lanes = 2 * (units // FORWARD_CUT)
    return pl.pallas_call(
        functools.partial(begin, dp, tn),
        out_shape=outs,
        in_specs=[ANY] * 5 + [VM] * 5 + [ANY] * 3,
        out_specs=tuple([ANY] * 10 + [VM] * 5 + [ANY] * 7),
        scratch_shapes=[vm(o.shape, o.dtype) for o in (blocks, wqkv, small)]
        + [vm((SMALL_ROWS, 128), F32), vm((256, length + 256), BF)]
        + [vm(o.shape, o.dtype) for o in outs[4:10] + outs[15:19]]
        + sems(dp) + sems(4 * gather_count(dp)) + sems(n_lanes * gather_count(dp)) + sems(dp)
        + [DMA((6 + n_lanes,)), DMA((13,))],
        compiler_params=params(5, TOP),
        name="begin",
    )(tok, wq, wk, wv, wo, bq, bv, bi, taps, ids, wi, wf, cot)


def waves(dp):
    return [[k for k in range(1, dp) if k % 4 == r] for r in (1, 2, 3, 0)]


def early_blocks(dp):
    return dp // 4


def call_attend_forward(dp, x, w, small, ids, wi, wf, cot):
    length, width = x.shape
    s = jax.ShapeDtypeStruct
    big = s((length, width), BF)
    tall = s((width, length), BF)
    low = s((LAND, width), BF)
    wide = s((LAND, width), F32)
    steps = s((ITERS, LAND, width), F32)
    tn = w.shape[0]
    depth, units = wi.shape
    whole = s((tn, dp // 4, 2, 2, depth, units), BF)
    outs = (big, big, big, tall, tall, big, low, low, low, wide, wide, s((ITERS + 1, LAND, width), F32), steps, steps, steps,
            whole, whole, s((dp,) + cot.shape[1:], BF))
    vm = pltpu.VMEM
    return pl.pallas_call(
        functools.partial(attend_forward, dp),
        out_shape=outs,
        in_specs=[ANY] * 2 + [VM] * 2 + [ANY] * 3,
        out_specs=tuple([ANY] * 6 + [VM] * 5 + [ANY] * 7),
        scratch_shapes=[vm((256, length + 256), BF)] + [vm(o.shape, o.dtype) for o in (x, w) + outs[:6] + outs[11:15]]
        + sems(4 * gather_count(dp)) + sems(dp) + [DMA((4,)), DMA((12,))],
        compiler_params=params(1, TOP),
        name="attend_forward",
    )(x, w, small, ids, wi, wf, cot)


ROOT_HALF = 0.7071067811865476
P_ERF = 0.3275911
C_ERF = (0.254829592, -0.284496736, 1.421413741, -1.453152027, 1.061405429)


def gelu_both(u):
    x = jnp.abs(u) * ROOT_HALF
    e = jnp.exp(-0.5 * u * u)
    t = 1.0 / (1.0 + P_ERF * x)
    poly = C_ERF[4]
    for c in (C_ERF[3], C_ERF[2], C_ERF[1], C_ERF[0]):
        poly = poly * t + c
    tail = 0.5 * poly * t * e
    phi = jnp.where(u < 0.0, tail, 1.0 - tail)
    return u * phi, phi + u * e * 0.3989422804014327


def norm_parts(r):
    n = r.shape[1]
    center = r - jnp.sum(r, axis=1, keepdims=True) * (1.0 / n)
    spread_ = jnp.sum(center * center, axis=1, keepdims=True) * (1.0 / n)
    rstd = lax.rsqrt(spread_ + 1e-05)
    return center * rstd, rstd


def norm_back(e, normed, rstd):
    n = e.shape[1]
    mean_e = jnp.sum(e, axis=1, keepdims=True) * (1.0 / n)
    mean_en = jnp.sum(e * normed, axis=1, keepdims=True) * (1.0 / n)
    return rstd * (e - mean_e - normed * mean_en)


def fold(a):
    return jnp.sum(a.reshape(a.shape[0] // 8, 8, a.shape[1]), axis=0)


def feed(dp, x_in, ctx_in, wo_in, wi_in, wf_in, bo_in, g1_in, s1_in, bf_in, g2_in, s2_in, small_ref, cot_ref, cota_ref,
         gr1_out, dc_out, dwo_out, dwi_out, dwf_out, vec_ref, bsum_ref, home_ref,
         act_ref, gi_ref, hid_ref, gr2_ref, turn_ref, n1_ref, n2_ref, rs1_ref, rs2_ref, out_ref, cots_ref,
         x_ref, ctx_ref, wo_ref, wi_ref, wf_ref, gr1_ref, dc_ref, dwo_ref, dwi_ref, dwf_ref,
         c_ss, c_rs, h_ss, h_rs, f_ss, f_rs, local, move):
    length, width = x_ref.shape
    tn = wo_ref.shape[0]
    cols = width // tn
    units = wi_ref.shape[2]
    size = 256
    chunk = 512
    part = length // dp
    per = size // part
    me = Place(dp, tn)
    x_l, ctx_l, wo_l, wi_l, wf_l = loads = [
        Fetch(a, b, move.at[k]).start() for k, (a, b) in enumerate((
            (x_in, x_ref), (ctx_in, ctx_ref), (wo_in, wo_ref), (wi_in, wi_ref), (wf_in, wf_ref)))]
    greet(me)
    mine = me.t * dp
    early = early_blocks(dp)
    arriving = [pltpu.make_async_copy(cot_ref.at[mine + me.i], cots_ref.at[me.i], local.at[0])]
    leaving, passing, turns = {}, {}, waves(dp)
    partner = (me.i, 1 - me.t)
    for k in range(1, dp):
        j, back = lax.rem(me.i + k, dp), lax.rem(me.i + dp - k, dp)
        if k <= early:
            arriving.append(pltpu.make_async_copy(cota_ref.at[back], cots_ref.at[back], c_ss.at[k]))
        else:
            arriving.append(remote(cot_ref.at[mine + j], cots_ref.at[me.i], c_ss.at[k], c_rs.at[k], (j, me.t)))
        leaving[k] = remote(out_ref.at[j], home_ref.at[mine + me.i], h_ss.at[k], h_rs.at[k], (j, me.t))
        if k in turns[0] + turns[1]:
            passing[k] = remote(home_ref.at[mine + back], home_ref.at[mine + back], f_ss.at[k], f_rs.at[k], partner)
    kept = pltpu.make_async_copy(out_ref.at[me.i], home_ref.at[mine + me.i], local.at[1])
    across = remote(out_ref.at[me.i], home_ref.at[mine + me.i], f_ss.at[0], f_rs.at[0], partner)
    start_all(arriving)
    bo, g1, s1, bf, g2, s2 = [
        r[...].astype(F32).reshape(1, width) for r in (bo_in, g1_in, s1_in, bf_in, g2_in, s2_in)]
    bi = [side_row(small_ref, t, ROWS_BI, units // 128) for t in range(tn)]
    vec_ref[...] = jnp.zeros_like(vec_ref)
    bsum_ref[...] = jnp.zeros_like(bsum_ref)

    def rows_at(i):
        return pl.ds(pl.multiple_of(i * size, size), size)

    def forward(i, carry):
        at = rows_at(i)
        attn = bo + x_ref[at, :].astype(F32)
        for t in range(tn):
            attn = attn + nt(ctx_ref[at, t * cols : (t + 1) * cols], wo_ref[t])
        n1, rstd1 = norm_parts(attn)
        n1_ref[at, :] = n1
        rs1_ref[at, :] = rstd1
        hidden = n1 * g1 + s1
        hid = hidden.astype(BF)
        hid_ref[at, :] = hid
        r2 = hidden + bf
        for t in range(tn):
            for c in range(0, units, chunk):
                own = slice(t * units + c, t * units + c + chunk)
                act, gp = gelu_both(nn(hid, wi_ref[t, :, c : c + chunk]) + bi[t][:, c : c + chunk])
                act_ref[at, own] = act.astype(BF)
                gi_ref[at, own] = gp.astype(BF)
        for t in range(tn):
            r2 = r2 + nt(act_ref[at, t * units : (t + 1) * units], wf_ref[t])
        n2, rstd2 = norm_parts(r2)
        n2_ref[at, :] = n2
        rs2_ref[at, :] = rstd2
        out_ref[pl.ds(i * per, per)] = (n2 * g2 + s2).reshape(per, part, width).astype(BF)
        return carry

    def backward(i, carry):
        at = rows_at(i)
        cot = cots_ref[pl.ds(i * per, per)].astype(F32).reshape(size, width)
        n2 = n2_ref[at, :]
        gr2 = norm_back(cot * g2, n2, rs2_ref[at, :])
        vec_ref[5] += fold(cot)
        vec_ref[4] += fold(cot * n2)
        vec_ref[3] += fold(gr2)
        low = gr2.astype(BF)
        gr2_ref[at, :] = low
        for t in range(tn):
            for c in range(0, units, chunk):
                own = slice(t * units + c, t * units + c + chunk)
                gi = nn(low, wf_ref[t, :, c : c + chunk]) * gi_ref[at, own].astype(F32)
                bsum_ref[:, own] += fold(gi)
                gi_ref[at, own] = gi.astype(BF)
        gh = gr2
        for t in range(tn):
            gh = gh + nt(gi_ref[at, t * units : (t + 1) * units], wi_ref[t])
        n1 = n1_ref[at, :]
        gr1 = norm_back(gh * g1, n1, rs1_ref[at, :])
        vec_ref[2] += fold(gh)
        vec_ref[1] += fold(gh * n1)
        vec_ref[0] += fold(gr1)
        low1 = gr1.astype(BF)
        gr1_ref[at, :] = low1
        for t in range(tn):
            dc_ref[at, t * cols : (t + 1) * cols] = nn(low1, wo_ref[t]).astype(BF)
        return carry

    wait_all(loads)
    lax.fori_loop(0, length // size, forward, 0)
    start_all([leaving[k] for k in turns[0]])
    kept.start()
    across.start()
    wait_all(arriving)
    n_back = length // size
    for i in range(n_back):
        backward(i, 0)
        if i == n_back // 2 - 1:
            start_all([leaving[k] for k in turns[1]])
            for k in turns[0]:
                leaving[k].wait()
                passing[k].start()
    start_all([leaving[k] for k in turns[2]])
    for k in turns[1]:
        leaving[k].wait()
        passing[k].start()
    start_all([leaving[k] for k in turns[3]])

    outs = [Fetch(gr1_ref, gr1_out, move.at[5]).start(), Fetch(dc_ref, dc_out, move.at[6]).start()]
    turn_ref[...] = turn(gr2_ref[...])
    for t in range(tn):
        for c in range(0, units, chunk):
            own = slice(t * units + c, t * units + c + chunk)
            dwf_ref[t, :, c : c + chunk] = nn(turn_ref[...], act_ref[:, own]).astype(BF)
    outs.append(Fetch(dwf_ref, dwf_out, move.at[7]).start())
    turn_ref[...] = turn(hid_ref[...])
    for t in range(tn):
        for c in range(0, units, chunk):
            own = slice(t * units + c, t * units + c + chunk)
            dwi_ref[t, :, c : c + chunk] = nn(turn_ref[...], gi_ref[:, own]).astype(BF)
    outs.append(Fetch(dwi_ref, dwi_out, move.at[8]).start())
    turn_ref[...] = turn(gr1_ref[...])
    for t in range(tn):
        dwo_ref[t] = nn(turn_ref[...], ctx_ref[:, t * cols : (t + 1) * cols]).astype(BF)
    outs.append(Fetch(dwo_ref, dwo_out, move.at[9]).start())
    wait_all([leaving[k] for k in turns[2] + turns[3]])
    kept.wait()
    across.wait()
    wait_all(passing.values())
    wait_all(outs)


def call_feed(dp, x, ctx, wo, wi, wf, vectors, small, cot, cota):
    length, width = x.shape
    tn, _, cols = wo.shape
    units = wi.shape[2]
    s = jax.ShapeDtypeStruct
    big = s((length, width), BF)
    blocks = (dp,) + cot.shape[1:]
    outs = (big, big, s((tn, width, cols), BF), s((tn, width, units), BF), s((tn, width, units), BF),
            s((6, 8, width), F32), s((8, tn * units), F32), s((tn * dp,) + blocks[1:], BF))
    vm = pltpu.VMEM
    return pl.pallas_call(
        functools.partial(feed, dp),
        out_shape=outs,
        in_specs=[ANY] * 5 + [VM] * 7 + [ANY] * 2,
        out_specs=tuple([ANY] * 5 + [VM] * 2 + [ANY]),
        scratch_shapes=[vm((length, tn * units), BF), vm((length, tn * units), BF), vm((length, width), BF),
                        vm((length, width), BF), vm((width, length), BF), vm((length, width), F32),
                        vm((length, width), F32), vm((length, 1), F32), vm((length, 1), F32), vm(blocks, BF),
                        vm(blocks, BF)] + [vm(o.shape, o.dtype) for o in (x, ctx, wo, wi, wf) + outs[:5]]
        + sems(dp) * 3 + [DMA((2,)), DMA((10,))],
        compiler_params=params(2, TOP),
        name="feed_forward",
    )(x, ctx, wo, wi, wf, *vectors, small, cot, cota)


NORTH_LANES = (1, 3, 5, 7)
BACK_CUT = 384
BACK_LAG = 4
SIDE_FIRST = 4
BACK_TICKS = (4, 1, 1, 2, 2, 2, 2, 1)


def staggered(lanes, lag):
    steps = []
    for step in range(len(lanes) + 2 * lag):
        todo = []
        for stage in (3, 2, 1):
            k = step - (stage - 1) * lag
            if 0 <= k < len(lanes):
                todo.append(lanes[k][stage])
        steps.append(todo)
    return steps


def row_of(column):
    return turn(jnp.broadcast_to(column, (column.shape[0], 128)))[0:1, :]


def attend_backward(dp, ids_ref, small_ref, lq_ref, lk_ref, mix_ref, sum_ref, ker_ref,
                    x_in, w_in, q_in, k_in, v_in, near_in, far_in, z_in, a_in, v2_in, w2_in, dc_in, gr1_in,
                    dwo_in, dwi_in, dwf_in, home_in,
                    gtok_ref, dw_ref, vecs_ref, gtap_ref, go_ref, gi_ref, gf_ref, home_ref,
                    x_ref, w_ref, q_ref, k_ref, v_ref, near_ref, far_ref, z_ref, a_ref, v2_ref, w2_ref, dc_ref, gr1_ref,
                    pre_ref, glq_ref, glk_ref, gsum_ref, gz_ref, gk_ref, padv_ref, padc_ref, xt_ref,
                    g_ss, g_rs, y_ss, y_rs, local, move, *bufs, carry=None):
    near_l, dc_l, z_l, a_l, v2_l, w2_l, far_l, q_l, k_l, v_l, x_l, w_l, gr1_l = [
        Fetch(a, b, move.at[k]).start() for k, (a, b) in enumerate((
            (near_in, near_ref), (dc_in, dc_ref), (z_in, z_ref), (a_in, a_ref), (v2_in, v2_ref), (w2_in, w2_ref),
            (far_in, far_ref), (q_in, q_ref), (k_in, k_ref), (v_in, v_ref), (x_in, x_ref), (w_in, w_ref), (gr1_in, gr1_ref)))]
    length, width = x_ref.shape
    tn = w_ref.shape[0]
    cols = width // tn
    scale = LAND ** -0.25
    size = length // dp
    pairs = width // 128
    groups = width // 256
    me = Place(dp, tn)
    n = reduce_count(dp)
    plan = []
    for src, dst in ((dwf_in, gf_ref), (dwi_in, gi_ref), (dwo_in, go_ref)):
        plan += [(src, lo, BACK_CUT, dst) for lo in range(0, src.shape[5], BACK_CUT)]
    lanes = []
    for k, (src, lo, w, dst) in enumerate(plan):
        lanes.append(reduce_lane(me, src, lo, w, bufs[5 * k : 5 * k + 5], Sub(g_ss, k * n), Sub(g_rs, k * n), local.at[k],
                                 [(dst, lo, 0, w)], k in NORTH_LANES))
    sides = []
    for k in waves(dp)[2] + waves(dp)[3]:
        j = me.t * dp + lax.rem(me.i + dp - k, dp)
        sides.append(remote(home_ref.at[j], home_ref.at[j], y_ss.at[k], y_rs.at[k], (me.i, 1 - me.t)))
    greet(me, carry is not None)
    for lane in lanes:
        lane[0]()
    steps = staggered(lanes, BACK_LAG)
    for k, side in enumerate(sides):
        steps[min(SIDE_FIRST + k, len(steps) - 1)].append(side.start)
    tick = Ticks([together(step) for step in steps])
    ids = ids_ref[pl.ds(own_sequence(), 1), :]
    member = jnp.where(lax.broadcasted_iota(jnp.int32, (LAND, length), 0) == ids, 1.0, 0.0).astype(F32)
    count = jnp.sum(member, axis=1, keepdims=True)
    member = member.astype(BF)
    valid = ids < LAND
    eye = pair_eye()

    near_l.wait()
    dc_l.wait()
    for g in range(groups):
        own = slice(g * 256, (g + 1) * 256)
        gsum_ref[:, own] = gather_diag(nn(near_ref[own, :], dc_ref[:, own]))
    tick(BACK_TICKS[0])
    wait_all([z_l, a_l, v2_l, w2_l])
    for p in range(pairs):
        own = slice(p * 128, (p + 1) * 128)
        gmix = gsum_ref[:, own]
        gz_ref[:, own] = pair_nt(gmix, sum_ref[:, own])
        gsum_ref[:, own] = pair_nn(pair_turn(z_ref[ITERS, :, own]), gmix)

    tick(BACK_TICKS[1])
    gk_ref[...] = jnp.zeros_like(gk_ref)

    def iterate(m, carry):
        n = ITERS - 1 - m
        for p in range(pairs):
            own = slice(p * 128, (p + 1) * 128)
            grad = 0.25 * gz_ref[:, own]
            kernel = ker_ref[:, own]
            z = z_ref[n, :, own]
            a = a_ref[n, :, own]
            v2 = v2_ref[n, :, own]
            w2 = w2_ref[n, :, own]
            dw2 = pair_nn(pair_turn(z), grad)
            at = pair_turn(a)
            dv2 = -pair_nn(at, dw2)
            da = -pair_nt(dw2, v2) - pair_nt(dv2, 7.0 * eye - a) + pair_nn(at, dv2)
            gk_ref[:, own] += pair_nt(da, z)
            gz_ref[:, own] = pair_nt(grad, w2) + pair_nn(pair_turn(kernel), da)
        return carry

    lax.fori_loop(0, ITERS // 2, iterate, 0)
    tick(BACK_TICKS[2])
    lax.fori_loop(ITERS // 2, ITERS, iterate, 0)
    tick(BACK_TICKS[3])
    wait_all([far_l, q_l, k_l, v_l])

    for p in range(pairs):
        own = slice(p * 128, (p + 1) * 128)
        kernel = ker_ref[:, own]
        gz = gz_ref[:, own]
        total = jnp.sum(pair_sum(kernel * kernel), axis=0, keepdims=True)
        kt = pair_turn(kernel)
        back = jnp.sum(pair_sum(gz * kt), axis=0, keepdims=True)
        gk = gk_ref[:, own] + pair_turn(gz) / total - kernel * (2.0 * back / (total * total))
        mid = kernel * (gk - pair_sum(kernel * gk))
        glq_ref[:, own] = pair_nn(mid, lk_ref[:, own].astype(F32))
        glk_ref[:, own] = pair_nn(pair_turn(mid), lq_ref[:, own].astype(F32))

    flip = jnp.where(
        lax.broadcasted_iota(jnp.int32, (256, 256), 0) + lax.broadcasted_iota(jnp.int32, (256, 256), 1) == 255, 1.0, 0.0
    ).astype(BF)
    taps = [reversed_taps(tap_rows(small_ref, t)) for t in range(tn)]
    padv_ref[...] = jnp.zeros_like(padv_ref)
    padc_ref[...] = jnp.zeros_like(padc_ref)
    inner = slice(128, 128 + length)
    for g in range(groups):
        own = slice(g * 256, (g + 1) * 256)
        lk4 = spread(lk_ref[:, own])
        lq4 = spread(lq_ref[:, own])
        near = near_ref[own, :].astype(F32)
        gnear = nt(spread(mix_ref[:, own]), dc_ref[:, own])
        drop = jnp.sum((near * gnear).reshape(4, LAND, length), axis=1, keepdims=True)
        first = (near * (gnear.reshape(4, LAND, length) - drop).reshape(256, length)).astype(BF)
        glk_ref[:, own] += gather_diag(nn(first, q_ref[:, own]))
        gsum4 = spread(gsum_ref[:, own].astype(BF))
        far = far_ref[own, :].astype(F32)
        gfar = nt(gsum4, v_ref[:, own])
        drop = jnp.sum(far * gfar, axis=1, keepdims=True)
        third = (far * (gfar - drop)).astype(BF)
        glq_ref[:, own] += gather_diag(nn(third, k_ref[:, own]))
        glq = turn((glq_ref[:, own] / count).astype(BF))
        glk = turn((glk_ref[:, own] / count).astype(BF))
        dq = (nn(turn(lk4), first) + nn(glq, member)) * scale
        dk = (nn(turn(lq4), third) + nn(glk, member)) * scale
        dv = nn(turn(gsum4), far_ref[own, :])

        vt = turn(v_ref[:, own])
        padv_ref[:, inner] = jnp.where(valid, vt, jnp.zeros_like(vt))
        padc_ref[:, inner] = turn(dc_ref[:, own])
        parts = []
        for h in range(4):
            band = band_of(taps, 4 * g + h)
            parts.append(unblock(nt(blocks_of(padc_ref, h * LAND, 256), band), 256))
            plain = jnp.concatenate(
                [padc_ref[h * LAND : (h + 1) * LAND, 128 + at : 128 + at + 256] for at in range(0, length, 256)], axis=0
            )
            gram = nn(nt(flip, plain).astype(BF), blocks_of(padv_ref, h * LAND, 256))
            gram = pltpu.roll(gram, 0, 1, stride=1, stride_axis=0)
            gtap_ref[4 * g + h : 4 * g + h + 1, :] = jnp.sum(gram, axis=0, keepdims=True)
        dv = dv + jnp.where(valid, jnp.concatenate(parts, axis=0), 0.0)
        vecs_ref[0:1, own] = row_of(jnp.sum(dq, axis=1, keepdims=True))
        vecs_ref[1:2, own] = row_of(jnp.sum(dv, axis=1, keepdims=True))
        for lower in range(0, 256, 128):
            c = g * 256 + lower
            t, r = c // cols, c % cols
            pre_ref[t, r : r + 128, :] = dq[lower : lower + 128].astype(BF)
            pre_ref[t, cols + r : cols + r + 128, :] = dk[lower : lower + 128].astype(BF)
            pre_ref[t, 2 * cols + r : 2 * cols + r + 128, :] = dv[lower : lower + 128].astype(BF)
        tick(BACK_TICKS[4 + g])

    wait_all([x_l, w_l, gr1_l])

    def weight_grads():
        xt_ref[...] = turn(x_ref[...])
        for t in range(tn):
            dw = nt(xt_ref[...], pre_ref[t])
            if carry:
                dw = dw.reshape(dw_ref.shape[1:])
            dw_ref[t] = dw.astype(BF)

    def token_grads():
        for at in range(0, length, 256):
            part = nn(w_ref[0], pre_ref[0, :, at : at + 256])
            for t in range(1, tn):
                part = part + nn(w_ref[t], pre_ref[t, :, at : at + 256])
            gtok_ref[at // size : (at + 256) // size] = (
                (gr1_ref[at : at + 256, :].astype(F32) + turn(part)).reshape(256 // size, size, width).astype(BF)
            )

    if carry:
        token_grads()
        carry.send_rows()
        tick(BACK_TICKS[7])
        weight_grads()
        carry.send_grads()
        carry.pack()
        carry.finish(tick.stages)
    else:
        weight_grads()
        tick(1)
        token_grads()
        tick.rest()
    for lane in lanes:
        lane[4]()
    wait_all(sides)


def end(dp, *refs):
    ins, refs = refs[:26], refs[26:]
    vec, bsum = ins[24:]
    go, gi, gf, home, g_home, gq, gk, gv, gbq, gbv, gtaps, gbi, *refs = refs
    n_outs, refs = refs[:6], refs[6:]
    gtok, dw, vecs, gtap, *refs = refs
    count = 13 + 9 + 6
    own, refs = refs[:count], refs[count:]
    n_bufs = len(refs) - 15 - 15
    bufs, refs = refs[:n_bufs], refs[n_bufs:]
    me = Place(dp, gtap.shape[0] // HEADS_HERE)
    carry = Carry(me, gtok, dw, vec, bsum, vecs, gtap, g_home, gq, gk, gv, gbq, gbv, gtaps, gbi, n_outs, *refs[:15], refs[15:])
    attend_backward(dp, *ins[:24], gtok, dw, vecs, gtap, go, gi, gf, home, *own, *bufs, carry=carry)


def call_end(dp, x, w, ids, small, saved, dc, gr1, dwo, dwi, dwf, home, vec, bsum, taps):
    q, k, v, near, far, lq, lk, mix, summ, ker, z, a, v2, w2 = saved
    length, width = x.shape
    tn = w.shape[0]
    cols = width // tn
    s = jax.ShapeDtypeStruct
    vm = pltpu.VMEM
    depth, units = dwi.shape[4:]
    share = s((depth, cols), F32)
    outs = (share, s((depth, units), F32), s((depth, units), F32), s(home.shape, BF), s(home.shape, BF), share, share, share,
            s((cols,), F32), s((cols,), F32), s(taps.shape, F32), s((units,), F32)) + (s((depth,), F32),) * 6
    little = (ids, small, lq, lk, mix, summ, ker)
    large = (x, w, q, k, v, near, far, z, a, v2, w2, dc, gr1)
    args = little + large + (dwo, dwi, dwf, home, vec, bsum)
    mini = vm((LAND, width), F32)
    n_lanes = (2 * units + cols) // BACK_CUT
    n = n_lanes * reduce_count(dp)
    scratch = [vm((dp,) + home.shape[1:], BF), vm((tn, dp // 4, 2, 2, depth, 3 * cols), BF), vm((8, width), F32),
               vm((width // LAND, 512), F32)]
    scratch += [vm(b.shape, b.dtype) for b in large] + [vm((tn, 3 * cols, length), BF)] + [mini] * 5
    scratch += [vm((256, length + 256), BF), vm((256, length + 256), BF), vm((width, length), BF)]
    scratch += sems(n) + sems(dp) + [DMA((n_lanes,)), DMA((len(large),))]
    for k in range(n_lanes):
        scratch += reduce_bufs(dp, tn, depth, BACK_CUT, k in NORTH_LANES)
    scratch += carry_scratch(dp, tn, depth, cols)
    return pl.pallas_call(
        functools.partial(end, dp),
        out_shape=outs,
        in_specs=[VM] * len(little) + [ANY] * (len(large) + 4) + [VM] * 2,
        out_specs=tuple([VM] * 3 + [ANY] * 2 + [VM] * 13),
        scratch_shapes=scratch,
        input_output_aliases={len(args) - 3: 3},
        compiler_params=params(6, TOP),
        name="end",
    )(*args)


def call_attend_backward(dp, x, w, ids, small, saved, dc, gr1, dwo, dwi, dwf, home):
    q, k, v, near, far, lq, lk, mix, summ, ker, z, a, v2, w2 = saved
    length, width = x.shape
    tn = w.shape[0]
    cols = width // tn
    s = jax.ShapeDtypeStruct
    depth, units = dwi.shape[4:]
    outs = (s((dp,) + home.shape[1:], BF), s((tn, width, 3 * cols), BF), s((8, width), F32),
            s((width // LAND, 512), F32), s((depth, cols), F32), s((depth, units), F32), s((depth, units), F32),
            s(home.shape, BF))
    little = (ids, small, lq, lk, mix, summ, ker)
    large = (x, w, q, k, v, near, far, z, a, v2, w2, dc, gr1)
    args = little + large + (dwo, dwi, dwf, home)
    vm = pltpu.VMEM
    mini = vm((LAND, width), F32)
    n_lanes = (2 * units + cols) // BACK_CUT
    n = n_lanes * reduce_count(dp)
    scratch = [vm(b.shape, b.dtype) for b in large] + [vm((tn, 3 * cols, length), BF)] + [mini] * 5
    scratch += [vm((256, length + 256), BF), vm((256, length + 256), BF), vm((width, length), BF)]
    scratch += sems(n) + sems(dp) + [DMA((n_lanes,)), DMA((len(large),))]
    for k in range(n_lanes):
        scratch += reduce_bufs(dp, tn, depth, BACK_CUT, k in NORTH_LANES)
    return pl.pallas_call(
        functools.partial(attend_backward, dp),
        out_shape=outs,
        in_specs=[VM] * len(little) + [ANY] * (len(args) - len(little)),
        out_specs=tuple([VM] * 7 + [ANY]),
        scratch_shapes=scratch,
        input_output_aliases={len(args) - 1: 7},
        compiler_params=params(3, TOP),
        name="attend_backward",
    )(*args)


def finish(n, *refs):
    ins, outs, held, sem = refs[:n], refs[n : 2 * n], refs[2 * n : 3 * n], refs[3 * n]
    loads = [pltpu.make_async_copy(a, b, sem.at[k]) for k, (a, b) in enumerate(zip(ins, held))]
    writes = [pltpu.make_async_copy(a, b, sem.at[n + k]) for k, (a, b) in enumerate(zip(held, outs))]
    start_all(loads)
    for a, b in zip(loads, writes):
        a.wait()
        b.start()
    wait_all(writes)


def call_finish(arrays):
    n = len(arrays)
    return pl.pallas_call(
        functools.partial(finish, n),
        out_shape=tuple(jax.ShapeDtypeStruct(a.shape, a.dtype) for a in arrays),
        in_specs=[ANY] * n,
        out_specs=(ANY,) * n,
        scratch_shapes=[pltpu.VMEM(a.shape, a.dtype) for a in arrays] + [DMA((2 * n,))],
        compiler_params=pltpu.CompilerParams(vmem_limit_bytes=TOP * 2**20),
        name="finish",
    )(*arrays)


def local(tokens, cotangent, landmark_ids, w_query, w_key, w_value, b_query, b_value, conv_taps, w_out, b_out,
          first_gain, first_shift, w_inner, b_inner, w_outer, b_outer, second_gain, second_shift):
    dp = lax.axis_size("dp")
    tn = lax.axis_size("tensor")
    part, width = tokens.shape[1:]
    length = dp * part
    cols = w_query.shape[1]
    vectors = [b_out, first_gain, first_shift, b_outer, second_gain, second_shift]

    def join(w):
        return w.reshape(tn, width, w.shape[-1])

    def cut(g):
        return g.reshape(tn, dp // 4, 2, 2, width // dp, g.shape[2])

    joined = width // dp % 16 == 0 and part % 16 == 0
    if joined:
        rows, wqkv, wout, small, *done = call_begin(
            dp, tn, tokens, w_query, w_key, w_value, w_out, b_query, b_value, b_inner, conv_taps,
            landmark_ids, w_inner, w_outer, cotangent)
    else:
        rows, wqkv, wout, small = call_bring(
            dp, tn, tokens, w_query, w_key, w_value, w_out, b_query, b_value, b_inner, conv_taps)
        done = call_attend_forward(
            dp, rows.reshape(length, width), join(wqkv), small, landmark_ids, w_inner, w_outer, cotangent)
    rows = rows.reshape(length, width)
    wqkv, wout = join(wqkv), join(wout)
    q, k, v, near, far, ctx, *rest_saved, wi, wf, cota = done
    gr1, dc, dwo, dwi, dwf, vec, bsum, home = call_feed(
        dp, rows, ctx, wout, join(wi), join(wf), vectors, small, cotangent, cota
    )
    back = (dp, rows, wqkv, landmark_ids, small, (q, k, v, near, far, *rest_saved), dc, gr1, cut(dwo), cut(dwi), cut(dwf), home)
    if joined:
        go, gi, gf, out_home, *ends = call_end(*back, vec, bsum, conv_taps)
    else:
        grad_rows, dwqkv, vecs, gtap, go, gi, gf, out_home = call_attend_backward(*back)
        ends = call_carry_home(dp, tn, grad_rows, cut(dwqkv), vec, bsum, vecs, gtap, conv_taps)
    grad_home, gq, gk, gv, gbq, gbv, gtaps, gbi, gbo, gg1, gs1, gbf, gg2, gs2 = ends
    return call_finish((out_home, grad_home, gq, gk, gv, gbq, gbv, gtaps, go, gbo, gg1, gs1, gi, gbi, gf, gbf, gg2, gs2))


def solution(mesh):
    return jax.shard_map(
        local,
        mesh=mesh,
        in_specs=(
            P(None, "dp", None),
            P(None, "dp", None),
            P(),
            P("dp", "tensor"),
            P("dp", "tensor"),
            P("dp", "tensor"),
            P("tensor"),
            P("tensor"),
            P("tensor", None),
            P("dp", "tensor"),
            P(),
            P(),
            P(),
            P("dp", "tensor"),
            P("tensor"),
            P("dp", "tensor"),
            P(),
            P(),
            P(),
        ),
        out_specs=(
            P(None, "dp", None),
            P(None, "dp", None),
            P("dp", "tensor"),
            P("dp", "tensor"),
            P("dp", "tensor"),
            P("tensor"),
            P("tensor"),
            P("tensor", None),
            P("dp", "tensor"),
            P("dp"),
            P("dp"),
            P("dp"),
            P("dp", "tensor"),
            P("tensor"),
            P("dp", "tensor"),
            P("dp"),
            P("dp"),
            P("dp"),
        ),
        check_vma=False,
    )
```

```python
import functools

import jax
import jax.numpy as jnp
from jax import lax
from jax.experimental import pallas as pl
from jax.experimental.pallas import tpu as pltpu
from jax.sharding import PartitionSpec as P

F32 = jnp.float32
BF = jnp.bfloat16
MESH = pl.DeviceIdType.MESH
ANY = pl.BlockSpec(memory_space=pl.ANY)
TOP = 62
VM = pl.BlockSpec(memory_space=pltpu.VMEM)
DMA = pltpu.SemaphoreType.DMA
SMALL_ROWS = 32


class Place:
    def __init__(self, dp, tn):
        self.dp, self.tn = dp, tn
        self.nz = dp // 4
        i = lax.axis_index("dp")
        self.i = i
        self.t = lax.axis_index("tensor")
        self.c = lax.rem(i, 2)
        self.x = lax.rem(i // 2, 2)
        self.z = i // 4

    def at(self, z=None, x=None, c=None, t=None):
        z = self.z if z is None else z
        x = self.x if x is None else x
        c = self.c if c is None else c
        t = self.t if t is None else t
        return (z * 4 + x * 2 + c, t)


def greet(me, rows=True):
    bar = pltpu.get_barrier_semaphore()
    if rows:
        peers = [(lax.rem(me.i + k, me.dp), me.t) for k in range(1, me.dp)]
    else:
        peers = [me.at(z=lax.rem(me.z + k, me.nz)) for k in range(1, me.nz)] + [me.at(x=1 - me.x), me.at(c=1 - me.c)]
    peers.append((me.i, 1 - me.t))
    for p in peers:
        pl.semaphore_signal(bar, 1, device_id=p, device_id_type=MESH)
    pl.semaphore_wait(bar, len(peers))


def remote(src, dst, ss, rs, to):
    return pltpu.make_async_remote_copy(
        src_ref=src, dst_ref=dst, send_sem=ss, recv_sem=rs, device_id=to, device_id_type=MESH
    )


def start_all(copies):
    for c in copies:
        c.start()


def wait_all(copies):
    for c in copies:
        c.wait()


def to_owner(me, src, out, ss, rs, local):
    copies = []
    for k in range(1, me.dp):
        j = lax.rem(me.i + k, me.dp)
        copies.append(remote(src.at[me.t * me.dp + j], out.at[me.i], ss.at[k], rs.at[k], (j, me.t)))
    copies.append(pltpu.make_async_copy(src.at[me.t * me.dp + me.i], out.at[me.i], local))
    return copies


def to_home(me, src, out, ss, rs, local):
    copies = []
    for k in range(1, me.dp):
        j = lax.rem(me.i + k, me.dp)
        copies.append(remote(src.at[j], out.at[me.i], ss.at[k], rs.at[k], (j, me.t)))
    copies.append(pltpu.make_async_copy(src.at[me.i], out.at[me.i], local))
    return copies


def gather_lane(me, src, own, out, cols, north_first, ss, rs, local):
    t, z, x, c, n = me.t, me.z, me.x, me.c, me.nz
    px, py, sib = me.at(x=1 - x), me.at(t=1 - t), me.at(c=1 - c)

    def move(ref, k, to):
        return remote(ref, ref, ss.at[k], rs.at[k], to)

    zs = [pltpu.make_async_copy(src.at[:, own], out.at[t, z, x, c, :, cols], local)]
    for k in range(1, n):
        to = me.at(z=lax.rem(z + k, n))
        zs.append(remote(src.at[:, own], out.at[t, z, x, c, :, cols], ss.at[k], rs.at[k], to))
    if north_first:
        first, second = move(out.at[t, :, x, c, :, cols], n, py), move(out.at[:, :, x, c, :, cols], n + 1, px)
        d2, d3 = move(out.at[:, :, x, c, :, cols], n + 2, sib), move(out.at[:, :, 1 - x, c, :, cols], n + 3, sib)
    else:
        first, second = move(out.at[t, :, x, c, :, cols], n, px), move(out.at[t, :, :, c, :, cols], n + 1, py)
        d2, d3 = move(out.at[t, :, :, c, :, cols], n + 2, sib), move(out.at[1 - t, :, :, c, :, cols], n + 3, sib)

    def s0():
        start_all(zs)

    def s1():
        wait_all(zs)
        first.start()

    def s2():
        first.wait()
        second.start()
        d2.start()

    def s3():
        second.wait()
        d3.start()

    def s4():
        d2.wait()
        d3.wait()

    return [s0, s1, s2, s3, s4]


def gather_count(dp):
    return dp // 4 + 4


def add_low(a, b):
    return (a.astype(F32) + b.astype(F32)).astype(BF)


def reduce_lane(me, src, lo, w, bufs, ss, rs, local, puts, north_first=False):
    t, z, x, c, n = me.t, me.z, me.x, me.c, me.nz
    mine, rc, r1, r2, rz = bufs
    cols = pl.ds(lo, w)

    def move(a, b, q, to):
        return remote(a, b, ss.at[q], rs.at[q], to)

    keep = pltpu.make_async_copy(src.at[:, :, :, c, :, cols], mine, local)
    core = move(src.at[:, :, :, 1 - c, :, cols], rc, 0, me.at(c=1 - c))
    px, py = me.at(x=1 - x), me.at(t=1 - t)
    if north_first:
        first = move(rc.at[1 - t], r1, 1, py)
        second = move(r1.at[:, 1 - x], r2, 2, px)
    else:
        first = move(rc.at[:, :, 1 - x], r1, 1, px)
        second = move(r1.at[1 - t], r2, 2, py)
    lines = []
    for q in range(1, n):
        to = lax.rem(z + q, n)
        lines.append(move(r2.at[to], rz.at[q], 2 + q, me.at(z=to)))

    def s0():
        keep.start()
        core.start()

    def s1():
        keep.wait()
        core.wait()
        rc[...] = add_low(rc[...], mine[...])
        first.start()

    def s2():
        first.wait()
        r1[...] = add_low(r1[...], rc[t] if north_first else rc[:, :, x])
        second.start()

    def s3():
        second.wait()
        r2[...] = add_low(r2[...], r1[:, x] if north_first else r1[t])
        start_all(lines)

    def s4():
        total = r2[z].astype(F32)
        wait_all(lines)
        for q in range(1, n):
            total = total + rz[q].astype(F32)
        for dst, at, first_col, width in puts:
            dst[:, at : at + width] = total[:, first_col : first_col + width]

    return [s0, s1, s2, s3, s4]


def reduce_bufs(dp, tn, depth, w, north_first=False):
    nz = dp // 4
    one = (nz, 2) if north_first else (tn, nz)
    return [pltpu.VMEM((tn, nz, 2, depth, w), BF), pltpu.VMEM((tn, nz, 2, depth, w), BF),
            pltpu.VMEM(one + (depth, w), BF), pltpu.VMEM((nz, depth, w), BF), pltpu.VMEM((nz, depth, w), BF)]


def reduce_count(dp):
    return dp // 4 + 2


class Fetch:
    def __init__(self, src, dst, sem):
        self.copy, self.open = pltpu.make_async_copy(src, dst, sem), True

    def start(self):
        self.copy.start()
        return self

    def wait(self):
        if self.open:
            self.copy.wait()
        self.open = False


class Sub:
    def __init__(self, ref, base):
        self.ref, self.base = ref, base

    @property
    def at(self):
        return self

    def __getitem__(self, k):
        return self.ref.at[self.base + k]


def together(functions):
    def run():
        for f in functions:
            f()
    return run


class Ticks:
    def __init__(self, stages):
        self.stages = list(stages)

    def __call__(self, count=1):
        for _ in range(min(count, len(self.stages))):
            self.stages.pop(0)()

    def rest(self):
        self(len(self.stages))


def sems(n):
    return [DMA((n,)), DMA((n,))]


def params(cid, mib):
    return pltpu.CompilerParams(collective_id=cid, has_side_effects=True, vmem_limit_bytes=mib * 2**20)


def fill_piece(piece, bq, bv, bi, taps):
    piece[...] = jnp.zeros_like(piece)
    for ref, first in ((bq, ROWS_BQ), (bv, ROWS_BV), (bi, ROWS_BI)):
        line = ref[...].astype(F32).reshape(1, ref.shape[0])
        for r in range(ref.shape[0] // 128):
            piece[first + r : first + r + 1, :] = line[:, r * 128 : (r + 1) * 128]
    heads, width = taps.shape
    tap = taps[...].astype(F32)
    piece[ROWS_TAPS : ROWS_TAPS + heads, :width] = tap


def bring(dp, tn, tok, wq, wk, wv, wo, bq, bv, bi, taps, rows, wqkv, wout, small,
          r_ss, r_rs, g_ss, g_rs, local, piece):
    me = Place(dp, tn)
    cols = wq.shape[1]
    n = gather_count(dp)
    lanes = []
    for k, (src, dst, lo) in enumerate(((wq, wqkv, 0), (wk, wqkv, cols), (wv, wqkv, 2 * cols), (wo, wout, 0))):
        lanes.append(gather_lane(me, src, pl.ds(0, cols), dst, pl.ds(lo, cols), k % 2 == 1,
                                 Sub(g_ss, k * n), Sub(g_rs, k * n), local.at[k]))
    fill_piece(piece, bq, bv, bi, taps)
    greet(me)
    for s in (0, 1):
        for lane in lanes[2 * s : 2 * s + 2]:
            lane[0]()
    moved = to_owner(me, tok, rows, r_ss, r_rs, local.at[4])
    start_all(moved)
    side = [remote(piece, small.at[me.t], r_ss.at[0], r_rs.at[0], (me.i, 1 - me.t)),
            pltpu.make_async_copy(piece, small.at[me.t], local.at[5])]
    start_all(side)
    for pair, stage in ((0, 1), (0, 2), (1, 1), (0, 3), (1, 2), (1, 3), (0, 4), (1, 4)):
        for lane in lanes[2 * pair : 2 * pair + 2]:
            lane[stage]()
    wait_all(side)
    wait_all(moved)


def call_bring(dp, tn, tok, wq, wk, wv, wo, bq, bv, bi, taps):
    s = jax.ShapeDtypeStruct
    depth, cols = wq.shape
    lead = (tn, dp // 4, 2, 2, depth)
    outs = (s((dp,) + tok.shape[1:], BF), s(lead + (3 * cols,), BF), s(lead + (cols,), BF), s((tn, SMALL_ROWS, 128), F32))
    return pl.pallas_call(
        functools.partial(bring, dp, tn),
        out_shape=outs,
        in_specs=[ANY] * 5 + [VM] * 4,
        out_specs=(ANY, ANY, ANY, ANY),
        scratch_shapes=sems(dp) + sems(4 * gather_count(dp)) + [DMA((6,)), pltpu.VMEM((SMALL_ROWS, 128), F32)],
        compiler_params=params(0, TOP),
        name="bring",
    )(tok, wq, wk, wv, wo, bq, bv, bi, taps)


def carry_home(dp, tn, g_rows, dwqkv, vec, bsum, vecs, gtap, g_home, gq, gk, gv, gbq, gbv, gtaps, gbi, *refs):
    n_outs, (r_ss, r_rs, v_ss, v_rs, g_ss, g_rs, local, norms, rest, nbuf, rbuf, nall, rall, nsum, rsum) = refs[:6], refs[6:21]
    bufs = refs[21:]
    me = Place(dp, tn)
    greet(me)
    c = Carry(me, g_rows, dwqkv, vec, bsum, vecs, gtap, g_home, gq, gk, gv, gbq, gbv, gtaps, gbi, n_outs, r_ss, r_rs, v_ss, v_rs,
              g_ss, g_rs, local, norms, rest, nbuf, rbuf, nall, rall, nsum, rsum, bufs)
    c.send_rows()
    c.send_grads()
    c.pack()
    c.finish([])


class Carry:
    def __init__(self, me, g_rows, dwqkv, vec, bsum, vecs, gtap, g_home, gq, gk, gv, gbq, gbv, gtaps, gbi, n_outs, r_ss, r_rs,
                 v_ss, v_rs, g_ss, g_rs, local, norms, rest, nbuf, rbuf, nall, rall, nsum, rsum, bufs):
        self.me, self.sources = me, (vec, bsum, vecs, gtap)
        self.results = (gbq, gbv, gtaps, gbi, n_outs)
        self.v = (v_ss, v_rs, norms, rest, nbuf, rbuf, nall, rall, nsum, rsum)
        self.cols = cols = gq.shape[1]
        dp, n = me.dp, reduce_count(me.dp)
        self.lanes = []
        for k, dst in enumerate((gq, gk, gv)):
            self.lanes.append(reduce_lane(me, dwqkv, k * cols, cols, bufs[5 * k : 5 * k + 5], Sub(g_ss, k * n),
                                          Sub(g_rs, k * n), local.at[1 + k], [(dst, 0, 0, cols)]))
        mine = me.t * dp
        self.partner = partner = (me.i, 1 - me.t)
        self.first = []
        for k in range(1, dp):
            j = lax.rem(me.i + k, dp)
            self.first.append(remote(g_rows.at[j], g_home.at[mine + me.i], r_ss.at[k], r_rs.at[k], (j, me.t)))
        self.own = pltpu.make_async_copy(g_rows.at[me.i], g_home.at[mine + me.i], local.at[0])
        self.second = [remote(g_rows.at[me.i], g_home.at[mine + me.i], r_ss.at[dp], r_rs.at[dp], partner)]
        for k in range(1, dp):
            j = mine + lax.rem(me.i + dp - k, dp)
            self.second.append(remote(g_home.at[j], g_home.at[j], r_ss.at[dp + k], r_rs.at[dp + k], partner))

    def send_rows(self):
        self.turns = waves(self.me.dp)
        for k in self.turns[0] + self.turns[1]:
            self.first[k - 1].start()
        self.own.start()
        self.second[0].start()

    def send_grads(self):
        for lane in self.lanes:
            lane[0]()

    def pack(self):
        me = self.me
        dp, tn, cols = me.dp, me.tn, self.cols
        vec, bsum, vecs, gtap = self.sources
        gbq, gbv, gtaps, gbi, n_outs = self.results
        v_ss, v_rs, norms, rest, nbuf, rbuf, nall, rall, nsum, rsum = self.v
        share = n_outs[0].shape[0]
        six = jnp.sum(vec[...], axis=1)
        norms[...] = jnp.zeros_like(norms)
        rest[...] = jnp.zeros_like(rest)
        for j in range(dp):
            norms[j, 0:6, :share] = six[:, j * share : (j + 1) * share]
        units = jnp.sum(bsum[...], axis=0, keepdims=True)
        per, taps = gtaps.shape
        for t in range(tn):
            for line, first_row, size in ((vecs[0:1, :], ROWS_BQ, cols), (vecs[1:2, :], ROWS_BV, cols),
                                          (units, ROWS_BI, gbi.shape[0])):
                for r in range(size // 128):
                    lo = t * size + r * 128
                    rest[t, first_row + r : first_row + r + 1, :] = line[:, lo : lo + 128]
            rest[t, ROWS_TAPS : ROWS_TAPS + per, :taps] = gtap[t * per : (t + 1) * per, FLIP_AT : FLIP_AT + taps]
        self.v1 = [remote(norms, nbuf, v_ss.at[0], v_rs.at[0], self.partner),
                   remote(rest.at[1 - me.t], rbuf, v_ss.at[1], v_rs.at[1], self.partner)]
        start_all(self.v1)

    def finish(self, others):
        me = self.me
        dp = me.dp
        gbq, gbv, gtaps, gbi, n_outs = self.results
        v_ss, v_rs, norms, rest, nbuf, rbuf, nall, rall, nsum, rsum = self.v
        for lane in self.lanes:
            lane[1]()
        wait_all(self.v1)
        nsum[...] = norms[...] + nbuf[...]
        rsum[...] = rest[me.t] + rbuf[...]
        v2 = []
        for k in range(1, dp):
            j = lax.rem(me.i + k, dp)
            v2.append(remote(nsum.at[j], nall.at[k], v_ss.at[2 * k], v_rs.at[2 * k], (j, me.t)))
            v2.append(remote(rsum, rall.at[k], v_ss.at[2 * k + 1], v_rs.at[2 * k + 1], (j, me.t)))
        start_all(v2)
        stages = list(others) + [lane[s] for s in (2, 3) for lane in self.lanes]
        n = len(self.turns)
        for w, turn_ in enumerate(self.turns):
            for k in turn_:
                self.first[k - 1].wait()
                self.second[k].start()
            if w + 2 < n:
                start_all([self.first[k - 1] for k in self.turns[w + 2]])
            for _ in range(-(-len(stages) // (n - w))):
                stages.pop(0)()
        for st in stages:
            st()
        wait_all(v2)
        ntot = nsum[me.i]
        rtot = rsum[...]
        for k in range(1, dp):
            ntot = ntot + nall[k]
            rtot = rtot + rall[k]
        share = n_outs[0].shape[0]
        per, taps = gtaps.shape
        for k in range(6):
            n_outs[k][...] = ntot[k, :share]
        for ref, first_row in ((gbq, ROWS_BQ), (gbv, ROWS_BV), (gbi, ROWS_BI)):
            size = ref.shape[0]
            ref[...] = jnp.concatenate(
                [rtot[first_row + r : first_row + r + 1] for r in range(size // 128)], axis=1).reshape(size)
        gtaps[...] = rtot[ROWS_TAPS : ROWS_TAPS + per, :taps]
        for lane in self.lanes:
            lane[4]()
        self.own.wait()
        wait_all(self.second)


def carry_scratch(dp, tn, depth, cols):
    norms, rest = (dp, 8, 128), (tn, 24, 128)
    scratch = sems(2 * dp) + sems(2 * dp) + sems(3 * reduce_count(dp)) + [DMA((4,))]
    scratch += [pltpu.VMEM(norms, F32), pltpu.VMEM(rest, F32),
                pltpu.VMEM(norms, F32), pltpu.VMEM(rest[1:], F32),
                pltpu.VMEM((dp,) + norms[1:], F32), pltpu.VMEM((dp,) + rest[1:], F32),
                pltpu.VMEM(norms, F32), pltpu.VMEM(rest[1:], F32)]
    for _ in range(3):
        scratch += reduce_bufs(dp, tn, depth, cols)
    return scratch


def call_carry_home(dp, tn, g_rows, dwqkv, vec, bsum, vecs, gtap, taps):
    s = jax.ShapeDtypeStruct
    r, w = g_rows.shape[1:]
    depth, cols = dwqkv.shape[4], dwqkv.shape[5] // 3
    share = s((depth, cols), F32)
    outs = (s((tn * dp, r, w), BF), share, share, share, s((cols,), F32), s((cols,), F32), s(taps.shape, F32),
            s((bsum.shape[1] // tn,), F32)) + (s((depth,), F32),) * 6
    scratch = carry_scratch(dp, tn, depth, cols)
    return pl.pallas_call(
        functools.partial(carry_home, dp, tn),
        out_shape=outs,
        in_specs=[ANY, ANY] + [VM] * 4,
        out_specs=(ANY,) + (VM,) * 13,
        scratch_shapes=scratch,
        compiler_params=params(4, TOP),
        name="carry_home",
    )(g_rows, dwqkv, vec, bsum, vecs, gtap)


F32 = jnp.float32
BF = jnp.bfloat16
LAND = 64
ITERS = 6
HEADS_HERE = 6
ROWS_BQ, ROWS_BV, ROWS_BI, ROWS_TAPS = 0, 3, 6, 18
EDGE = 112
TAPS = 33
FLIP_AT = 367


def nn(a, b):
    return lax.dot_general(a, b, (((1,), (0,)), ((), ())), preferred_element_type=F32)


def nt(a, b):
    return lax.dot_general(a, b, (((1,), (1,)), ((), ())), preferred_element_type=F32)


def turn(a):
    return jnp.transpose(a, (1, 0))


def same_head(rows, columns):
    left = lax.broadcasted_iota(jnp.int32, (rows, columns), 0) // LAND
    right = lax.broadcasted_iota(jnp.int32, (rows, columns), 1) // LAND
    return left == right


def spread(small):
    n = small.shape[1] // LAND
    tall = jnp.concatenate([small] * n, axis=0)
    return jnp.where(same_head(n * LAND, n * LAND), tall, jnp.zeros_like(tall))


def gather_diag(full):
    n = full.shape[1] // LAND
    lane = lax.broadcasted_iota(jnp.int32, (LAND, full.shape[1]), 1) // LAND
    out = full[:LAND]
    for h in range(1, n):
        out = jnp.where(lane == h, full[h * LAND : (h + 1) * LAND], out)
    return out


def halves(a):
    high = a.astype(BF)
    return high, (a - high.astype(F32)).astype(BF)


def pair_nn(a, b):
    ah, al = halves(a)
    bh, bl = halves(b)
    bh, bl = spread(bh), spread(bl)
    wide = jnp.concatenate([bh, bl], axis=1)
    r = nn(jnp.concatenate([ah, al], axis=1), jnp.concatenate([wide, wide], axis=0))
    return r[:, : 2 * LAND] + r[:, 2 * LAND :]


def pair_nt(a, b):
    ah, al = halves(a)
    bh, bl = halves(b)
    bh, bl = spread(bh), spread(bl)
    tall = jnp.concatenate([bh, bl], axis=0)
    r = nt(jnp.concatenate([ah, al], axis=1), jnp.concatenate([tall, tall], axis=1))
    return r[:, : 2 * LAND] + r[:, 2 * LAND :]


def pair_turn(a):
    t = turn(a)
    return jnp.concatenate([t[:LAND], t[LAND:]], axis=1)


def pair_sum(a):
    left = lax.broadcasted_iota(jnp.int32, a.shape, 1) < LAND
    low = jnp.sum(jnp.where(left, a, 0.0), axis=1, keepdims=True)
    high = jnp.sum(jnp.where(left, 0.0, a), axis=1, keepdims=True)
    return jnp.where(left, low, high)


def pair_softmax(a):
    left = lax.broadcasted_iota(jnp.int32, a.shape, 1) < LAND
    low = jnp.max(jnp.where(left, a, -1e30), axis=1, keepdims=True)
    high = jnp.max(jnp.where(left, -1e30, a), axis=1, keepdims=True)
    e = jnp.exp(a - jnp.where(left, low, high))
    return e / pair_sum(e)


def pair_eye():
    r = lax.broadcasted_iota(jnp.int32, (LAND, 2 * LAND), 0)
    c = lax.broadcasted_iota(jnp.int32, (LAND, 2 * LAND), 1) % LAND
    return jnp.where(r == c, 1.0, 0.0).astype(F32)


def toeplitz(row, size, width):
    return pltpu.roll(jnp.broadcast_to(row, (size, width)), 0, 1, stride=1, stride_axis=0)


def blocks_of(ref, lower, block):
    length = ref.shape[1] - 256
    return jnp.concatenate(
        [ref[lower : lower + LAND, at : at + block + 256] for at in range(0, length, block)], axis=0
    )


def unblock(stacked, block):
    n = stacked.shape[0] // LAND
    return jnp.concatenate([stacked[i * LAND : (i + 1) * LAND] for i in range(n)], axis=1)


def own_sequence():
    return lax.axis_index("tensor") * lax.axis_size("dp") + lax.axis_index("dp")


def side_row(small_ref, t, first, count):
    return jnp.concatenate([small_ref[t, r : r + 1, :] for r in range(first, first + count)], axis=1)


def band_of(rows, head):
    h = head % HEADS_HERE
    row = jnp.concatenate([rows[head // HEADS_HERE][h : h + 1, :], jnp.zeros((1, 384), F32)], axis=1)
    return toeplitz(pltpu.roll(row, EDGE, 1), 256, 512).astype(BF)


def tap_rows(small_ref, t):
    return small_ref[t, ROWS_TAPS : ROWS_TAPS + 8, :]


def reversed_taps(rows):
    turned = jnp.where(
        lax.broadcasted_iota(jnp.int32, (128, 128), 0) + lax.broadcasted_iota(jnp.int32, (128, 128), 1) == TAPS - 1, 1.0, 0.0
    ).astype(BF)
    return nn(rows.astype(BF), turned)


def forward_core(rows_of, weight_of, tn, small_ref, ids_ref, q_ref, k_ref, v_ref, near_ref, far_ref, ctx_ref,
                 lq_ref, lk_ref, mix_ref, sum_ref, ker_ref, z_ref, a_ref, v2_ref, w2_ref, pad_ref, tick, ready, writes):
    length, width = q_ref.shape
    cols = width // tn
    scale = LAND ** -0.25
    rows_at = 256
    pairs = width // 128
    groups = width // 256
    q_w, k_w, v_w, near_w, far_w, ctx_w, z_w, a_w, v2_w, w2_w = writes
    ready()
    bq = [side_row(small_ref, t, ROWS_BQ, 3) for t in range(tn)]
    bv = [side_row(small_ref, t, ROWS_BV, 3) for t in range(tn)]

    def project(i, carry):
        at = pl.ds(pl.multiple_of(i * rows_at, rows_at), rows_at)
        for t in range(tn):
            out = nn(rows_of(at, i), weight_of(t))
            own = slice(t * cols, (t + 1) * cols)
            q_ref[at, own] = ((out[:, :cols] + bq[t]) * scale).astype(BF)
            k_ref[at, own] = (out[:, cols : 2 * cols] * scale).astype(BF)
            v_ref[at, own] = (out[:, 2 * cols :] + bv[t]).astype(BF)
        return carry

    lax.fori_loop(0, length // rows_at, project, 0)
    start_all([q_w, k_w, v_w])
    tick()

    ids = ids_ref[pl.ds(own_sequence(), 1), :]
    member = jnp.where(lax.broadcasted_iota(jnp.int32, (LAND, length), 0) == ids, 1.0, 0.0).astype(F32)
    count = jnp.sum(member, axis=1, keepdims=True)
    member = member.astype(BF)
    valid = ids < LAND
    lq_ref[...] = (nn(member, q_ref[...]) / count).astype(BF)
    lk_ref[...] = (nn(member, k_ref[...]) / count).astype(BF)

    eye = pair_eye()
    for p in range(pairs):
        own = slice(p * 128, (p + 1) * 128)
        scores = nt(lq_ref[:, own], spread(lk_ref[:, own]))
        kernel = pair_softmax(scores)
        ker_ref[:, own] = kernel
        left = lax.broadcasted_iota(jnp.int32, kernel.shape, 1) < LAND
        total = jnp.sum(pair_sum(kernel * kernel), axis=0, keepdims=True)
        z_ref[0, :, own] = pair_turn(kernel) / total
    tick()

    for g in range(groups):
        own = slice(g * 256, (g + 1) * 256)
        scores = nt(spread(lk_ref[:, own]), q_ref[:, own]).reshape(4, LAND, length)
        scores = jnp.exp(scores - jnp.max(scores, axis=1, keepdims=True))
        scores = scores / jnp.sum(scores, axis=1, keepdims=True)
        near_ref[own, :] = scores.reshape(256, length).astype(BF)
        scores = nt(spread(lq_ref[:, own]), k_ref[:, own])
        scores = jnp.where(valid, scores, -1e30)
        scores = jnp.exp(scores - jnp.max(scores, axis=1, keepdims=True))
        scores = scores / jnp.sum(scores, axis=1, keepdims=True)
        far_ref[own, :] = scores.astype(BF)
        sum_ref[:, own] = gather_diag(nn(far_ref[own, :], v_ref[:, own]))
        tick()
    start_all([near_w, far_w])

    def iterate(n, carry):
        for p in range(pairs):
            own = slice(p * 128, (p + 1) * 128)
            z = z_ref[n, :, own]
            a = pair_nn(ker_ref[:, own], z)
            v2 = 15.0 * eye - pair_nn(a, 7.0 * eye - a)
            w2 = 13.0 * eye - pair_nn(a, v2)
            a_ref[n, :, own] = a
            v2_ref[n, :, own] = v2
            w2_ref[n, :, own] = w2
            z_ref[n + 1, :, own] = 0.25 * pair_nn(z, w2)
        return carry

    lax.fori_loop(0, ITERS // 2, iterate, 0)
    tick()
    lax.fori_loop(ITERS // 2, ITERS, iterate, 0)
    start_all([z_w, a_w, v2_w, w2_w])
    tick()

    for p in range(pairs):
        own = slice(p * 128, (p + 1) * 128)
        mix_ref[:, own] = pair_nn(z_ref[ITERS, :, own], sum_ref[:, own]).astype(BF)

    pad_ref[...] = jnp.zeros_like(pad_ref)
    taps = [tap_rows(small_ref, t) for t in range(tn)]
    for g in range(groups):
        own = slice(g * 256, (g + 1) * 256)
        att = nn(turn(spread(mix_ref[:, own])), near_ref[own, :])
        vt = turn(v_ref[:, own])
        pad_ref[:, 128 : 128 + length] = jnp.where(valid, vt, jnp.zeros_like(vt))
        parts = []
        for h in range(4):
            band = band_of(taps, 4 * g + h)
            parts.append(unblock(nt(blocks_of(pad_ref, h * LAND, 256), band), 256))
        att = (att + jnp.concatenate(parts, axis=0)).astype(BF)
        ctx_ref[:, own] = turn(att)
        tick()


def attend_forward(dp, x_in, w_in, small_ref, ids_ref, wi_ref, wf_ref, cot_ref,
                   q_out, k_out, v_out, near_out, far_out, ctx_out, lq_ref, lk_ref, mix_ref, sum_ref, ker_ref,
                   z_out, a_out, v2_out, w2_out, wi_all, wf_all, cota_ref, pad_ref, x_ref, w_ref, q_ref, k_ref, v_ref,
                   near_ref, far_ref, ctx_ref, z_ref, a_ref, v2_ref, w2_ref, g_ss, g_rs, c_ss, c_rs, local, move):
    length, width = x_ref.shape
    tn = w_ref.shape[0]
    loads = [Fetch(x_in, x_ref, move.at[0]).start(), Fetch(w_in, w_ref, move.at[1]).start()]
    writes = [
        Fetch(a, b, move.at[2 + k]) for k, (a, b) in enumerate((
            (q_ref, q_out), (k_ref, k_out), (v_ref, v_out), (near_ref, near_out), (far_ref, far_out), (ctx_ref, ctx_out),
            (z_ref, z_out), (a_ref, a_out), (v2_ref, v2_out), (w2_ref, w2_out)))]
    me = Place(dp, tn)
    n = gather_count(dp)
    half = wi_ref.shape[1] // 2
    lanes = []
    for p, (src, dst) in enumerate(((wi_ref, wi_all), (wf_ref, wf_all))):
        for h in range(2):
            own, k = pl.ds(h * half, half), 2 * p + h
            lanes.append(gather_lane(me, src, own, dst, own, h == 1, Sub(g_ss, k * n), Sub(g_rs, k * n), local.at[k]))

    def stage(pair, s):
        def run():
            for lane in lanes[2 * pair : 2 * pair + 2]:
                lane[s]()
        return run

    greet(me)
    stage(0, 0)()
    stage(1, 0)()
    arriving = []
    for k in range(1, early_blocks(dp) + 1):
        j = lax.rem(me.i + k, dp)
        arriving.append(remote(cot_ref.at[me.t * dp + j], cota_ref.at[me.i], c_ss.at[k], c_rs.at[k], (j, me.t)))
    start_all(arriving)
    tick = Ticks([stage(0, 1), stage(0, 2), stage(1, 1), stage(0, 3), stage(1, 2), stage(1, 3), stage(0, 4), stage(1, 4)])
    forward_core(lambda at, i: x_ref[at, :], lambda t: w_ref[t], tn, small_ref, ids_ref, q_ref, k_ref, v_ref, near_ref,
                 far_ref, ctx_ref, lq_ref, lk_ref, mix_ref, sum_ref, ker_ref, z_ref, a_ref, v2_ref, w2_ref, pad_ref,
                 tick, lambda: wait_all(loads), writes)
    writes[5].start()
    tick.rest()
    wait_all(arriving)
    wait_all(writes)


def begin(dp, tn, tok, wq, wk, wv, wo, bq, bv, bi, taps, ids_ref, wi_ref, wf_ref, cot_ref,
          rows_out, wqkv_out, wout, small_out, q_out, k_out, v_out, near_out, far_out, ctx_out,
          lq_ref, lk_ref, mix_ref, sum_ref, ker_ref, z_out, a_out, v2_out, w2_out, wi_all, wf_all, cota_ref,
          x_ref, w_ref, small_ref, piece, pad_ref, q_ref, k_ref, v_ref, near_ref, far_ref, ctx_ref, z_ref, a_ref, v2_ref, w2_ref,
          r_ss, r_rs, p_ss, p_rs, g_ss, g_rs, c_ss, c_rs, local, move):
    me = Place(dp, tn)
    cols = wq.shape[1]
    n = gather_count(dp)
    first = []
    for k, (src, dst, lo) in enumerate(((wq, w_ref, 0), (wk, w_ref, cols), (wv, w_ref, 2 * cols), (wo, wout, 0))):
        first.append(gather_lane(me, src, pl.ds(0, cols), dst, pl.ds(lo, cols), k % 2 == 1,
                                 Sub(p_ss, k * n), Sub(p_rs, k * n), local.at[k]))
    lanes = []
    parts = wi_ref.shape[1] // FORWARD_CUT
    for p, (src, dst) in enumerate(((wi_ref, wi_all), (wf_ref, wf_all))):
        for h in range(parts):
            own, k = pl.ds(h * FORWARD_CUT, FORWARD_CUT), parts * p + h
            lanes.append(gather_lane(me, src, own, dst, own, h % 2 == 1, Sub(g_ss, k * n), Sub(g_rs, k * n), local.at[6 + k]))

    def stage(pair, s):
        def run():
            for lane in lanes[2 * pair : 2 * pair + 2]:
                lane[s]()
        return run

    fill_piece(piece, bq, bv, bi, taps)
    greet(me)
    for lane in first:
        lane[0]()
    moved = to_owner(me, tok, x_ref, r_ss, r_rs, local.at[4])
    start_all(moved)
    side = [remote(piece, small_ref.at[me.t], r_ss.at[0], r_rs.at[0], (me.i, 1 - me.t)),
            pltpu.make_async_copy(piece, small_ref.at[me.t], local.at[5])]
    start_all(side)
    arriving = []
    for k in range(1, early_blocks(dp) + 1):
        j = lax.rem(me.i + k, dp)
        arriving.append(remote(cot_ref.at[me.t * dp + j], cota_ref.at[me.i], c_ss.at[k], c_rs.at[k], (j, me.t)))
    pairs = len(lanes) // 2
    for pair, st in ((0, 1), (0, 2), (1, 1), (1, 2)):
        for lane in first[2 * pair : 2 * pair + 2]:
            lane[st]()
    for pair in range(FORWARD_EARLY):
        stage(pair, 0)()
    for lane in first:
        lane[3]()
    for pair in range(FORWARD_EARLY):
        stage(pair, 1)()
        stage(pair + FORWARD_EARLY, 0)()
        stage(pair, 2)()
    for lane in first:
        lane[4]()
    wait_all(side)
    wait_all(moved)
    rolled = 2 * FORWARD_EARLY
    while rolled < FORWARD_EARLY + FORWARD_AHEAD:
        stage(rolled, 0)()
        rolled += 1
    keep = [Fetch(x_ref, rows_out, move.at[0]).start(), Fetch(w_ref, wqkv_out, move.at[1]).start(),
            Fetch(small_ref, small_out, move.at[12]).start()]
    writes = [
        Fetch(a, b, move.at[2 + k]) for k, (a, b) in enumerate((
            (q_ref, q_out), (k_ref, k_out), (v_ref, v_out), (near_ref, near_out), (far_ref, far_out), (ctx_ref, ctx_out),
            (z_ref, z_out), (a_ref, a_out), (v2_ref, v2_out), (w2_ref, w2_out)))]
    todo = []
    for pair in range(FORWARD_EARLY, pairs):
        steps = [stage(pair, 1)]
        if rolled < pairs:
            steps.append(stage(rolled, 0))
            rolled += 1
        if rolled == pairs:
            steps.append(lambda: start_all(arriving))
            rolled += 1
        todo += [together(steps), stage(pair, 2)]
    todo += [stage(pair, 3) for pair in range(pairs)] + [stage(pair, 4) for pair in range(pairs)]
    tick = Ticks(todo)
    width = q_ref.shape[1]
    part = x_ref.shape[1]
    per = 256 // part
    forward_core(lambda at, i: x_ref[pl.ds(i * per, per)].reshape(256, width), lambda t: w_ref[t].reshape(width, 3 * cols),
                 tn, small_ref, ids_ref, q_ref, k_ref, v_ref, near_ref, far_ref, ctx_ref, lq_ref, lk_ref, mix_ref, sum_ref,
                 ker_ref, z_ref, a_ref, v2_ref, w2_ref, pad_ref, tick, lambda: None, writes)
    writes[5].start()
    tick.rest()
    wait_all(arriving)
    wait_all(writes)
    wait_all(keep)


FORWARD_CUT = 384
FORWARD_EARLY = 1
FORWARD_AHEAD = 2


def call_begin(dp, tn, tok, wq, wk, wv, wo, bq, bv, bi, taps, ids, wi, wf, cot):
    s = jax.ShapeDtypeStruct
    vm = pltpu.VMEM
    depth, cols = wq.shape
    units = wi.shape[1]
    part, width = tok.shape[1:]
    length = dp * part
    lead = (tn, dp // 4, 2, 2, depth)
    big, tall = s((length, width), BF), s((width, length), BF)
    low, wide = s((LAND, width), BF), s((LAND, width), F32)
    steps, steps1 = s((ITERS, LAND, width), F32), s((ITERS + 1, LAND, width), F32)
    whole = s(lead + (units,), BF)
    blocks = s((dp, part, width), BF)
    small = s((tn, SMALL_ROWS, 128), F32)
    wqkv = s(lead + (3 * cols,), BF)
    outs = (blocks, wqkv, s(lead + (cols,), BF), small,
            big, big, big, tall, tall, big, low, low, low, wide, wide, steps1, steps, steps, steps, whole, whole, blocks)
    n_lanes = 2 * (units // FORWARD_CUT)
    return pl.pallas_call(
        functools.partial(begin, dp, tn),
        out_shape=outs,
        in_specs=[ANY] * 5 + [VM] * 5 + [ANY] * 3,
        out_specs=tuple([ANY] * 10 + [VM] * 5 + [ANY] * 7),
        scratch_shapes=[vm(o.shape, o.dtype) for o in (blocks, wqkv, small)]
        + [vm((SMALL_ROWS, 128), F32), vm((256, length + 256), BF)]
        + [vm(o.shape, o.dtype) for o in outs[4:10] + outs[15:19]]
        + sems(dp) + sems(4 * gather_count(dp)) + sems(n_lanes * gather_count(dp)) + sems(dp)
        + [DMA((6 + n_lanes,)), DMA((13,))],
        compiler_params=params(5, TOP),
        name="begin",
    )(tok, wq, wk, wv, wo, bq, bv, bi, taps, ids, wi, wf, cot)


def waves(dp):
    return [[k for k in range(1, dp) if k % 4 == r] for r in (1, 2, 3, 0)]


def early_blocks(dp):
    return dp // 4


def call_attend_forward(dp, x, w, small, ids, wi, wf, cot):
    length, width = x.shape
    s = jax.ShapeDtypeStruct
    big = s((length, width), BF)
    tall = s((width, length), BF)
    low = s((LAND, width), BF)
    wide = s((LAND, width), F32)
    steps = s((ITERS, LAND, width), F32)
    tn = w.shape[0]
    depth, units = wi.shape
    whole = s((tn, dp // 4, 2, 2, depth, units), BF)
    outs = (big, big, big, tall, tall, big, low, low, low, wide, wide, s((ITERS + 1, LAND, width), F32), steps, steps, steps,
            whole, whole, s((dp,) + cot.shape[1:], BF))
    vm = pltpu.VMEM
    return pl.pallas_call(
        functools.partial(attend_forward, dp),
        out_shape=outs,
        in_specs=[ANY] * 2 + [VM] * 2 + [ANY] * 3,
        out_specs=tuple([ANY] * 6 + [VM] * 5 + [ANY] * 7),
        scratch_shapes=[vm((256, length + 256), BF)] + [vm(o.shape, o.dtype) for o in (x, w) + outs[:6] + outs[11:15]]
        + sems(4 * gather_count(dp)) + sems(dp) + [DMA((4,)), DMA((12,))],
        compiler_params=params(1, TOP),
        name="attend_forward",
    )(x, w, small, ids, wi, wf, cot)


ROOT_HALF = 0.7071067811865476
P_ERF = 0.3275911
C_ERF = (0.254829592, -0.284496736, 1.421413741, -1.453152027, 1.061405429)


def gelu_both(u):
    x = jnp.abs(u) * ROOT_HALF
    e = jnp.exp(-0.5 * u * u)
    t = 1.0 / (1.0 + P_ERF * x)
    poly = C_ERF[4]
    for c in (C_ERF[3], C_ERF[2], C_ERF[1], C_ERF[0]):
        poly = poly * t + c
    tail = 0.5 * poly * t * e
    phi = jnp.where(u < 0.0, tail, 1.0 - tail)
    return u * phi, phi + u * e * 0.3989422804014327


def norm_parts(r):
    n = r.shape[1]
    center = r - jnp.sum(r, axis=1, keepdims=True) * (1.0 / n)
    spread_ = jnp.sum(center * center, axis=1, keepdims=True) * (1.0 / n)
    rstd = lax.rsqrt(spread_ + 1e-05)
    return center * rstd, rstd


def norm_back(e, normed, rstd):
    n = e.shape[1]
    mean_e = jnp.sum(e, axis=1, keepdims=True) * (1.0 / n)
    mean_en = jnp.sum(e * normed, axis=1, keepdims=True) * (1.0 / n)
    return rstd * (e - mean_e - normed * mean_en)


def fold(a):
    return jnp.sum(a.reshape(a.shape[0] // 8, 8, a.shape[1]), axis=0)


def feed(dp, x_in, ctx_in, wo_in, wi_in, wf_in, bo_in, g1_in, s1_in, bf_in, g2_in, s2_in, small_ref, cot_ref, cota_ref,
         gr1_out, dc_out, dwo_out, dwi_out, dwf_out, vec_ref, bsum_ref, home_ref,
         act_ref, gi_ref, hid_ref, gr2_ref, turn_ref, n1_ref, n2_ref, rs1_ref, rs2_ref, out_ref, cots_ref,
         x_ref, ctx_ref, wo_ref, wi_ref, wf_ref, gr1_ref, dc_ref, dwo_ref, dwi_ref, dwf_ref,
         c_ss, c_rs, h_ss, h_rs, f_ss, f_rs, local, move):
    length, width = x_ref.shape
    tn = wo_ref.shape[0]
    cols = width // tn
    units = wi_ref.shape[2]
    size = 256
    chunk = 512
    part = length // dp
    per = size // part
    me = Place(dp, tn)
    x_l, ctx_l, wo_l, wi_l, wf_l = loads = [
        Fetch(a, b, move.at[k]).start() for k, (a, b) in enumerate((
            (x_in, x_ref), (ctx_in, ctx_ref), (wo_in, wo_ref), (wi_in, wi_ref), (wf_in, wf_ref)))]
    greet(me)
    mine = me.t * dp
    early = early_blocks(dp)
    arriving = [pltpu.make_async_copy(cot_ref.at[mine + me.i], cots_ref.at[me.i], local.at[0])]
    leaving, passing, turns = {}, {}, waves(dp)
    partner = (me.i, 1 - me.t)
    for k in range(1, dp):
        j, back = lax.rem(me.i + k, dp), lax.rem(me.i + dp - k, dp)
        if k <= early:
            arriving.append(pltpu.make_async_copy(cota_ref.at[back], cots_ref.at[back], c_ss.at[k]))
        else:
            arriving.append(remote(cot_ref.at[mine + j], cots_ref.at[me.i], c_ss.at[k], c_rs.at[k], (j, me.t)))
        leaving[k] = remote(out_ref.at[j], home_ref.at[mine + me.i], h_ss.at[k], h_rs.at[k], (j, me.t))
        if k in turns[0] + turns[1]:
            passing[k] = remote(home_ref.at[mine + back], home_ref.at[mine + back], f_ss.at[k], f_rs.at[k], partner)
    kept = pltpu.make_async_copy(out_ref.at[me.i], home_ref.at[mine + me.i], local.at[1])
    across = remote(out_ref.at[me.i], home_ref.at[mine + me.i], f_ss.at[0], f_rs.at[0], partner)
    start_all(arriving)
    bo, g1, s1, bf, g2, s2 = [
        r[...].astype(F32).reshape(1, width) for r in (bo_in, g1_in, s1_in, bf_in, g2_in, s2_in)]
    bi = [side_row(small_ref, t, ROWS_BI, units // 128) for t in range(tn)]
    vec_ref[...] = jnp.zeros_like(vec_ref)
    bsum_ref[...] = jnp.zeros_like(bsum_ref)

    def rows_at(i):
        return pl.ds(pl.multiple_of(i * size, size), size)

    def forward(i, carry):
        at = rows_at(i)
        attn = bo + x_ref[at, :].astype(F32)
        for t in range(tn):
            attn = attn + nt(ctx_ref[at, t * cols : (t + 1) * cols], wo_ref[t])
        n1, rstd1 = norm_parts(attn)
        n1_ref[at, :] = n1
        rs1_ref[at, :] = rstd1
        hidden = n1 * g1 + s1
        hid = hidden.astype(BF)
        hid_ref[at, :] = hid
        r2 = hidden + bf
        for t in range(tn):
            for c in range(0, units, chunk):
                own = slice(t * units + c, t * units + c + chunk)
                act, gp = gelu_both(nn(hid, wi_ref[t, :, c : c + chunk]) + bi[t][:, c : c + chunk])
                act_ref[at, own] = act.astype(BF)
                gi_ref[at, own] = gp.astype(BF)
        for t in range(tn):
            r2 = r2 + nt(act_ref[at, t * units : (t + 1) * units], wf_ref[t])
        n2, rstd2 = norm_parts(r2)
        n2_ref[at, :] = n2
        rs2_ref[at, :] = rstd2
        out_ref[pl.ds(i * per, per)] = (n2 * g2 + s2).reshape(per, part, width).astype(BF)
        return carry

    def backward(i, carry):
        at = rows_at(i)
        cot = cots_ref[pl.ds(i * per, per)].astype(F32).reshape(size, width)
        n2 = n2_ref[at, :]
        gr2 = norm_back(cot * g2, n2, rs2_ref[at, :])
        vec_ref[5] += fold(cot)
        vec_ref[4] += fold(cot * n2)
        vec_ref[3] += fold(gr2)
        low = gr2.astype(BF)
        gr2_ref[at, :] = low
        for t in range(tn):
            for c in range(0, units, chunk):
                own = slice(t * units + c, t * units + c + chunk)
                gi = nn(low, wf_ref[t, :, c : c + chunk]) * gi_ref[at, own].astype(F32)
                bsum_ref[:, own] += fold(gi)
                gi_ref[at, own] = gi.astype(BF)
        gh = gr2
        for t in range(tn):
            gh = gh + nt(gi_ref[at, t * units : (t + 1) * units], wi_ref[t])
        n1 = n1_ref[at, :]
        gr1 = norm_back(gh * g1, n1, rs1_ref[at, :])
        vec_ref[2] += fold(gh)
        vec_ref[1] += fold(gh * n1)
        vec_ref[0] += fold(gr1)
        low1 = gr1.astype(BF)
        gr1_ref[at, :] = low1
        for t in range(tn):
            dc_ref[at, t * cols : (t + 1) * cols] = nn(low1, wo_ref[t]).astype(BF)
        return carry

    wait_all(loads)
    lax.fori_loop(0, length // size, forward, 0)
    start_all([leaving[k] for k in turns[0]])
    kept.start()
    across.start()
    wait_all(arriving)
    n_back = length // size
    for i in range(n_back):
        backward(i, 0)
        if i == n_back // 2 - 1:
            start_all([leaving[k] for k in turns[1]])
            for k in turns[0]:
                leaving[k].wait()
                passing[k].start()
    start_all([leaving[k] for k in turns[2]])
    for k in turns[1]:
        leaving[k].wait()
        passing[k].start()
    start_all([leaving[k] for k in turns[3]])

    outs = [Fetch(gr1_ref, gr1_out, move.at[5]).start(), Fetch(dc_ref, dc_out, move.at[6]).start()]
    turn_ref[...] = turn(gr2_ref[...])
    for t in range(tn):
        for c in range(0, units, chunk):
            own = slice(t * units + c, t * units + c + chunk)
            dwf_ref[t, :, c : c + chunk] = nn(turn_ref[...], act_ref[:, own]).astype(BF)
    outs.append(Fetch(dwf_ref, dwf_out, move.at[7]).start())
    turn_ref[...] = turn(hid_ref[...])
    for t in range(tn):
        for c in range(0, units, chunk):
            own = slice(t * units + c, t * units + c + chunk)
            dwi_ref[t, :, c : c + chunk] = nn(turn_ref[...], gi_ref[:, own]).astype(BF)
    outs.append(Fetch(dwi_ref, dwi_out, move.at[8]).start())
    turn_ref[...] = turn(gr1_ref[...])
    for t in range(tn):
        dwo_ref[t] = nn(turn_ref[...], ctx_ref[:, t * cols : (t + 1) * cols]).astype(BF)
    outs.append(Fetch(dwo_ref, dwo_out, move.at[9]).start())
    wait_all([leaving[k] for k in turns[2] + turns[3]])
    kept.wait()
    across.wait()
    wait_all(passing.values())
    wait_all(outs)


def call_feed(dp, x, ctx, wo, wi, wf, vectors, small, cot, cota):
    length, width = x.shape
    tn, _, cols = wo.shape
    units = wi.shape[2]
    s = jax.ShapeDtypeStruct
    big = s((length, width), BF)
    blocks = (dp,) + cot.shape[1:]
    outs = (big, big, s((tn, width, cols), BF), s((tn, width, units), BF), s((tn, width, units), BF),
            s((6, 8, width), F32), s((8, tn * units), F32), s((tn * dp,) + blocks[1:], BF))
    vm = pltpu.VMEM
    return pl.pallas_call(
        functools.partial(feed, dp),
        out_shape=outs,
        in_specs=[ANY] * 5 + [VM] * 7 + [ANY] * 2,
        out_specs=tuple([ANY] * 5 + [VM] * 2 + [ANY]),
        scratch_shapes=[vm((length, tn * units), BF), vm((length, tn * units), BF), vm((length, width), BF),
                        vm((length, width), BF), vm((width, length), BF), vm((length, width), F32),
                        vm((length, width), F32), vm((length, 1), F32), vm((length, 1), F32), vm(blocks, BF),
                        vm(blocks, BF)] + [vm(o.shape, o.dtype) for o in (x, ctx, wo, wi, wf) + outs[:5]]
        + sems(dp) * 3 + [DMA((2,)), DMA((10,))],
        compiler_params=params(2, TOP),
        name="feed_forward",
    )(x, ctx, wo, wi, wf, *vectors, small, cot, cota)


NORTH_LANES = (1, 3, 5, 7)
BACK_CUT = 384
BACK_LAG = 6
SIDE_FIRST = 6
BACK_TICKS = (6, 0, 0, 2, 2, 2, 2, 1)


def staggered(lanes, lag):
    steps = []
    for step in range(len(lanes) + 2 * lag):
        todo = []
        for stage in (3, 2, 1):
            k = step - (stage - 1) * lag
            if 0 <= k < len(lanes):
                todo.append(lanes[k][stage])
        steps.append(todo)
    return steps


def row_of(column):
    return turn(jnp.broadcast_to(column, (column.shape[0], 128)))[0:1, :]


def attend_backward(dp, ids_ref, small_ref, lq_ref, lk_ref, mix_ref, sum_ref, ker_ref,
                    x_in, w_in, q_in, k_in, v_in, near_in, far_in, z_in, a_in, v2_in, w2_in, dc_in, gr1_in,
                    dwo_in, dwi_in, dwf_in, home_in,
                    gtok_ref, dw_ref, vecs_ref, gtap_ref, go_ref, gi_ref, gf_ref, home_ref,
                    x_ref, w_ref, q_ref, k_ref, v_ref, near_ref, far_ref, z_ref, a_ref, v2_ref, w2_ref, dc_ref, gr1_ref,
                    pre_ref, glq_ref, glk_ref, gsum_ref, gz_ref, gk_ref, padv_ref, padc_ref, xt_ref,
                    g_ss, g_rs, y_ss, y_rs, local, move, *bufs, carry=None):
    near_l, dc_l, z_l, a_l, v2_l, w2_l, far_l, q_l, k_l, v_l, x_l, w_l, gr1_l = [
        Fetch(a, b, move.at[k]).start() for k, (a, b) in enumerate((
            (near_in, near_ref), (dc_in, dc_ref), (z_in, z_ref), (a_in, a_ref), (v2_in, v2_ref), (w2_in, w2_ref),
            (far_in, far_ref), (q_in, q_ref), (k_in, k_ref), (v_in, v_ref), (x_in, x_ref), (w_in, w_ref), (gr1_in, gr1_ref)))]
    length, width = x_ref.shape
    tn = w_ref.shape[0]
    cols = width // tn
    scale = LAND ** -0.25
    size = length // dp
    pairs = width // 128
    groups = width // 256
    me = Place(dp, tn)
    n = reduce_count(dp)
    plan = []
    for src, dst in ((dwf_in, gf_ref), (dwi_in, gi_ref), (dwo_in, go_ref)):
        plan += [(src, lo, BACK_CUT, dst) for lo in range(0, src.shape[5], BACK_CUT)]
    lanes = []
    for k, (src, lo, w, dst) in enumerate(plan):
        lanes.append(reduce_lane(me, src, lo, w, bufs[5 * k : 5 * k + 5], Sub(g_ss, k * n), Sub(g_rs, k * n), local.at[k],
                                 [(dst, lo, 0, w)], k in NORTH_LANES))
    sides = []
    for k in waves(dp)[2] + waves(dp)[3]:
        j = me.t * dp + lax.rem(me.i + dp - k, dp)
        sides.append(remote(home_ref.at[j], home_ref.at[j], y_ss.at[k], y_rs.at[k], (me.i, 1 - me.t)))
    greet(me, carry is not None)
    for lane in lanes:
        lane[0]()
    steps = staggered(lanes, BACK_LAG)
    for k, side in enumerate(sides):
        steps[min(SIDE_FIRST + k, len(steps) - 1)].append(side.start)
    tick = Ticks([together(step) for step in steps])
    ids = ids_ref[pl.ds(own_sequence(), 1), :]
    member = jnp.where(lax.broadcasted_iota(jnp.int32, (LAND, length), 0) == ids, 1.0, 0.0).astype(F32)
    count = jnp.sum(member, axis=1, keepdims=True)
    member = member.astype(BF)
    valid = ids < LAND
    eye = pair_eye()

    near_l.wait()
    dc_l.wait()
    for g in range(groups):
        own = slice(g * 256, (g + 1) * 256)
        gsum_ref[:, own] = gather_diag(nn(near_ref[own, :], dc_ref[:, own]))
    tick(BACK_TICKS[0])
    wait_all([z_l, a_l, v2_l, w2_l])
    for p in range(pairs):
        own = slice(p * 128, (p + 1) * 128)
        gmix = gsum_ref[:, own]
        gz_ref[:, own] = pair_nt(gmix, sum_ref[:, own])
        gsum_ref[:, own] = pair_nn(pair_turn(z_ref[ITERS, :, own]), gmix)

    tick(BACK_TICKS[1])
    gk_ref[...] = jnp.zeros_like(gk_ref)

    def iterate(m, carry):
        n = ITERS - 1 - m
        for p in range(pairs):
            own = slice(p * 128, (p + 1) * 128)
            grad = 0.25 * gz_ref[:, own]
            kernel = ker_ref[:, own]
            z = z_ref[n, :, own]
            a = a_ref[n, :, own]
            v2 = v2_ref[n, :, own]
            w2 = w2_ref[n, :, own]
            dw2 = pair_nn(pair_turn(z), grad)
            at = pair_turn(a)
            dv2 = -pair_nn(at, dw2)
            da = -pair_nt(dw2, v2) - pair_nt(dv2, 7.0 * eye - a) + pair_nn(at, dv2)
            gk_ref[:, own] += pair_nt(da, z)
            gz_ref[:, own] = pair_nt(grad, w2) + pair_nn(pair_turn(kernel), da)
        return carry

    lax.fori_loop(0, ITERS // 2, iterate, 0)
    tick(BACK_TICKS[2])
    lax.fori_loop(ITERS // 2, ITERS, iterate, 0)
    tick(BACK_TICKS[3])
    wait_all([far_l, q_l, k_l, v_l])

    for p in range(pairs):
        own = slice(p * 128, (p + 1) * 128)
        kernel = ker_ref[:, own]
        gz = gz_ref[:, own]
        total = jnp.sum(pair_sum(kernel * kernel), axis=0, keepdims=True)
        kt = pair_turn(kernel)
        back = jnp.sum(pair_sum(gz * kt), axis=0, keepdims=True)
        gk = gk_ref[:, own] + pair_turn(gz) / total - kernel * (2.0 * back / (total * total))
        mid = kernel * (gk - pair_sum(kernel * gk))
        glq_ref[:, own] = pair_nn(mid, lk_ref[:, own].astype(F32))
        glk_ref[:, own] = pair_nn(pair_turn(mid), lq_ref[:, own].astype(F32))

    flip = jnp.where(
        lax.broadcasted_iota(jnp.int32, (256, 256), 0) + lax.broadcasted_iota(jnp.int32, (256, 256), 1) == 255, 1.0, 0.0
    ).astype(BF)
    taps = [reversed_taps(tap_rows(small_ref, t)) for t in range(tn)]
    padv_ref[...] = jnp.zeros_like(padv_ref)
    padc_ref[...] = jnp.zeros_like(padc_ref)
    inner = slice(128, 128 + length)
    for g in range(groups):
        own = slice(g * 256, (g + 1) * 256)
        lk4 = spread(lk_ref[:, own])
        lq4 = spread(lq_ref[:, own])
        near = near_ref[own, :].astype(F32)
        gnear = nt(spread(mix_ref[:, own]), dc_ref[:, own])
        drop = jnp.sum((near * gnear).reshape(4, LAND, length), axis=1, keepdims=True)
        first = (near * (gnear.reshape(4, LAND, length) - drop).reshape(256, length)).astype(BF)
        glk_ref[:, own] += gather_diag(nn(first, q_ref[:, own]))
        gsum4 = spread(gsum_ref[:, own].astype(BF))
        far = far_ref[own, :].astype(F32)
        gfar = nt(gsum4, v_ref[:, own])
        drop = jnp.sum(far * gfar, axis=1, keepdims=True)
        third = (far * (gfar - drop)).astype(BF)
        glq_ref[:, own] += gather_diag(nn(third, k_ref[:, own]))
        glq = turn((glq_ref[:, own] / count).astype(BF))
        glk = turn((glk_ref[:, own] / count).astype(BF))
        dq = (nn(turn(lk4), first) + nn(glq, member)) * scale
        dk = (nn(turn(lq4), third) + nn(glk, member)) * scale
        dv = nn(turn(gsum4), far_ref[own, :])

        vt = turn(v_ref[:, own])
        padv_ref[:, inner] = jnp.where(valid, vt, jnp.zeros_like(vt))
        padc_ref[:, inner] = turn(dc_ref[:, own])
        parts = []
        for h in range(4):
            band = band_of(taps, 4 * g + h)
            parts.append(unblock(nt(blocks_of(padc_ref, h * LAND, 256), band), 256))
            plain = jnp.concatenate(
                [padc_ref[h * LAND : (h + 1) * LAND, 128 + at : 128 + at + 256] for at in range(0, length, 256)], axis=0
            )
            gram = nn(nt(flip, plain).astype(BF), blocks_of(padv_ref, h * LAND, 256))
            gram = pltpu.roll(gram, 0, 1, stride=1, stride_axis=0)
            gtap_ref[4 * g + h : 4 * g + h + 1, :] = jnp.sum(gram, axis=0, keepdims=True)
        dv = dv + jnp.where(valid, jnp.concatenate(parts, axis=0), 0.0)
        vecs_ref[0:1, own] = row_of(jnp.sum(dq, axis=1, keepdims=True))
        vecs_ref[1:2, own] = row_of(jnp.sum(dv, axis=1, keepdims=True))
        for lower in range(0, 256, 128):
            c = g * 256 + lower
            t, r = c // cols, c % cols
            pre_ref[t, r : r + 128, :] = dq[lower : lower + 128].astype(BF)
            pre_ref[t, cols + r : cols + r + 128, :] = dk[lower : lower + 128].astype(BF)
            pre_ref[t, 2 * cols + r : 2 * cols + r + 128, :] = dv[lower : lower + 128].astype(BF)
        tick(BACK_TICKS[4 + g])

    wait_all([x_l, w_l, gr1_l])

    def weight_grads():
        xt_ref[...] = turn(x_ref[...])
        for t in range(tn):
            dw = nt(xt_ref[...], pre_ref[t])
            if carry:
                dw = dw.reshape(dw_ref.shape[1:])
            dw_ref[t] = dw.astype(BF)

    def token_grads():
        for at in range(0, length, 256):
            part = nn(w_ref[0], pre_ref[0, :, at : at + 256])
            for t in range(1, tn):
                part = part + nn(w_ref[t], pre_ref[t, :, at : at + 256])
            gtok_ref[at // size : (at + 256) // size] = (
                (gr1_ref[at : at + 256, :].astype(F32) + turn(part)).reshape(256 // size, size, width).astype(BF)
            )

    if carry:
        token_grads()
        carry.send_rows()
        tick(BACK_TICKS[7])
        weight_grads()
        carry.send_grads()
        carry.pack()
        carry.finish(tick.stages)
    else:
        weight_grads()
        tick(1)
        token_grads()
        tick.rest()
    for lane in lanes:
        lane[4]()
    wait_all(sides)


def end(dp, *refs):
    ins, refs = refs[:26], refs[26:]
    vec, bsum = ins[24:]
    go, gi, gf, home, g_home, gq, gk, gv, gbq, gbv, gtaps, gbi, *refs = refs
    n_outs, refs = refs[:6], refs[6:]
    gtok, dw, vecs, gtap, *refs = refs
    count = 13 + 9 + 6
    own, refs = refs[:count], refs[count:]
    n_bufs = len(refs) - 15 - 15
    bufs, refs = refs[:n_bufs], refs[n_bufs:]
    me = Place(dp, gtap.shape[0] // HEADS_HERE)
    carry = Carry(me, gtok, dw, vec, bsum, vecs, gtap, g_home, gq, gk, gv, gbq, gbv, gtaps, gbi, n_outs, *refs[:15], refs[15:])
    attend_backward(dp, *ins[:24], gtok, dw, vecs, gtap, go, gi, gf, home, *own, *bufs, carry=carry)


def call_end(dp, x, w, ids, small, saved, dc, gr1, dwo, dwi, dwf, home, vec, bsum, taps):
    q, k, v, near, far, lq, lk, mix, summ, ker, z, a, v2, w2 = saved
    length, width = x.shape
    tn = w.shape[0]
    cols = width // tn
    s = jax.ShapeDtypeStruct
    vm = pltpu.VMEM
    depth, units = dwi.shape[4:]
    share = s((depth, cols), F32)
    outs = (share, s((depth, units), F32), s((depth, units), F32), s(home.shape, BF), s(home.shape, BF), share, share, share,
            s((cols,), F32), s((cols,), F32), s(taps.shape, F32), s((units,), F32)) + (s((depth,), F32),) * 6
    little = (ids, small, lq, lk, mix, summ, ker)
    large = (x, w, q, k, v, near, far, z, a, v2, w2, dc, gr1)
    args = little + large + (dwo, dwi, dwf, home, vec, bsum)
    mini = vm((LAND, width), F32)
    n_lanes = (2 * units + cols) // BACK_CUT
    n = n_lanes * reduce_count(dp)
    scratch = [vm((dp,) + home.shape[1:], BF), vm((tn, dp // 4, 2, 2, depth, 3 * cols), BF), vm((8, width), F32),
               vm((width // LAND, 512), F32)]
    scratch += [vm(b.shape, b.dtype) for b in large] + [vm((tn, 3 * cols, length), BF)] + [mini] * 5
    scratch += [vm((256, length + 256), BF), vm((256, length + 256), BF), vm((width, length), BF)]
    scratch += sems(n) + sems(dp) + [DMA((n_lanes,)), DMA((len(large),))]
    for k in range(n_lanes):
        scratch += reduce_bufs(dp, tn, depth, BACK_CUT, k in NORTH_LANES)
    scratch += carry_scratch(dp, tn, depth, cols)
    return pl.pallas_call(
        functools.partial(end, dp),
        out_shape=outs,
        in_specs=[VM] * len(little) + [ANY] * (len(large) + 4) + [VM] * 2,
        out_specs=tuple([VM] * 3 + [ANY] * 2 + [VM] * 13),
        scratch_shapes=scratch,
        input_output_aliases={len(args) - 3: 3},
        compiler_params=params(6, TOP),
        name="end",
    )(*args)


def call_attend_backward(dp, x, w, ids, small, saved, dc, gr1, dwo, dwi, dwf, home):
    q, k, v, near, far, lq, lk, mix, summ, ker, z, a, v2, w2 = saved
    length, width = x.shape
    tn = w.shape[0]
    cols = width // tn
    s = jax.ShapeDtypeStruct
    depth, units = dwi.shape[4:]
    outs = (s((dp,) + home.shape[1:], BF), s((tn, width, 3 * cols), BF), s((8, width), F32),
            s((width // LAND, 512), F32), s((depth, cols), F32), s((depth, units), F32), s((depth, units), F32),
            s(home.shape, BF))
    little = (ids, small, lq, lk, mix, summ, ker)
    large = (x, w, q, k, v, near, far, z, a, v2, w2, dc, gr1)
    args = little + large + (dwo, dwi, dwf, home)
    vm = pltpu.VMEM
    mini = vm((LAND, width), F32)
    n_lanes = (2 * units + cols) // BACK_CUT
    n = n_lanes * reduce_count(dp)
    scratch = [vm(b.shape, b.dtype) for b in large] + [vm((tn, 3 * cols, length), BF)] + [mini] * 5
    scratch += [vm((256, length + 256), BF), vm((256, length + 256), BF), vm((width, length), BF)]
    scratch += sems(n) + sems(dp) + [DMA((n_lanes,)), DMA((len(large),))]
    for k in range(n_lanes):
        scratch += reduce_bufs(dp, tn, depth, BACK_CUT, k in NORTH_LANES)
    return pl.pallas_call(
        functools.partial(attend_backward, dp),
        out_shape=outs,
        in_specs=[VM] * len(little) + [ANY] * (len(args) - len(little)),
        out_specs=tuple([VM] * 7 + [ANY]),
        scratch_shapes=scratch,
        input_output_aliases={len(args) - 1: 7},
        compiler_params=params(3, TOP),
        name="attend_backward",
    )(*args)


def finish(n, *refs):
    ins, outs, held, sem = refs[:n], refs[n : 2 * n], refs[2 * n : 3 * n], refs[3 * n]
    loads = [pltpu.make_async_copy(a, b, sem.at[k]) for k, (a, b) in enumerate(zip(ins, held))]
    writes = [pltpu.make_async_copy(a, b, sem.at[n + k]) for k, (a, b) in enumerate(zip(held, outs))]
    start_all(loads)
    for a, b in zip(loads, writes):
        a.wait()
        b.start()
    wait_all(writes)


def call_finish(arrays):
    n = len(arrays)
    return pl.pallas_call(
        functools.partial(finish, n),
        out_shape=tuple(jax.ShapeDtypeStruct(a.shape, a.dtype) for a in arrays),
        in_specs=[ANY] * n,
        out_specs=(ANY,) * n,
        scratch_shapes=[pltpu.VMEM(a.shape, a.dtype) for a in arrays] + [DMA((2 * n,))],
        compiler_params=pltpu.CompilerParams(vmem_limit_bytes=TOP * 2**20),
        name="finish",
    )(*arrays)


def local(tokens, cotangent, landmark_ids, w_query, w_key, w_value, b_query, b_value, conv_taps, w_out, b_out,
          first_gain, first_shift, w_inner, b_inner, w_outer, b_outer, second_gain, second_shift):
    dp = lax.axis_size("dp")
    tn = lax.axis_size("tensor")
    part, width = tokens.shape[1:]
    length = dp * part
    cols = w_query.shape[1]
    vectors = [b_out, first_gain, first_shift, b_outer, second_gain, second_shift]

    def join(w):
        return w.reshape(tn, width, w.shape[-1])

    def cut(g):
        return g.reshape(tn, dp // 4, 2, 2, width // dp, g.shape[2])

    joined = width // dp % 16 == 0 and part % 16 == 0
    if joined:
        rows, wqkv, wout, small, *done = call_begin(
            dp, tn, tokens, w_query, w_key, w_value, w_out, b_query, b_value, b_inner, conv_taps,
            landmark_ids, w_inner, w_outer, cotangent)
    else:
        rows, wqkv, wout, small = call_bring(
            dp, tn, tokens, w_query, w_key, w_value, w_out, b_query, b_value, b_inner, conv_taps)
        done = call_attend_forward(
            dp, rows.reshape(length, width), join(wqkv), small, landmark_ids, w_inner, w_outer, cotangent)
    rows = rows.reshape(length, width)
    wqkv, wout = join(wqkv), join(wout)
    q, k, v, near, far, ctx, *rest_saved, wi, wf, cota = done
    gr1, dc, dwo, dwi, dwf, vec, bsum, home = call_feed(
        dp, rows, ctx, wout, join(wi), join(wf), vectors, small, cotangent, cota
    )
    back = (dp, rows, wqkv, landmark_ids, small, (q, k, v, near, far, *rest_saved), dc, gr1, cut(dwo), cut(dwi), cut(dwf), home)
    if joined:
        go, gi, gf, out_home, *ends = call_end(*back, vec, bsum, conv_taps)
    else:
        grad_rows, dwqkv, vecs, gtap, go, gi, gf, out_home = call_attend_backward(*back)
        ends = call_carry_home(dp, tn, grad_rows, cut(dwqkv), vec, bsum, vecs, gtap, conv_taps)
    grad_home, gq, gk, gv, gbq, gbv, gtaps, gbi, gbo, gg1, gs1, gbf, gg2, gs2 = ends
    return call_finish((out_home, grad_home, gq, gk, gv, gbq, gbv, gtaps, go, gbo, gg1, gs1, gi, gbi, gf, gbf, gg2, gs2))


def solution(mesh):
    return jax.shard_map(
        local,
        mesh=mesh,
        in_specs=(
            P(None, "dp", None),
            P(None, "dp", None),
            P(),
            P("dp", "tensor"),
            P("dp", "tensor"),
            P("dp", "tensor"),
            P("tensor"),
            P("tensor"),
            P("tensor", None),
            P("dp", "tensor"),
            P(),
            P(),
            P(),
            P("dp", "tensor"),
            P("tensor"),
            P("dp", "tensor"),
            P(),
            P(),
            P(),
        ),
        out_specs=(
            P(None, "dp", None),
            P(None, "dp", None),
            P("dp", "tensor"),
            P("dp", "tensor"),
            P("dp", "tensor"),
            P("tensor"),
            P("tensor"),
            P("tensor", None),
            P("dp", "tensor"),
            P("dp"),
            P("dp"),
            P("dp"),
            P("dp", "tensor"),
            P("tensor"),
            P("dp", "tensor"),
            P("dp"),
            P("dp"),
            P("dp"),
        ),
        check_vma=False,
    )
```
